32 devices in a mesh: slab: 8 (over z, core), cell: 4 (over y, x).
Axes of the slice: x: 2, y: 2, z: 4, core: 2. Of those that a mesh axis runs over, the one named last changes fastest.
Arguments:
- centers: float32 [3, 2048], P(None, ('slab', 'cell')), may hold values from -0.8 to 0.8
- offsets: float32 [3, 2048, 312], P(None, ('slab', 'cell')), may hold values from -0.5 to 0.5
- forces: float32 [3, 2048, 312], P(None, ('slab', 'cell')), may hold values from -6 to 6
- upsample: float32 [312, 1248], replicated, may hold values from -0.3125 to 0.3125
- translate: float32 [3, 165, 165], replicated, may hold values from -0.5 to 0.5
- owner_cell: int32 [32, 4, 2], P(('slab', 'cell')), may hold values from 0 to 63, as said below
- peer_cell: int32 [32, 4, 2], P(('slab', 'cell')), may hold values from 0 to 63, as said below
- live: int32 [32, 4, 2], P(('slab', 'cell')), may hold values 0 or 1
Outputs:
- velocity: float32 [3, 2048, 312], P(None, ('slab', 'cell'))
The draws below stay inside these ranges and needn't reach their ends.
Inputs may be any that keep to these rules, and one draw needn't show every extreme that they name: `owner_cell`: every cell takes part in at most one pair slot of all devices, as owner or as partner. `peer_cell`: every cell takes part in at most one pair slot of all devices, as owner or as partner.
All inputs are finite; a program needn't handle non-finite values. No bound on the sum of `live` on one device may be relied on, other than what follows from the above.
Results may differ from the reference program's by a relative error of at most 0.00019.
Values sent between devices are 32-bit elements; how exact they have to be, the bound alone decides.
No kernel may reach another device: no remote copies, remote signals or barrier semaphores. Data moves between devices by JAX's collectives and lax.ppermute only.
A program may use at most 64 MiB of HBM per device.

```python
import math
import jax
import jax.numpy as jnp
from jax import lax

CELLS_DEV = 64
SLOT = 2
P_SIZE = 312
DEGREE = 8
UP = 1248
NT = 165
CELLS = 2048
N_SLAB = 8
N_CELL = 4


def place_value(order, value, position):
    where_now = jnp.argmax(order == value)
    held = order[position]
    return order.at[where_now].set(held).at[position].set(value)


def pair_lists(key):
    device_count = N_SLAB * N_CELL
    used = N_CELL * SLOT
    device_keys = jax.random.split(key, device_count)
    orders = jax.vmap(lambda one_key: jax.random.permutation(one_key, CELLS_DEV))(device_keys).astype(jnp.int32)
    first_row = place_value(place_value(orders[0], CELLS_DEV - 1, 0), 0, 1)
    second_row = place_value(place_value(orders[1], CELLS_DEV - 1, used), 0, used + 1)
    orders = orders.at[0].set(first_row).at[1].set(second_row)
    owners = orders[:, :used].reshape(device_count, N_CELL, SLOT)
    backward = orders[:, used:2 * used].reshape(N_SLAB, N_CELL, N_CELL, SLOT)
    partners = jnp.transpose(backward, (0, 2, 1, 3)).reshape(device_count, N_CELL, SLOT)
    return (owners, partners)


def draw_owner_cell(key, part):
    owners, partners = pair_lists(key)
    return owners


def draw_peer_cell(key, part):
    owners, partners = pair_lists(key)
    return partners


def draw_offsets(key, part):
    key = jax.random.fold_in(key, 11)
    radius_key, turn_key, rise_key, rough_key = jax.random.split(key, 4)
    radius = jax.random.uniform(radius_key, (CELLS,), jnp.float32, 0.22, 0.36)
    rough = jnp.clip(0.12 * jax.random.normal(rough_key, (CELLS, P_SIZE), jnp.float32), -0.3, 0.3)
    turn = jax.random.uniform(turn_key, (CELLS, P_SIZE), jnp.float32, -math.pi, math.pi)
    rise = jax.random.uniform(rise_key, (CELLS, P_SIZE), jnp.float32, -1.0, 1.0)
    flat = jnp.sqrt(jnp.maximum(1.0 - rise * rise, 0.0))
    direction = jnp.stack([flat * jnp.cos(turn), flat * jnp.sin(turn), rise])
    length = radius[:, None] * (1.0 + rough)
    return (length[None] * direction).astype(jnp.float32)


def draw_centers(key, part):
    owners, partners = pair_lists(key)
    key = jax.random.fold_in(key, 7)
    base_key, near_key, turn_key, rise_key = jax.random.split(key, 4)
    device_count = N_SLAB * N_CELL
    used = N_CELL * SLOT
    base = jax.random.uniform(base_key, (3, CELLS), jnp.float32, -0.6, 0.6)
    reach = jax.random.uniform(near_key, (device_count * used,), jnp.float32, 0.1, 0.2)
    turn = jax.random.uniform(turn_key, (device_count * used,), jnp.float32, -math.pi, math.pi)
    rise = jax.random.uniform(rise_key, (device_count * used,), jnp.float32, -1.0, 1.0)
    flat = jnp.sqrt(jnp.maximum(1.0 - rise * rise, 0.0))
    direction = jnp.stack([flat * jnp.cos(turn), flat * jnp.sin(turn), rise])
    device_ids = jnp.arange(device_count, dtype=jnp.int32)
    peer_ids = jnp.repeat(jnp.arange(N_CELL, dtype=jnp.int32), SLOT)
    first_cell = (device_ids[:, None] * CELLS_DEV + owners.reshape(device_count, used)).reshape(-1)
    second_cell = ((device_ids[:, None] // N_CELL * N_CELL + peer_ids[None, :]) * CELLS_DEV + partners.reshape(device_count, used)).reshape(-1)
    moved = base[:, first_cell] + reach[None, :] * direction
    return base.at[:, second_cell].set(moved).astype(jnp.float32)


def place_ends(result, rng, low, high):
    shape = result.shape
    place = [jax.random.randint(jax.random.fold_in(rng, axis), (), 0, shape[axis]) for axis in range(len(shape))]
    result = result.at[tuple(place)].set(low)
    longest = shape.index(max(shape))
    place[longest] = (place[longest] + 1) % shape[longest]
    return result.at[tuple(place)].set(high)


def levels(stream_key, extent, cuts, least, high):
    def one(axis_at, parts):
        heights = jax.random.uniform(jax.random.fold_in(jax.random.fold_in(stream_key, 6), axis_at), (parts,), jnp.float32, least / len(cuts), high / len(cuts))
        return jnp.repeat(jnp.exp(heights), extent[axis_at] // parts).reshape((-1,) + (1,) * (len(extent) - axis_at - 1))

    loudness = one(*cuts[0])
    for cut in cuts[1:]:
        loudness = loudness * one(*cut)
    return loudness


def scatter_about(stream_key, dims, width, most, cuts=(), kind=jnp.bfloat16):
    result = width * jax.random.normal(stream_key, dims, jnp.float32)
    if cuts:
        result = result * levels(stream_key, dims, cuts, -0.22, 0.18)
    return jnp.clip(result, -most, most).astype(kind)


def setup_inputs(seed: int = 0) -> dict:
    key_list = jax.random.split(jax.random.key(seed), 9)
    return {
        "centers": draw_centers(jax.random.fold_in(key_list[8], 71), 0),
        "offsets": draw_offsets(jax.random.fold_in(key_list[8], 71), 0),
        "forces": scatter_about(key_list[2], (3, CELLS, P_SIZE), 1.0, 6.0, ((1, 32),), jnp.float32),
        "upsample": scatter_about(key_list[3], (P_SIZE, UP), P_SIZE ** -0.5, 0.3125, (), jnp.float32),
        "translate": scatter_about(key_list[4], (3, NT, NT), NT ** -0.5, 0.5, (), jnp.float32),
        "owner_cell": draw_owner_cell(jax.random.fold_in(key_list[8], 71), 0),
        "peer_cell": draw_peer_cell(jax.random.fold_in(key_list[8], 71), 0),
        "live": place_ends((jax.random.randint(key_list[7], (N_SLAB * N_CELL, N_CELL, SLOT), 0, 2) < 1).astype(jnp.int32), jax.random.fold_in(key_list[7], 1), 0, 1),
    }


soften = 0.0025
highest = lax.Precision.HIGHEST

def stokeslet(targets, sources, strengths):
    differ = targets[:, :, None] - sources[:, None, :]
    radius_sq = lax.optimization_barrier(jnp.sum(differ * differ, axis=0))
    inverse = lax.rsqrt(radius_sq + soften)
    inverse_cube = inverse * inverse * inverse
    projected = lax.optimization_barrier(jnp.sum(differ * strengths[:, None, :], axis=0))
    summed = (radius_sq + 2.0 * soften)[None] * strengths[:, None, :] + projected[None] * differ
    return lax.optimization_barrier(jnp.sum(summed * inverse_cube[None], axis=2)) / sources.shape[1]

def monomials(points):
    powers_x = [jnp.ones_like(points[0])]
    powers_y = [jnp.ones_like(points[1])]
    powers_z = [jnp.ones_like(points[2])]
    for number in range(DEGREE):
        powers_x.append(powers_x[-1] * points[0])
        powers_y.append(powers_y[-1] * points[1])
        powers_z.append(powers_z[-1] * points[2])
    terms = []
    for first in range(DEGREE + 1):
        for second in range(DEGREE + 1 - first):
            for third in range(DEGREE + 1 - first - second):
                terms.append(powers_x[first] * powers_y[second] * powers_z[third])
    return jnp.stack(terms)

def reference(centers, offsets, forces, upsample, translate, owner_cell, peer_cell, live):
    cells_all = centers.shape[1]
    device_count = N_SLAB * N_CELL
    per_device = N_CELL * SLOT
    points = centers[:, :, None] + offsets
    device_ids = jnp.arange(device_count, dtype=jnp.int32)
    peer_ids = jnp.repeat(jnp.arange(N_CELL, dtype=jnp.int32), SLOT)
    first_cell = device_ids[:, None] * CELLS_DEV + owner_cell.reshape(device_count, per_device)
    second_cell = (device_ids[:, None] // N_CELL * N_CELL + peer_ids[None, :]) * CELLS_DEV + peer_cell.reshape(device_count, per_device)
    live_weight = live.reshape(device_count, per_device).astype(jnp.float32)

    def upsampled(cell_index):
        spread = centers[:, cell_index][:, None] + jnp.dot(offsets[:, cell_index], upsample, precision=highest)
        strength = jnp.dot(forces[:, cell_index], upsample, precision=highest)
        return (spread, strength)

    def one_pair(cell_a, cell_b, weight):
        spread_a, strength_a = upsampled(cell_a)
        spread_b, strength_b = upsampled(cell_b)
        on_b = stokeslet(points[:, cell_b], spread_a, strength_a) * weight
        on_a = stokeslet(points[:, cell_a], spread_b, strength_b) * weight
        return (on_a, on_b)

    def one_device(operands):
        return jax.vmap(one_pair)(operands[0], operands[1], operands[2])
    on_a, on_b = lax.map(one_device, (first_cell, second_cell, live_weight))
    near_field = jnp.zeros((3, cells_all, P_SIZE), jnp.float32)
    near_field = near_field.at[:, first_cell.reshape(-1)].add(jnp.moveaxis(on_a.reshape(-1, 3, P_SIZE), 0, 1))
    near_field = near_field.at[:, second_cell.reshape(-1)].add(jnp.moveaxis(on_b.reshape(-1, 3, P_SIZE), 0, 1))
    moment_scale = 1.0 / math.sqrt(N_CELL * CELLS_DEV * P_SIZE)
    slab_points = jnp.moveaxis(points.reshape(3, N_SLAB, N_CELL * CELLS_DEV * P_SIZE), 1, 0)
    slab_forces = jnp.moveaxis(forces.reshape(3, N_SLAB, N_CELL * CELLS_DEV * P_SIZE), 1, 0)

    def moment(operands):
        return jnp.dot(monomials(operands[0]), operands[1].T, precision=highest) * moment_scale
    moments = lax.map(moment, (slab_points, slab_forces))
    empty_slab = jnp.zeros((1, NT, 3), jnp.float32)
    from_below = jnp.concatenate([empty_slab, moments[:-1]], axis=0)
    from_above = jnp.concatenate([moments[1:], empty_slab], axis=0)
    local_coef = jnp.einsum('kj,sjc->skc', translate[0], moments, precision=highest)
    local_coef = local_coef + jnp.einsum('kj,sjc->skc', translate[1], from_below, precision=highest)
    local_coef = local_coef + jnp.einsum('kj,sjc->skc', translate[2], from_above, precision=highest)

    def evaluate(operands):
        return jnp.dot(operands[1].T, monomials(operands[0]), precision=highest)
    far_field = lax.map(evaluate, (slab_points, local_coef))
    far_field = jnp.moveaxis(far_field, 0, 1).reshape(3, cells_all, P_SIZE)
    return near_field + far_field
```

```python
import functools
import math

import jax
import jax.numpy as jnp
from jax import lax
from jax.experimental import pallas as pl
from jax.experimental.pallas import tpu as pltpu
from jax.sharding import PartitionSpec as P

DEGREE = 8
LANE = 128
ROWS = 8
soften = 0.0025
highest = lax.Precision.HIGHEST
f32 = jnp.float32
bf16 = jnp.bfloat16

TERMS = [
    (i, j, k)
    for i in range(DEGREE + 1)
    for j in range(DEGREE + 1 - i)
    for k in range(DEGREE + 1 - i - j)
]
TERM_AT = {term: at for at, term in enumerate(TERMS)}
NT = len(TERMS)
SECTION = 256

NN = (((1,), (0,)), ((), ()))
NT_DIMS = (((1,), (1,)), ((), ()))


def rounded_up(size, unit):
    return -(-size // unit) * unit


def vmem_limit(mib):
    return pltpu.CompilerParams(vmem_limit_bytes=mib * 1024 * 1024)


def work(micros):
    return pl.CostEstimate(flops=int(micros * 1.0e9), bytes_accessed=0, transcendentals=0)


SMEM = pl.BlockSpec(memory_space=pltpu.SMEM)
VMEM = pl.BlockSpec(memory_space=pltpu.VMEM)
HBM = pl.BlockSpec(memory_space=pltpu.HBM)


def fetch(pairs, sems):
    copies = [
        pltpu.make_async_copy(source, target, sems.at[at])
        for at, (source, target) in enumerate(pairs)
    ]
    for copy in copies:
        copy.start()
    return copies


def center_columns(center_row, cells):
    row = lax.broadcasted_iota(jnp.int32, (cells, cells), 0)
    col = lax.broadcasted_iota(jnp.int32, (cells, cells), 1)
    diagonal = jnp.where(row == col, jnp.broadcast_to(center_row, (cells, cells)), 0.0)
    return lax.dot_general(
        diagonal, jnp.ones((cells, LANE), f32), NN, precision=highest, preferred_element_type=f32
    )


def packed_tail(first, second, width):
    gap = jnp.zeros((first.shape[0], LANE // 2 - width), f32)
    return jnp.concatenate([first, gap, second, gap], axis=1)


def pack_points(store, array_ref, coord, shift, cells, count):
    full = count // LANE
    rest = count - full * LANE
    half = cells // 2
    for tile in range(full):
        part = array_ref[coord, :, tile * LANE : (tile + 1) * LANE]
        if shift is not None:
            part = part + shift
        store[coord, tile * cells : (tile + 1) * cells, :] = part
    first = array_ref[coord, :half, full * LANE : count]
    second = array_ref[coord, half:, full * LANE : count]
    if shift is not None:
        first = first + shift[:half, :rest]
        second = second + shift[half:, :rest]
    store[coord, full * cells : full * cells + half, :] = packed_tail(first, second, rest)


def moments_kernel(
    scale, centers_ref, offsets_hbm, forces_hbm, out_ref, offsets_ref, forces_ref, sems, pts, frc, acc
):
    copies = fetch([(offsets_hbm, offsets_ref), (forces_hbm, forces_ref)], sems)
    for copy in copies:
        copy.wait()
    cells, count = offsets_ref.shape[1:]
    for coord in range(3):
        shift = center_columns(centers_ref[coord : coord + 1, :], cells)
        pack_points(pts, offsets_ref, coord, shift, cells, count)
        pack_points(frc, forces_ref, coord, None, cells, count)
    total = pts.shape[1]
    chunk = total // 2

    def one_component(comp, carry):
        for part in range(2):
            rows = slice(part * chunk, (part + 1) * chunk)
            x, y, z = (pts[coord, rows, :] for coord in range(3))
            by_x = frc[comp, rows, :]
            for i in range(DEGREE + 1):
                if i:
                    by_x = by_x * x
                by_y = by_x
                for j in range(DEGREE + 1 - i):
                    if j:
                        by_y = by_y * y
                    by_z = by_y
                    for k in range(DEGREE + 1 - i - j):
                        if k:
                            by_z = by_z * z
                        at = TERM_AT[(i, j, k)] * ROWS
                        summed = jnp.sum(by_z.reshape(chunk // ROWS, ROWS, LANE), axis=0)
                        if part:
                            summed = summed + acc[comp, at : at + ROWS, :]
                        acc[comp, at : at + ROWS, :] = summed
        return carry

    lax.fori_loop(0, 3, one_component, 0)
    out_ref[...] = jnp.zeros_like(out_ref)
    ones = jnp.ones((ROWS, LANE), f32)
    for comp in range(3):
        folded = acc[comp, pl.ds(0, NT, stride=ROWS), :]
        for row in range(1, ROWS):
            folded = folded + acc[comp, pl.ds(row, NT, stride=ROWS), :]
        sums = lax.dot_general(
            ones, folded, NT_DIMS, precision=highest, preferred_element_type=f32
        )
        out_ref[2 * comp : 2 * comp + 1, :] = sums[0:1, 0:LANE] * scale
        out_ref[2 * comp + 1 : 2 * comp + 2, 0 : NT - LANE] = sums[0:1, LANE:NT] * scale


def moments(centers, offsets, forces, scale):
    cells, count = offsets.shape[1:]
    total = cells * (count // LANE) + cells // 2
    return pl.pallas_call(
        functools.partial(moments_kernel, scale),
        out_shape=jax.ShapeDtypeStruct((ROWS, LANE), f32),
        in_specs=[VMEM, HBM, HBM],
        scratch_shapes=[
            pltpu.VMEM(offsets.shape, f32),
            pltpu.VMEM(forces.shape, f32),
            pltpu.SemaphoreType.DMA((2,)),
            pltpu.VMEM((3, total, LANE), f32),
            pltpu.VMEM((3, total, LANE), f32),
            pltpu.VMEM((3, NT * ROWS, LANE), f32),
        ],
        compiler_params=vmem_limit(60),
        cost_estimate=work(3),
        name="moments",
    )(centers, offsets, forces)


PARTNER, LIVE, OWNER = 0, 1, 2


def table_kernel(partner_ref, live_ref, owner_ref, out_ref):
    peers = out_ref.shape[0]
    lane = lax.broadcasted_iota(jnp.int32, (1, LANE), 1)
    out_ref[...] = jnp.zeros_like(out_ref)
    for peer in range(peers):
        for row, ref in ((PARTNER, partner_ref), (LIVE, live_ref), (OWNER, owner_ref)):
            values = jnp.zeros((1, LANE), jnp.int32)
            for slot in range(ref.shape[1]):
                values = jnp.where(lane == slot, ref[0, slot, peer], values)
            out_ref[peer, row : row + 1, :] = values


def pair_table(peer_cell, live, owner_cell):
    turned = [jnp.swapaxes(each, 1, 2) for each in (peer_cell, live, owner_cell)]
    return pl.pallas_call(
        table_kernel,
        out_shape=jax.ShapeDtypeStruct((peer_cell.shape[1], 4, LANE), jnp.int32),
        in_specs=[SMEM, SMEM, SMEM],
        compiler_params=vmem_limit(60),
        name="pair_table",
    )(*turned)


def pack_kernel(
    mine_ref,
    theirs_ref,
    centers_ref,
    offsets_ref,
    forces_ref,
    own_ref,
    inner_ref,
    outer_ref,
    out_ref,
):
    peers, blocks, _, width = out_ref.shape
    slots = blocks // 2
    count = offsets_ref.shape[2]
    out_ref[...] = jnp.zeros_like(out_ref)
    for peer in range(peers):
        for tile, held_ref in enumerate((own_ref, inner_ref, outer_ref)):
            out_ref[peer, blocks - 1, :, tile * LANE : (tile + 1) * LANE] = held_ref[...]

    def one_cell(peer, block, cell):
        for coord in range(3):
            out_ref[peer, block, coord : coord + 1, 0:count] = offsets_ref[
                coord, pl.ds(cell, 1), :
            ]
            out_ref[peer, block, 3 + coord : 4 + coord, 0:count] = forces_ref[
                coord, pl.ds(cell, 1), :
            ]
            out_ref[peer, block, coord : coord + 1, count:width] = jnp.full(
                (1, width - count), centers_ref[coord, cell], f32
            )

    def one_peer(peer, carry):
        for slot in range(slots):
            one_cell(peer, slot, mine_ref[peer, OWNER, slot])
            one_cell(peer, slots + slot, theirs_ref[peer, PARTNER, slot])
        return carry

    lax.fori_loop(0, peers, one_peer, 0)


def pack(mine, theirs, slots, centers, offsets, forces, own, inner, outer):
    peers = mine.shape[0]
    width = rounded_up(offsets.shape[2], LANE)
    return pl.pallas_call(
        pack_kernel,
        out_shape=jax.ShapeDtypeStruct((peers, 2 * slots + 1, ROWS, width), f32),
        in_specs=[SMEM, SMEM, SMEM] + [VMEM] * 5,
        compiler_params=vmem_limit(28),
        cost_estimate=work(1),
        name="pack",
    )(mine, theirs, centers, offsets, forces, own, inner, outer)


def two_parts(value):
    high = value.astype(bf16)
    return high, (value - high.astype(f32)).astype(bf16)


def three_parts(value):
    high = value.astype(bf16).astype(f32)
    rest = value - high
    middle = rest.astype(bf16).astype(f32)
    return high, middle, rest - middle


def upsampled(rows, up_high, up_low):
    size = rows.shape[0]
    rows_high, rows_low = two_parts(rows)
    both = jnp.concatenate([rows_high, rows_low], axis=0)
    by_high = lax.dot_general(both, up_high[...], NN, preferred_element_type=f32)
    by_low = lax.dot_general(rows_high, up_low[...], NN, preferred_element_type=f32)
    return by_high[:size] + (by_high[size:] + by_low)


def near_one(raised, source, target, count, up_count):
    width = target.shape[1]
    up_width = raised.shape[1]
    held = rounded_up(count, 16)
    row = lax.broadcasted_iota(jnp.int32, (ROWS, 1), 0)
    is_place = row < 3

    def by_row(parts):
        result = jnp.zeros((ROWS, parts[0].shape[1]), f32)
        for at, part in enumerate(parts):
            result = jnp.where(row == at, part, result)
        return result

    apart = jnp.where(is_place, source[:, count : count + 1] - target[:, count : count + 1], 0.0)
    both = raised + apart
    z = jnp.where(is_place, both, 0.0)
    z_low = pltpu.roll(z, 3, 0)
    z_sq = jnp.sum(z * z, axis=0, keepdims=True)
    z_dot_g = jnp.sum(z_low * both, axis=0, keepdims=True)
    blocks = [both]
    blocks += [both[a : a + 1] * both for a in range(3)]
    blocks.append((z_sq + 2.0 * soften) * both + z_dot_g * z_low)
    split = [three_parts(block) for block in blocks]
    columns = jnp.concatenate([parts[p] for p in range(3) for parts in split], axis=0).astype(bf16)

    zh, zm, zl = three_parts(-2.0 * z)
    one_z = jnp.ones((1, up_width), f32)
    z_norm = by_row([one_z, one_z, one_z, *three_parts(z_sq + soften)])
    z_side = jnp.concatenate(
        [zh, zh, zm, zm, zl, zh, z_norm, jnp.zeros_like(z_norm)], axis=0
    ).astype(bf16)

    y = jnp.where(is_place, target, 0.0)
    y_sq = jnp.sum(y * y, axis=0, keepdims=True)
    yh, ym, yl = three_parts(y)
    one_y = jnp.ones((1, width), f32)
    y_norm = by_row([*three_parts(y_sq), one_y, one_y, one_y])
    y_side = jnp.concatenate([yh, ym, yh, ym, yh, yl, y_norm, jnp.zeros_like(y_norm)], axis=0)
    y_rows = jnp.transpose(y_side)[0:held].astype(bf16)

    weights = []
    for start in range(0, up_width, SECTION):
        span = slice(start, min(start + SECTION, up_width))
        radius_sq = lax.dot_general(y_rows, z_side[:, span], NN, preferred_element_type=f32)
        inverse = lax.rsqrt(radius_sq)
        weights.append(jnp.concatenate(two_parts(inverse * inverse * inverse), axis=0))
    total = lax.dot_general(
        jnp.concatenate(weights, axis=1), columns, NT_DIMS, preferred_element_type=f32
    )
    summed = total[:held] + total[held:]
    lanes = summed.shape[1]
    summed = jnp.concatenate([summed, jnp.zeros((held, LANE - lanes), f32)], axis=1)
    summed = jnp.concatenate([summed, jnp.zeros((width - held, LANE), f32)], axis=0)
    across = jnp.transpose(summed)
    third = 5 * ROWS
    folded = across[0:third] + (across[third : 2 * third] + across[2 * third : 3 * third])
    plain, constant = folded[0:ROWS], folded[4 * ROWS : 5 * ROWS]
    crossed = [folded[(1 + a) * ROWS : (2 + a) * ROWS] for a in range(3)]
    y_low = pltpu.roll(y, 3, 0)
    along = jnp.sum(y_low * plain, axis=0, keepdims=True)
    for a in range(3):
        along = along - crossed[a][3 + a : 4 + a]
    value = y_sq * plain + y_low * along + constant
    for a in range(3):
        value = value - 2.0 * (y[a : a + 1] * crossed[a])
        turned = jnp.sum(y_low * crossed[a], axis=0, keepdims=True)
        value = value - jnp.where(row == 3 + a, turned, 0.0)
    return value * (1.0 / up_count)


def direction(mine_ref, theirs_ref, peer, block, slots):
    backward = block < slots
    slot = jnp.where(backward, block, block - slots)
    alive = jnp.where(backward, theirs_ref[peer, LIVE, slot], mine_ref[peer, LIVE, slot])
    cell = jnp.where(backward, theirs_ref[peer, PARTNER, slot], mine_ref[peer, OWNER, slot])
    return alive, cell


def opposite(block, slots):
    return jnp.where(block < slots, block + slots, block - slots)


def listed(total, alive, order):
    def body(at, held):
        order[held] = at
        return held + alive(at)

    held = lax.fori_loop(0, total, body, 0)

    @pl.when(held > 0)
    def _():
        order[held] = order[jnp.maximum(held - 1, 0)]

    return held


def split_upsample(upsample_ref, high_ref, low_ref):
    count, up_count = upsample_ref.shape
    below = count // 16 * 16
    beyond = up_count // LANE * LANE
    for ref in (high_ref, low_ref):
        ref[below:, :] = jnp.zeros((ref.shape[0] - below, ref.shape[1]), bf16)
        ref[:, beyond:] = jnp.zeros((ref.shape[0], ref.shape[1] - beyond), bf16)
    high, low = two_parts(upsample_ref[...])
    for ref, part in ((high_ref, high), (low_ref, low)):
        ref[0:count, 0:up_count] = part


def near_self_kernel(
    mine_ref, sent_ref, upsample_ref, out_ref, high_ref, low_ref, raised, order
):
    blocks, width = out_ref.shape[0], out_ref.shape[2]
    slots = blocks // 2
    count, up_count = upsample_ref.shape
    me = lax.axis_index("cell")
    split_upsample(upsample_ref, high_ref, low_ref)
    source = sent_ref[me, 0:blocks]
    raised[...] = upsampled(source.reshape(blocks * ROWS, width), high_ref, low_ref)

    def alive(block):
        return mine_ref[me, LIVE, jnp.where(block < slots, block, block - slots)]

    def compute(block):
        at = pl.multiple_of(block * ROWS, ROWS)
        target = sent_ref[me, opposite(block, slots)]
        return near_one(raised[pl.ds(at, ROWS), :], sent_ref[me, block], target, count, up_count)

    def two(step, carry):
        pair = [order[2 * step + at] for at in range(2)]
        results = [compute(block) for block in pair]
        for block, result in zip(pair, results):
            out_ref[block] = result
        return carry

    held = listed(blocks, alive, order)
    lax.fori_loop(0, (held + 1) // 2, two, 0)


def near_self(mine, sent, upsample):
    _, blocks, _, width = sent.shape
    blocks = blocks - 1
    up_width = rounded_up(upsample.shape[1], LANE)
    return pl.pallas_call(
        near_self_kernel,
        out_shape=jax.ShapeDtypeStruct((blocks, ROWS, width), f32),
        in_specs=[SMEM, VMEM, VMEM],
        scratch_shapes=[
            pltpu.VMEM((width, up_width), bf16),
            pltpu.VMEM((width, up_width), bf16),
            pltpu.VMEM((blocks * ROWS, up_width), f32),
            pltpu.SMEM((blocks + 1,), jnp.int32),
        ],
        compiler_params=vmem_limit(28),
        cost_estimate=work(4),
        name="near_self",
    )(mine, sent, upsample)


def finish_kernel(
    mine_ref,
    theirs_ref,
    centers_ref,
    offsets_ref,
    translate_ref,
    upsample_ref,
    sent_ref,
    recv_ref,
    own_near_ref,
    out_ref,
    high_ref,
    low_ref,
    raised,
    near,
    pts,
    far,
    coef_wide,
    order,
):
    up_count = upsample_ref.shape[1]
    split_upsample(upsample_ref, high_ref, low_ref)
    cells, count = offsets_ref.shape[1:]
    peers, blocks, _, width = recv_ref.shape
    blocks = blocks - 1
    slots = blocks // 2
    me = lax.axis_index("cell")

    def place(pair):
        peer = pair // blocks
        return peer, pair - peer * blocks

    def alive(pair):
        peer, block = place(pair)
        found, _ = direction(mine_ref, theirs_ref, peer, block, slots)
        return jnp.where(peer == me, 0, found)

    held = listed(peers * blocks, alive, order)
    for peer in range(peers):
        rows = recv_ref[peer, 0:blocks].reshape(blocks * ROWS, width)
        near[peer * blocks * ROWS : (peer + 1) * blocks * ROWS, :] = rows

    total = recv_ref[0, blocks]
    for peer in range(1, peers):
        total = total + recv_ref[peer, blocks]
    odd = lax.rem(lax.axis_index("slab"), 2)
    local = jnp.zeros((ROWS, NT), f32)
    for tile, which in enumerate((0, 2 - odd, 1 + odd)):
        summed = total[:, tile * LANE : (tile + 1) * LANE]
        rows = [
            jnp.concatenate([summed[2 * c : 2 * c + 1], summed[2 * c + 1 : 2 * c + 2]], axis=1)
            for c in range(3)
        ]
        rows.append(jnp.zeros((ROWS - 3, 2 * LANE), f32))
        local = local + lax.dot_general(
            jnp.concatenate(rows, axis=0)[:, 0:NT],
            translate_ref[which],
            NT_DIMS,
            precision=highest,
            preferred_element_type=f32,
        )
    nt_width = rounded_up(NT, LANE)
    padded = jnp.concatenate([local, jnp.zeros((ROWS, nt_width - NT), f32)], axis=1)
    tall = jnp.concatenate([padded, jnp.zeros((LANE - ROWS, nt_width), f32)], axis=0)
    upright = jnp.transpose(tall)
    for comp in range(3):
        coef_wide[comp] = jnp.broadcast_to(upright[:, comp : comp + 1], (nt_width, LANE))

    for coord in range(3):
        shift = center_columns(centers_ref[coord : coord + 1, :], cells)
        pack_points(pts, offsets_ref, coord, shift, cells, count)
    raised[...] = upsampled(near[...], high_ref, low_ref)

    def compute(pair):
        peer, block = place(pair)
        at = pl.multiple_of(pair * ROWS, ROWS)
        target = sent_ref[peer, opposite(block, slots)]
        return near_one(raised[pl.ds(at, ROWS), :], recv_ref[peer, block], target, count, up_count)

    def two(step):
        chosen = [order[2 * step + at] for at in range(2)]
        results = [compute(pair) for pair in chosen]
        for pair, result in zip(chosen, results):
            near[pl.ds(pl.multiple_of(pair * ROWS, ROWS), ROWS), :] = result

    slices = 6
    chunk = pts.shape[1] // 4

    def evaluate(step):
        comp = step // 2
        for part in range(2):
            start = pl.multiple_of((step - 2 * comp) * 2 * chunk + part * chunk, ROWS)
            x, y, z = (pts[coord, pl.ds(start, chunk), :] for coord in range(3))
            by_x = None
            for i in range(DEGREE, -1, -1):
                by_y = None
                for j in range(DEGREE - i, -1, -1):
                    by_z = None
                    for k in range(DEGREE - i - j, -1, -1):
                        at = TERM_AT[(i, j, k)]
                        value = coef_wide[comp, at : at + 1, :]
                        by_z = value if by_z is None else by_z * z + value
                    by_y = by_z if by_y is None else by_y * y + by_z
                by_x = by_y if by_x is None else by_x * x + by_y
            far[comp, pl.ds(start, chunk), :] = by_x

    steps = (held + 1) // 2
    shared = jnp.minimum(steps, slices)

    def both(step, carry):
        evaluate(step)
        two(step)
        return carry

    def near_only(step, carry):
        two(step)
        return carry

    def far_only(step, carry):
        evaluate(step)
        return carry

    lax.fori_loop(0, shared, both, 0)
    lax.fori_loop(shared, steps, near_only, 0)
    lax.fori_loop(shared, slices, far_only, 0)

    full = count // LANE
    rest = count - full * LANE
    half = cells // 2
    for comp in range(3):
        for tile in range(full):
            out_ref[comp, :, tile * LANE : (tile + 1) * LANE] = far[
                comp, tile * cells : (tile + 1) * cells, :
            ]
        tail = far[comp, full * cells : full * cells + half, :]
        out_ref[comp, 0:half, full * LANE : count] = tail[:, 0:rest]
        out_ref[comp, half:cells, full * LANE : count] = tail[:, LANE // 2 : LANE // 2 + rest]

    def add(cell, value):
        for comp in range(3):
            out_ref[comp, pl.ds(cell, 1), :] = (
                out_ref[comp, pl.ds(cell, 1), :] + value[3 + comp : 4 + comp, 0:count]
            )

    def add_pair(step, carry):
        pair = order[step]
        peer, block = place(pair)
        _, cell = direction(mine_ref, theirs_ref, peer, block, slots)
        add(cell, near[pl.ds(pl.multiple_of(pair * ROWS, ROWS), ROWS), :])
        return carry

    lax.fori_loop(0, held, add_pair, 0)

    def add_own(block, carry):
        found, cell = direction(mine_ref, theirs_ref, me, block, slots)

        @pl.when(found > 0)
        def _():
            add(cell, own_near_ref[block])

        return carry

    lax.fori_loop(0, blocks, add_own, 0)


def finish(mine, theirs, centers, offsets, translate, upsample, sent, recv, own_near):
    cells, count = offsets.shape[1:]
    peers, blocks, _, width = sent.shape
    blocks = blocks - 1
    total = cells * (count // LANE) + cells // 2
    pairs = peers * blocks
    up_width = rounded_up(upsample.shape[1], LANE)
    return pl.pallas_call(
        finish_kernel,
        out_shape=jax.ShapeDtypeStruct(offsets.shape, f32),
        in_specs=[SMEM, SMEM] + [VMEM] * 7,
        scratch_shapes=[
            pltpu.VMEM((width, up_width), bf16),
            pltpu.VMEM((width, up_width), bf16),
            pltpu.VMEM((pairs * ROWS, up_width), f32),
            pltpu.VMEM((pairs * ROWS, width), f32),
            pltpu.VMEM((3, total, LANE), f32),
            pltpu.VMEM((3, total, LANE), f32),
            pltpu.VMEM((3, rounded_up(NT, LANE), LANE), f32),
            pltpu.SMEM((pairs + 1,), jnp.int32),
        ],
        compiler_params=vmem_limit(28),
        cost_estimate=work(15),
        name="finish",
    )(mine, theirs, centers, offsets, translate, upsample, sent, recv, own_near)


def on_device(centers, offsets, forces, upsample, translate, owner_cell, peer_cell, live):
    cells, count = offsets.shape[1:]
    peers, slots = owner_cell.shape[1:]
    slabs = lax.axis_size("slab")
    exchange = functools.partial(
        lax.all_to_all, axis_name="cell", split_axis=0, concat_axis=0, tiled=True
    )
    mine = pair_table(peer_cell, live, owner_cell)
    theirs = exchange(mine)
    centers, mine = lax.optimization_barrier((centers, mine))
    scale = 1.0 / math.sqrt(cells * peers * count)
    own = moments(centers, offsets, forces, scale)
    swaps = [
        [(i, i + 1) for i in range(first, slabs - 1, 2)]
        + [(i + 1, i) for i in range(first, slabs - 1, 2)]
        for first in (0, 1)
    ]
    inner = lax.ppermute(own, "slab", swaps[0])
    outer = lax.ppermute(own, "slab", swaps[1])
    sent = pack(mine, theirs, slots, centers, offsets, forces, own, inner, outer)
    recv = exchange(sent)
    own_near = near_self(mine, sent, upsample)
    return finish(mine, theirs, centers, offsets, translate, upsample, sent, recv, own_near)


def solution(mesh):
    return jax.shard_map(
        on_device,
        mesh=mesh,
        in_specs=(
            P(None, ("slab", "cell")),
            P(None, ("slab", "cell"), None),
            P(None, ("slab", "cell"), None),
            P(),
            P(),
            P(("slab", "cell"), None, None),
            P(("slab", "cell"), None, None),
            P(("slab", "cell"), None, None),
        ),
        out_specs=P(None, ("slab", "cell"), None),
        check_vma=False,
    )
```

```python
import functools
import math

import jax
import jax.numpy as jnp
from jax import lax
from jax.experimental import pallas as pl
from jax.experimental.pallas import tpu as pltpu
from jax.sharding import PartitionSpec as P

DEGREE = 8
LANE = 128
ROWS = 8
soften = 0.0025
highest = lax.Precision.HIGHEST
f32 = jnp.float32
bf16 = jnp.bfloat16

TERMS = [
    (i, j, k)
    for i in range(DEGREE + 1)
    for j in range(DEGREE + 1 - i)
    for k in range(DEGREE + 1 - i - j)
]
TERM_AT = {term: at for at, term in enumerate(TERMS)}
NT = len(TERMS)
SECTION = 256

NN = (((1,), (0,)), ((), ()))
NT_DIMS = (((1,), (1,)), ((), ()))


def rounded_up(size, unit):
    return -(-size // unit) * unit


def vmem_limit(mib):
    return pltpu.CompilerParams(vmem_limit_bytes=mib * 1024 * 1024)


def work(micros):
    return pl.CostEstimate(flops=int(micros * 1.0e9), bytes_accessed=0, transcendentals=0)


SMEM = pl.BlockSpec(memory_space=pltpu.SMEM)
VMEM = pl.BlockSpec(memory_space=pltpu.VMEM)
HBM = pl.BlockSpec(memory_space=pltpu.HBM)


def fetch(pairs, sems):
    copies = [
        pltpu.make_async_copy(source, target, sems.at[at])
        for at, (source, target) in enumerate(pairs)
    ]
    for copy in copies:
        copy.start()
    return copies


def center_columns(center_row, cells):
    row = lax.broadcasted_iota(jnp.int32, (cells, cells), 0)
    col = lax.broadcasted_iota(jnp.int32, (cells, cells), 1)
    diagonal = jnp.where(row == col, jnp.broadcast_to(center_row, (cells, cells)), 0.0)
    return lax.dot_general(
        diagonal, jnp.ones((cells, LANE), f32), NN, precision=highest, preferred_element_type=f32
    )


def packed_tail(first, second, width):
    gap = jnp.zeros((first.shape[0], LANE // 2 - width), f32)
    return jnp.concatenate([first, gap, second, gap], axis=1)


def pack_points(store, array_ref, coord, shift, cells, count):
    full = count // LANE
    rest = count - full * LANE
    half = cells // 2
    for tile in range(full):
        part = array_ref[coord, :, tile * LANE : (tile + 1) * LANE]
        if shift is not None:
            part = part + shift
        store[coord, tile * cells : (tile + 1) * cells, :] = part
    first = array_ref[coord, :half, full * LANE : count]
    second = array_ref[coord, half:, full * LANE : count]
    if shift is not None:
        first = first + shift[:half, :rest]
        second = second + shift[half:, :rest]
    store[coord, full * cells : full * cells + half, :] = packed_tail(first, second, rest)


def moments_kernel(
    scale, centers_ref, offsets_hbm, forces_hbm, out_ref, offsets_ref, forces_ref, sems, pts, frc, acc
):
    copies = fetch([(offsets_hbm, offsets_ref), (forces_hbm, forces_ref)], sems)
    for copy in copies:
        copy.wait()
    cells, count = offsets_ref.shape[1:]
    for coord in range(3):
        shift = center_columns(centers_ref[coord : coord + 1, :], cells)
        pack_points(pts, offsets_ref, coord, shift, cells, count)
        pack_points(frc, forces_ref, coord, None, cells, count)
    total = pts.shape[1]
    chunk = total // 2

    def one_component(comp, carry):
        for part in range(2):
            rows = slice(part * chunk, (part + 1) * chunk)
            x, y, z = (pts[coord, rows, :] for coord in range(3))
            by_x = frc[comp, rows, :]
            for i in range(DEGREE + 1):
                if i:
                    by_x = by_x * x
                by_y = by_x
                for j in range(DEGREE + 1 - i):
                    if j:
                        by_y = by_y * y
                    by_z = by_y
                    for k in range(DEGREE + 1 - i - j):
                        if k:
                            by_z = by_z * z
                        at = TERM_AT[(i, j, k)] * ROWS
                        summed = jnp.sum(by_z.reshape(chunk // ROWS, ROWS, LANE), axis=0)
                        if part:
                            summed = summed + acc[comp, at : at + ROWS, :]
                        acc[comp, at : at + ROWS, :] = summed
        return carry

    lax.fori_loop(0, 3, one_component, 0)
    out_ref[...] = jnp.zeros_like(out_ref)
    ones = jnp.ones((ROWS, LANE), f32)
    for comp in range(3):
        folded = acc[comp, pl.ds(0, NT, stride=ROWS), :]
        for row in range(1, ROWS):
            folded = folded + acc[comp, pl.ds(row, NT, stride=ROWS), :]
        sums = lax.dot_general(
            ones, folded, NT_DIMS, precision=highest, preferred_element_type=f32
        )
        out_ref[2 * comp : 2 * comp + 1, :] = sums[0:1, 0:LANE] * scale
        out_ref[2 * comp + 1 : 2 * comp + 2, 0 : NT - LANE] = sums[0:1, LANE:NT] * scale


def moments(centers, offsets, forces, scale):
    cells, count = offsets.shape[1:]
    total = cells * (count // LANE) + cells // 2
    return pl.pallas_call(
        functools.partial(moments_kernel, scale),
        out_shape=jax.ShapeDtypeStruct((ROWS, LANE), f32),
        in_specs=[VMEM, HBM, HBM],
        scratch_shapes=[
            pltpu.VMEM(offsets.shape, f32),
            pltpu.VMEM(forces.shape, f32),
            pltpu.SemaphoreType.DMA((2,)),
            pltpu.VMEM((3, total, LANE), f32),
            pltpu.VMEM((3, total, LANE), f32),
            pltpu.VMEM((3, NT * ROWS, LANE), f32),
        ],
        compiler_params=vmem_limit(60),
        cost_estimate=work(3),
        name="moments",
    )(centers, offsets, forces)


PARTNER, LIVE, OWNER = 0, 1, 2
GROUP = 4


def table_kernel(partner_ref, live_ref, owner_ref, out_ref):
    peers = out_ref.shape[0]
    lane = lax.broadcasted_iota(jnp.int32, (1, LANE), 1)
    out_ref[...] = jnp.zeros_like(out_ref)
    for peer in range(peers):
        for row, ref in ((PARTNER, partner_ref), (LIVE, live_ref), (OWNER, owner_ref)):
            values = jnp.zeros((1, LANE), jnp.int32)
            for slot in range(ref.shape[1]):
                values = jnp.where(lane == slot, ref[0, slot, peer], values)
            out_ref[peer, row : row + 1, :] = values


def pair_table(peer_cell, live, owner_cell):
    turned = [jnp.swapaxes(each, 1, 2) for each in (peer_cell, live, owner_cell)]
    return pl.pallas_call(
        table_kernel,
        out_shape=jax.ShapeDtypeStruct((peer_cell.shape[1], 4, LANE), jnp.int32),
        in_specs=[SMEM, SMEM, SMEM],
        compiler_params=vmem_limit(60),
        name="pair_table",
    )(*turned)


def pack_kernel(
    mine_ref,
    theirs_ref,
    centers_ref,
    offsets_ref,
    forces_ref,
    own_ref,
    inner_ref,
    outer_ref,
    out_ref,
):
    peers, blocks, _, width = out_ref.shape
    slots = blocks // 2
    count = offsets_ref.shape[2]
    out_ref[...] = jnp.zeros_like(out_ref)
    for peer in range(peers):
        for tile, held_ref in enumerate((own_ref, inner_ref, outer_ref)):
            out_ref[peer, blocks - 1, :, tile * LANE : (tile + 1) * LANE] = held_ref[...]

    def one_cell(peer, block, cell):
        for coord in range(3):
            out_ref[peer, block, coord : coord + 1, 0:count] = offsets_ref[
                coord, pl.ds(cell, 1), :
            ]
            out_ref[peer, block, 3 + coord : 4 + coord, 0:count] = forces_ref[
                coord, pl.ds(cell, 1), :
            ]
            out_ref[peer, block, coord : coord + 1, count:width] = jnp.full(
                (1, width - count), centers_ref[coord, cell], f32
            )

    def one_peer(peer, carry):
        for slot in range(slots):
            one_cell(peer, slot, mine_ref[peer, OWNER, slot])
            one_cell(peer, slots + slot, theirs_ref[peer, PARTNER, slot])
        return carry

    lax.fori_loop(0, peers, one_peer, 0)


def pack(mine, theirs, slots, centers, offsets, forces, own, inner, outer):
    peers = mine.shape[0]
    width = rounded_up(offsets.shape[2], LANE)
    return pl.pallas_call(
        pack_kernel,
        out_shape=jax.ShapeDtypeStruct((peers, 2 * slots + 1, ROWS, width), f32),
        in_specs=[SMEM, SMEM, SMEM] + [VMEM] * 5,
        compiler_params=vmem_limit(28),
        cost_estimate=work(1),
        name="pack",
    )(mine, theirs, centers, offsets, forces, own, inner, outer)


def two_parts(value):
    high = value.astype(bf16)
    return high, (value - high.astype(f32)).astype(bf16)


def three_parts(value):
    high = value.astype(bf16).astype(f32)
    rest = value - high
    middle = rest.astype(bf16).astype(f32)
    return high, middle, rest - middle


def upsampled(rows, up_high, up_low):
    size = rows.shape[0]
    rows_high, rows_low = two_parts(rows)
    both = jnp.concatenate([rows_high, rows_low], axis=0)
    by_high = lax.dot_general(both, up_high[...], NN, preferred_element_type=f32)
    by_low = lax.dot_general(rows_high, up_low[...], NN, preferred_element_type=f32)
    return by_high[:size] + (by_high[size:] + by_low)


def near_one(raised, source, target, count, up_count):
    width = target.shape[1]
    up_width = raised.shape[1]
    held = rounded_up(count, 16)
    row = lax.broadcasted_iota(jnp.int32, (ROWS, 1), 0)
    is_place = row < 3

    def by_row(parts):
        result = jnp.zeros((ROWS, parts[0].shape[1]), f32)
        for at, part in enumerate(parts):
            result = jnp.where(row == at, part, result)
        return result

    apart = jnp.where(is_place, source[:, count : count + 1] - target[:, count : count + 1], 0.0)
    both = raised + apart
    z = jnp.where(is_place, both, 0.0)
    z_low = pltpu.roll(z, 3, 0)
    z_sq = jnp.sum(z * z, axis=0, keepdims=True)
    z_dot_g = jnp.sum(z_low * both, axis=0, keepdims=True)
    blocks = [both]
    blocks += [both[a : a + 1] * both for a in range(3)]
    blocks.append((z_sq + 2.0 * soften) * both + z_dot_g * z_low)
    split = [three_parts(block) for block in blocks]
    columns = jnp.concatenate([parts[p] for p in range(3) for parts in split], axis=0).astype(bf16)

    zh, zm, zl = three_parts(-2.0 * z)
    one_z = jnp.ones((1, up_width), f32)
    z_norm = by_row([one_z, one_z, one_z, *three_parts(z_sq + soften)])
    z_side = jnp.concatenate(
        [zh, zh, zm, zm, zl, zh, z_norm, jnp.zeros_like(z_norm)], axis=0
    ).astype(bf16)

    y = jnp.where(is_place, target, 0.0)
    y_sq = jnp.sum(y * y, axis=0, keepdims=True)
    yh, ym, yl = three_parts(y)
    one_y = jnp.ones((1, width), f32)
    y_norm = by_row([*three_parts(y_sq), one_y, one_y, one_y])
    y_side = jnp.concatenate([yh, ym, yh, ym, yh, yl, y_norm, jnp.zeros_like(y_norm)], axis=0)
    y_rows = jnp.transpose(y_side)[0:held].astype(bf16)

    weights = []
    for start in range(0, up_width, SECTION):
        span = slice(start, min(start + SECTION, up_width))
        radius_sq = lax.dot_general(y_rows, z_side[:, span], NN, preferred_element_type=f32)
        inverse = lax.rsqrt(radius_sq)
        weights.append(jnp.concatenate(two_parts(inverse * inverse * inverse), axis=0))
    total = lax.dot_general(
        jnp.concatenate(weights, axis=1), columns, NT_DIMS, preferred_element_type=f32
    )
    summed = total[:held] + total[held:]
    lanes = summed.shape[1]
    summed = jnp.concatenate([summed, jnp.zeros((held, LANE - lanes), f32)], axis=1)
    summed = jnp.concatenate([summed, jnp.zeros((width - held, LANE), f32)], axis=0)
    across = jnp.transpose(summed)
    third = 5 * ROWS
    folded = across[0:third] + (across[third : 2 * third] + across[2 * third : 3 * third])
    plain, constant = folded[0:ROWS], folded[4 * ROWS : 5 * ROWS]
    crossed = [folded[(1 + a) * ROWS : (2 + a) * ROWS] for a in range(3)]
    y_low = pltpu.roll(y, 3, 0)
    along = jnp.sum(y_low * plain, axis=0, keepdims=True)
    for a in range(3):
        along = along - crossed[a][3 + a : 4 + a]
    value = y_sq * plain + y_low * along + constant
    for a in range(3):
        value = value - 2.0 * (y[a : a + 1] * crossed[a])
        turned = jnp.sum(y_low * crossed[a], axis=0, keepdims=True)
        value = value - jnp.where(row == 3 + a, turned, 0.0)
    return value * (1.0 / up_count)


def direction(mine_ref, theirs_ref, peer, block, slots):
    backward = block < slots
    slot = jnp.where(backward, block, block - slots)
    alive = jnp.where(backward, theirs_ref[peer, LIVE, slot], mine_ref[peer, LIVE, slot])
    cell = jnp.where(backward, theirs_ref[peer, PARTNER, slot], mine_ref[peer, OWNER, slot])
    return alive, cell


def opposite(block, slots):
    return jnp.where(block < slots, block + slots, block - slots)


def listed(total, alive, order, group):
    def body(at, held):
        order[held] = at
        return held + alive(at)

    held = lax.fori_loop(0, total, body, 0)

    @pl.when(held > 0)
    def _():
        for extra in range(group - 1):
            order[held + extra] = order[jnp.maximum(held - 1, 0)]

    return held


def split_upsample(upsample_ref, high_ref, low_ref):
    count, up_count = upsample_ref.shape
    below = count // 16 * 16
    beyond = up_count // LANE * LANE
    for ref in (high_ref, low_ref):
        ref[below:, :] = jnp.zeros((ref.shape[0] - below, ref.shape[1]), bf16)
        ref[:, beyond:] = jnp.zeros((ref.shape[0], ref.shape[1] - beyond), bf16)
    high, low = two_parts(upsample_ref[...])
    for ref, part in ((high_ref, high), (low_ref, low)):
        ref[0:count, 0:up_count] = part


def near_self_kernel(
    mine_ref, sent_ref, upsample_ref, out_ref, high_ref, low_ref, raised, order
):
    blocks, width = out_ref.shape[0], out_ref.shape[2]
    slots = blocks // 2
    count, up_count = upsample_ref.shape
    me = lax.axis_index("cell")
    split_upsample(upsample_ref, high_ref, low_ref)
    source = sent_ref[me, 0:blocks]
    raised[...] = upsampled(source.reshape(blocks * ROWS, width), high_ref, low_ref)

    def alive(block):
        return mine_ref[me, LIVE, jnp.where(block < slots, block, block - slots)]

    def compute(block):
        at = pl.multiple_of(block * ROWS, ROWS)
        target = sent_ref[me, opposite(block, slots)]
        return near_one(raised[pl.ds(at, ROWS), :], sent_ref[me, block], target, count, up_count)

    def two(step, carry):
        pair = [order[2 * step + at] for at in range(2)]
        results = [compute(block) for block in pair]
        for block, result in zip(pair, results):
            out_ref[block] = result
        return carry

    held = listed(blocks, alive, order, 2)
    lax.fori_loop(0, (held + 1) // 2, two, 0)


def near_self(mine, sent, upsample):
    _, blocks, _, width = sent.shape
    blocks = blocks - 1
    up_width = rounded_up(upsample.shape[1], LANE)
    return pl.pallas_call(
        near_self_kernel,
        out_shape=jax.ShapeDtypeStruct((blocks, ROWS, width), f32),
        in_specs=[SMEM, VMEM, VMEM],
        scratch_shapes=[
            pltpu.VMEM((width, up_width), bf16),
            pltpu.VMEM((width, up_width), bf16),
            pltpu.VMEM((blocks * ROWS, up_width), f32),
            pltpu.SMEM((blocks + 1,), jnp.int32),
        ],
        compiler_params=vmem_limit(28),
        cost_estimate=work(4),
        name="near_self",
    )(mine, sent, upsample)


def finish_kernel(
    mine_ref,
    theirs_ref,
    centers_ref,
    offsets_ref,
    translate_ref,
    upsample_ref,
    sent_ref,
    recv_ref,
    own_near_ref,
    out_ref,
    high_ref,
    low_ref,
    raised,
    near,
    pts,
    far,
    coef_wide,
    order,
):
    up_count = upsample_ref.shape[1]
    split_upsample(upsample_ref, high_ref, low_ref)
    cells, count = offsets_ref.shape[1:]
    peers, blocks, _, width = recv_ref.shape
    blocks = blocks - 1
    slots = blocks // 2
    me = lax.axis_index("cell")

    def place(pair):
        peer = pair // blocks
        return peer, pair - peer * blocks

    def alive(pair):
        peer, block = place(pair)
        found, _ = direction(mine_ref, theirs_ref, peer, block, slots)
        return jnp.where(peer == me, 0, found)

    held = listed(peers * blocks, alive, order, GROUP)
    for peer in range(peers):
        rows = recv_ref[peer, 0:blocks].reshape(blocks * ROWS, width)
        near[peer * blocks * ROWS : (peer + 1) * blocks * ROWS, :] = rows

    total = recv_ref[0, blocks]
    for peer in range(1, peers):
        total = total + recv_ref[peer, blocks]
    odd = lax.rem(lax.axis_index("slab"), 2)
    local = jnp.zeros((ROWS, NT), f32)
    for tile, which in enumerate((0, 2 - odd, 1 + odd)):
        summed = total[:, tile * LANE : (tile + 1) * LANE]
        rows = [
            jnp.concatenate([summed[2 * c : 2 * c + 1], summed[2 * c + 1 : 2 * c + 2]], axis=1)
            for c in range(3)
        ]
        rows.append(jnp.zeros((ROWS - 3, 2 * LANE), f32))
        local = local + lax.dot_general(
            jnp.concatenate(rows, axis=0)[:, 0:NT],
            translate_ref[which],
            NT_DIMS,
            precision=highest,
            preferred_element_type=f32,
        )
    nt_width = rounded_up(NT, LANE)
    padded = jnp.concatenate([local, jnp.zeros((ROWS, nt_width - NT), f32)], axis=1)
    tall = jnp.concatenate([padded, jnp.zeros((LANE - ROWS, nt_width), f32)], axis=0)
    upright = jnp.transpose(tall)
    for comp in range(3):
        coef_wide[comp] = jnp.broadcast_to(upright[:, comp : comp + 1], (nt_width, LANE))

    for coord in range(3):
        shift = center_columns(centers_ref[coord : coord + 1, :], cells)
        pack_points(pts, offsets_ref, coord, shift, cells, count)
    raised[...] = upsampled(near[...], high_ref, low_ref)

    def compute(pair):
        peer, block = place(pair)
        at = pl.multiple_of(pair * ROWS, ROWS)
        target = sent_ref[peer, opposite(block, slots)]
        return near_one(raised[pl.ds(at, ROWS), :], recv_ref[peer, block], target, count, up_count)

    def several(step, carry):
        chosen = [order[GROUP * step + at] for at in range(GROUP)]
        results = [compute(pair) for pair in chosen]
        for pair, result in zip(chosen, results):
            near[pl.ds(pl.multiple_of(pair * ROWS, ROWS), ROWS), :] = result
        return carry

    lax.fori_loop(0, (held + GROUP - 1) // GROUP, several, 0)

    slices = 6
    chunk = pts.shape[1] // 4

    def evaluate(step, carry):
        comp = step // 2
        for part in range(2):
            start = pl.multiple_of((step - 2 * comp) * 2 * chunk + part * chunk, ROWS)
            x, y, z = (pts[coord, pl.ds(start, chunk), :] for coord in range(3))
            by_x = None
            for i in range(DEGREE, -1, -1):
                by_y = None
                for j in range(DEGREE - i, -1, -1):
                    by_z = None
                    for k in range(DEGREE - i - j, -1, -1):
                        at = TERM_AT[(i, j, k)]
                        value = coef_wide[comp, at : at + 1, :]
                        by_z = value if by_z is None else by_z * z + value
                    by_y = by_z if by_y is None else by_y * y + by_z
                by_x = by_y if by_x is None else by_x * x + by_y
            far[comp, pl.ds(start, chunk), :] = by_x
        return carry

    lax.fori_loop(0, slices, evaluate, 0)

    full = count // LANE
    rest = count - full * LANE
    half = cells // 2
    for comp in range(3):
        for tile in range(full):
            out_ref[comp, :, tile * LANE : (tile + 1) * LANE] = far[
                comp, tile * cells : (tile + 1) * cells, :
            ]
        tail = far[comp, full * cells : full * cells + half, :]
        out_ref[comp, 0:half, full * LANE : count] = tail[:, 0:rest]
        out_ref[comp, half:cells, full * LANE : count] = tail[:, LANE // 2 : LANE // 2 + rest]

    def add(cell, value):
        for comp in range(3):
            out_ref[comp, pl.ds(cell, 1), :] = (
                out_ref[comp, pl.ds(cell, 1), :] + value[3 + comp : 4 + comp, 0:count]
            )

    def add_pair(step, carry):
        pair = order[step]
        peer, block = place(pair)
        _, cell = direction(mine_ref, theirs_ref, peer, block, slots)
        add(cell, near[pl.ds(pl.multiple_of(pair * ROWS, ROWS), ROWS), :])
        return carry

    lax.fori_loop(0, held, add_pair, 0)

    def add_own(block, carry):
        found, cell = direction(mine_ref, theirs_ref, me, block, slots)

        @pl.when(found > 0)
        def _():
            add(cell, own_near_ref[block])

        return carry

    lax.fori_loop(0, blocks, add_own, 0)


def finish(mine, theirs, centers, offsets, translate, upsample, sent, recv, own_near):
    cells, count = offsets.shape[1:]
    peers, blocks, _, width = sent.shape
    blocks = blocks - 1
    total = cells * (count // LANE) + cells // 2
    pairs = peers * blocks
    up_width = rounded_up(upsample.shape[1], LANE)
    return pl.pallas_call(
        finish_kernel,
        out_shape=jax.ShapeDtypeStruct(offsets.shape, f32),
        in_specs=[SMEM, SMEM] + [VMEM] * 7,
        scratch_shapes=[
            pltpu.VMEM((width, up_width), bf16),
            pltpu.VMEM((width, up_width), bf16),
            pltpu.VMEM((pairs * ROWS, up_width), f32),
            pltpu.VMEM((pairs * ROWS, width), f32),
            pltpu.VMEM((3, total, LANE), f32),
            pltpu.VMEM((3, total, LANE), f32),
            pltpu.VMEM((3, rounded_up(NT, LANE), LANE), f32),
            pltpu.SMEM((pairs + GROUP,), jnp.int32),
        ],
        compiler_params=vmem_limit(28),
        cost_estimate=work(15),
        name="finish",
    )(mine, theirs, centers, offsets, translate, upsample, sent, recv, own_near)


def on_device(centers, offsets, forces, upsample, translate, owner_cell, peer_cell, live):
    cells, count = offsets.shape[1:]
    peers, slots = owner_cell.shape[1:]
    slabs = lax.axis_size("slab")
    exchange = functools.partial(
        lax.all_to_all, axis_name="cell", split_axis=0, concat_axis=0, tiled=True
    )
    mine = pair_table(peer_cell, live, owner_cell)
    theirs = exchange(mine)
    centers, mine = lax.optimization_barrier((centers, mine))
    scale = 1.0 / math.sqrt(cells * peers * count)
    own = moments(centers, offsets, forces, scale)
    swaps = [
        [(i, i + 1) for i in range(first, slabs - 1, 2)]
        + [(i + 1, i) for i in range(first, slabs - 1, 2)]
        for first in (0, 1)
    ]
    inner = lax.ppermute(own, "slab", swaps[0])
    outer = lax.ppermute(own, "slab", swaps[1])
    sent = pack(mine, theirs, slots, centers, offsets, forces, own, inner, outer)
    recv = exchange(sent)
    own_near = near_self(mine, sent, upsample)
    return finish(mine, theirs, centers, offsets, translate, upsample, sent, recv, own_near)


def solution(mesh):
    return jax.shard_map(
        on_device,
        mesh=mesh,
        in_specs=(
            P(None, ("slab", "cell")),
            P(None, ("slab", "cell"), None),
            P(None, ("slab", "cell"), None),
            P(),
            P(),
            P(("slab", "cell"), None, None),
            P(("slab", "cell"), None, None),
            P(("slab", "cell"), None, None),
        ),
        out_specs=P(None, ("slab", "cell"), None),
        check_vma=False,
    )
```

```python
import functools
import math

import jax
import jax.numpy as jnp
from jax import lax
from jax.experimental import pallas as pl
from jax.experimental.pallas import tpu as pltpu
from jax.sharding import PartitionSpec as P

DEGREE = 8
LANE = 128
ROWS = 8
soften = 0.0025
highest = lax.Precision.HIGHEST
f32 = jnp.float32
bf16 = jnp.bfloat16

TERMS = [
    (i, j, k)
    for i in range(DEGREE + 1)
    for j in range(DEGREE + 1 - i)
    for k in range(DEGREE + 1 - i - j)
]
TERM_AT = {term: at for at, term in enumerate(TERMS)}
NT = len(TERMS)
SECTION = 256

NN = (((1,), (0,)), ((), ()))
NT_DIMS = (((1,), (1,)), ((), ()))


def rounded_up(size, unit):
    return -(-size // unit) * unit


def vmem_limit(mib):
    return pltpu.CompilerParams(vmem_limit_bytes=mib * 1024 * 1024)


def work(micros):
    return pl.CostEstimate(flops=int(micros * 1.0e9), bytes_accessed=0, transcendentals=0)


SMEM = pl.BlockSpec(memory_space=pltpu.SMEM)
VMEM = pl.BlockSpec(memory_space=pltpu.VMEM)
HBM = pl.BlockSpec(memory_space=pltpu.HBM)


def fetch(pairs, sems):
    copies = [
        pltpu.make_async_copy(source, target, sems.at[at])
        for at, (source, target) in enumerate(pairs)
    ]
    for copy in copies:
        copy.start()
    return copies


def center_columns(center_row, cells):
    row = lax.broadcasted_iota(jnp.int32, (cells, cells), 0)
    col = lax.broadcasted_iota(jnp.int32, (cells, cells), 1)
    diagonal = jnp.where(row == col, jnp.broadcast_to(center_row, (cells, cells)), 0.0)
    return lax.dot_general(
        diagonal, jnp.ones((cells, LANE), f32), NN, precision=highest, preferred_element_type=f32
    )


def packed_tail(first, second, width):
    gap = jnp.zeros((first.shape[0], LANE // 2 - width), f32)
    return jnp.concatenate([first, gap, second, gap], axis=1)


def pack_points(store, array_ref, coord, shift, cells, count):
    full = count // LANE
    rest = count - full * LANE
    half = cells // 2
    for tile in range(full):
        part = array_ref[coord, :, tile * LANE : (tile + 1) * LANE]
        if shift is not None:
            part = part + shift
        store[coord, tile * cells : (tile + 1) * cells, :] = part
    first = array_ref[coord, :half, full * LANE : count]
    second = array_ref[coord, half:, full * LANE : count]
    if shift is not None:
        first = first + shift[:half, :rest]
        second = second + shift[half:, :rest]
    store[coord, full * cells : full * cells + half, :] = packed_tail(first, second, rest)


def moments_kernel(
    scale, centers_ref, offsets_hbm, forces_hbm, out_ref, offsets_ref, forces_ref, sems, pts, frc, acc
):
    copies = fetch([(offsets_hbm, offsets_ref), (forces_hbm, forces_ref)], sems)
    for copy in copies:
        copy.wait()
    cells, count = offsets_ref.shape[1:]
    for coord in range(3):
        shift = center_columns(centers_ref[coord : coord + 1, :], cells)
        pack_points(pts, offsets_ref, coord, shift, cells, count)
        pack_points(frc, forces_ref, coord, None, cells, count)
    total = pts.shape[1]
    chunk = total // 2

    def one_component(comp, carry):
        for part in range(2):
            rows = slice(part * chunk, (part + 1) * chunk)
            x, y, z = (pts[coord, rows, :] for coord in range(3))
            by_x = frc[comp, rows, :]
            for i in range(DEGREE + 1):
                if i:
                    by_x = by_x * x
                by_y = by_x
                for j in range(DEGREE + 1 - i):
                    if j:
                        by_y = by_y * y
                    by_z = by_y
                    for k in range(DEGREE + 1 - i - j):
                        if k:
                            by_z = by_z * z
                        at = TERM_AT[(i, j, k)] * ROWS
                        summed = jnp.sum(by_z.reshape(chunk // ROWS, ROWS, LANE), axis=0)
                        if part:
                            summed = summed + acc[comp, at : at + ROWS, :]
                        acc[comp, at : at + ROWS, :] = summed
        return carry

    lax.fori_loop(0, 3, one_component, 0)
    out_ref[...] = jnp.zeros_like(out_ref)
    ones = jnp.ones((ROWS, LANE), f32)
    for comp in range(3):
        folded = acc[comp, pl.ds(0, NT, stride=ROWS), :]
        for row in range(1, ROWS):
            folded = folded + acc[comp, pl.ds(row, NT, stride=ROWS), :]
        sums = lax.dot_general(
            ones, folded, NT_DIMS, precision=highest, preferred_element_type=f32
        )
        out_ref[2 * comp : 2 * comp + 1, :] = sums[0:1, 0:LANE] * scale
        out_ref[2 * comp + 1 : 2 * comp + 2, 0 : NT - LANE] = sums[0:1, LANE:NT] * scale


def moments(centers, offsets, forces, scale):
    cells, count = offsets.shape[1:]
    total = cells * (count // LANE) + cells // 2
    return pl.pallas_call(
        functools.partial(moments_kernel, scale),
        out_shape=jax.ShapeDtypeStruct((ROWS, LANE), f32),
        in_specs=[VMEM, HBM, HBM],
        scratch_shapes=[
            pltpu.VMEM(offsets.shape, f32),
            pltpu.VMEM(forces.shape, f32),
            pltpu.SemaphoreType.DMA((2,)),
            pltpu.VMEM((3, total, LANE), f32),
            pltpu.VMEM((3, total, LANE), f32),
            pltpu.VMEM((3, NT * ROWS, LANE), f32),
        ],
        compiler_params=vmem_limit(60),
        cost_estimate=work(3),
        name="moments",
    )(centers, offsets, forces)


PARTNER, LIVE, OWNER = 0, 1, 2


def table_kernel(partner_ref, live_ref, owner_ref, out_ref):
    peers = out_ref.shape[0]
    lane = lax.broadcasted_iota(jnp.int32, (1, LANE), 1)
    out_ref[...] = jnp.zeros_like(out_ref)
    for peer in range(peers):
        for row, ref in ((PARTNER, partner_ref), (LIVE, live_ref), (OWNER, owner_ref)):
            values = jnp.zeros((1, LANE), jnp.int32)
            for slot in range(ref.shape[1]):
                values = jnp.where(lane == slot, ref[0, slot, peer], values)
            out_ref[peer, row : row + 1, :] = values


def pair_table(peer_cell, live, owner_cell):
    turned = [jnp.swapaxes(each, 1, 2) for each in (peer_cell, live, owner_cell)]
    return pl.pallas_call(
        table_kernel,
        out_shape=jax.ShapeDtypeStruct((peer_cell.shape[1], 4, LANE), jnp.int32),
        in_specs=[SMEM, SMEM, SMEM],
        compiler_params=vmem_limit(60),
        name="pair_table",
    )(*turned)


def pack_kernel(
    mine_ref,
    theirs_ref,
    centers_ref,
    offsets_ref,
    forces_ref,
    own_ref,
    inner_ref,
    outer_ref,
    out_ref,
):
    peers, blocks, _, width = out_ref.shape
    slots = blocks // 2
    count = offsets_ref.shape[2]
    out_ref[...] = jnp.zeros_like(out_ref)
    for peer in range(peers):
        for tile, held_ref in enumerate((own_ref, inner_ref, outer_ref)):
            out_ref[peer, blocks - 1, :, tile * LANE : (tile + 1) * LANE] = held_ref[...]

    def one_cell(peer, block, cell):
        for coord in range(3):
            out_ref[peer, block, coord : coord + 1, 0:count] = offsets_ref[
                coord, pl.ds(cell, 1), :
            ]
            out_ref[peer, block, 3 + coord : 4 + coord, 0:count] = forces_ref[
                coord, pl.ds(cell, 1), :
            ]
            out_ref[peer, block, coord : coord + 1, count:width] = jnp.full(
                (1, width - count), centers_ref[coord, cell], f32
            )

    def one_peer(peer, carry):
        for slot in range(slots):
            one_cell(peer, slot, mine_ref[peer, OWNER, slot])
            one_cell(peer, slots + slot, theirs_ref[peer, PARTNER, slot])
        return carry

    lax.fori_loop(0, peers, one_peer, 0)


def pack(mine, theirs, slots, centers, offsets, forces, own, inner, outer):
    peers = mine.shape[0]
    width = rounded_up(offsets.shape[2], LANE)
    return pl.pallas_call(
        pack_kernel,
        out_shape=jax.ShapeDtypeStruct((peers, 2 * slots + 1, ROWS, width), f32),
        in_specs=[SMEM, SMEM, SMEM] + [VMEM] * 5,
        compiler_params=vmem_limit(28),
        cost_estimate=work(1),
        name="pack",
    )(mine, theirs, centers, offsets, forces, own, inner, outer)


def two_parts(value):
    high = value.astype(bf16)
    return high, (value - high.astype(f32)).astype(bf16)


def three_parts(value):
    high = value.astype(bf16).astype(f32)
    rest = value - high
    middle = rest.astype(bf16).astype(f32)
    return high, middle, rest - middle


def upsampled(rows, up_high, up_low):
    size = rows.shape[0]
    rows_high, rows_low = two_parts(rows)
    both = jnp.concatenate([rows_high, rows_low], axis=0)
    by_high = lax.dot_general(both, up_high[...], NN, preferred_element_type=f32)
    by_low = lax.dot_general(rows_high, up_low[...], NN, preferred_element_type=f32)
    return by_high[:size] + (by_high[size:] + by_low)


def near_one(raised, source, target, count, up_count):
    width = target.shape[1]
    up_width = raised.shape[1]
    held = rounded_up(count, 16)
    row = lax.broadcasted_iota(jnp.int32, (ROWS, 1), 0)
    is_place = row < 3

    def by_row(parts):
        result = jnp.zeros((ROWS, parts[0].shape[1]), f32)
        for at, part in enumerate(parts):
            result = jnp.where(row == at, part, result)
        return result

    apart = jnp.where(is_place, source[:, count : count + 1] - target[:, count : count + 1], 0.0)
    both = raised + apart
    z = jnp.where(is_place, both, 0.0)
    z_low = pltpu.roll(z, 3, 0)
    z_sq = jnp.sum(z * z, axis=0, keepdims=True)
    z_dot_g = jnp.sum(z_low * both, axis=0, keepdims=True)
    blocks = [both]
    blocks += [both[a : a + 1] * both for a in range(3)]
    blocks.append((z_sq + 2.0 * soften) * both + z_dot_g * z_low)
    split = [three_parts(block) for block in blocks]
    columns = jnp.concatenate([parts[p] for p in range(3) for parts in split], axis=0).astype(bf16)

    zh, zm, zl = three_parts(-2.0 * z)
    one_z = jnp.ones((1, up_width), f32)
    z_norm = by_row([one_z, one_z, one_z, *three_parts(z_sq + soften)])
    z_side = jnp.concatenate(
        [zh, zh, zm, zm, zl, zh, z_norm, jnp.zeros_like(z_norm)], axis=0
    ).astype(bf16)

    y = jnp.where(is_place, target, 0.0)
    y_sq = jnp.sum(y * y, axis=0, keepdims=True)
    yh, ym, yl = three_parts(y)
    one_y = jnp.ones((1, width), f32)
    y_norm = by_row([*three_parts(y_sq), one_y, one_y, one_y])
    y_side = jnp.concatenate([yh, ym, yh, ym, yh, yl, y_norm, jnp.zeros_like(y_norm)], axis=0)
    y_rows = jnp.transpose(y_side)[0:held].astype(bf16)

    weights = []
    for start in range(0, up_width, SECTION):
        span = slice(start, min(start + SECTION, up_width))
        radius_sq = lax.dot_general(y_rows, z_side[:, span], NN, preferred_element_type=f32)
        weight = jnp.exp2(lax.log(radius_sq) * (-1.5 / math.log(2.0)))
        weights.append(jnp.concatenate(two_parts(weight), axis=0))
    total = lax.dot_general(
        jnp.concatenate(weights, axis=1), columns, NT_DIMS, preferred_element_type=f32
    )
    summed = total[:held] + total[held:]
    lanes = summed.shape[1]
    summed = jnp.concatenate([summed, jnp.zeros((held, LANE - lanes), f32)], axis=1)
    summed = jnp.concatenate([summed, jnp.zeros((width - held, LANE), f32)], axis=0)
    across = jnp.transpose(summed)
    third = 5 * ROWS
    folded = across[0:third] + (across[third : 2 * third] + across[2 * third : 3 * third])
    plain, constant = folded[0:ROWS], folded[4 * ROWS : 5 * ROWS]
    crossed = [folded[(1 + a) * ROWS : (2 + a) * ROWS] for a in range(3)]
    y_low = pltpu.roll(y, 3, 0)
    along = jnp.sum(y_low * plain, axis=0, keepdims=True)
    for a in range(3):
        along = along - crossed[a][3 + a : 4 + a]
    value = y_sq * plain + y_low * along + constant
    for a in range(3):
        value = value - 2.0 * (y[a : a + 1] * crossed[a])
        turned = jnp.sum(y_low * crossed[a], axis=0, keepdims=True)
        value = value - jnp.where(row == 3 + a, turned, 0.0)
    return value * (1.0 / up_count)


def direction(mine_ref, theirs_ref, peer, block, slots):
    backward = block < slots
    slot = jnp.where(backward, block, block - slots)
    alive = jnp.where(backward, theirs_ref[peer, LIVE, slot], mine_ref[peer, LIVE, slot])
    cell = jnp.where(backward, theirs_ref[peer, PARTNER, slot], mine_ref[peer, OWNER, slot])
    return alive, cell


def opposite(block, slots):
    return jnp.where(block < slots, block + slots, block - slots)


def listed(total, alive, order):
    def body(at, held):
        order[held] = at
        return held + alive(at)

    held = lax.fori_loop(0, total, body, 0)

    @pl.when(held > 0)
    def _():
        order[held] = order[jnp.maximum(held - 1, 0)]

    return held


def split_upsample(upsample_ref, high_ref, low_ref):
    count, up_count = upsample_ref.shape
    below = count // 16 * 16
    beyond = up_count // LANE * LANE
    for ref in (high_ref, low_ref):
        ref[below:, :] = jnp.zeros((ref.shape[0] - below, ref.shape[1]), bf16)
        ref[:, beyond:] = jnp.zeros((ref.shape[0], ref.shape[1] - beyond), bf16)
    high, low = two_parts(upsample_ref[...])
    for ref, part in ((high_ref, high), (low_ref, low)):
        ref[0:count, 0:up_count] = part


def near_self_kernel(
    mine_ref, sent_ref, upsample_ref, out_ref, high_ref, low_ref, raised, order
):
    blocks, width = out_ref.shape[0], out_ref.shape[2]
    slots = blocks // 2
    count, up_count = upsample_ref.shape
    me = lax.axis_index("cell")
    split_upsample(upsample_ref, high_ref, low_ref)
    source = sent_ref[me, 0:blocks]
    raised[...] = upsampled(source.reshape(blocks * ROWS, width), high_ref, low_ref)

    def alive(block):
        return mine_ref[me, LIVE, jnp.where(block < slots, block, block - slots)]

    def compute(block):
        at = pl.multiple_of(block * ROWS, ROWS)
        target = sent_ref[me, opposite(block, slots)]
        return near_one(raised[pl.ds(at, ROWS), :], sent_ref[me, block], target, count, up_count)

    def two(step, carry):
        pair = [order[2 * step + at] for at in range(2)]
        results = [compute(block) for block in pair]
        for block, result in zip(pair, results):
            out_ref[block] = result
        return carry

    held = listed(blocks, alive, order)
    lax.fori_loop(0, (held + 1) // 2, two, 0)


def near_self(mine, sent, upsample):
    _, blocks, _, width = sent.shape
    blocks = blocks - 1
    up_width = rounded_up(upsample.shape[1], LANE)
    return pl.pallas_call(
        near_self_kernel,
        out_shape=jax.ShapeDtypeStruct((blocks, ROWS, width), f32),
        in_specs=[SMEM, VMEM, VMEM],
        scratch_shapes=[
            pltpu.VMEM((width, up_width), bf16),
            pltpu.VMEM((width, up_width), bf16),
            pltpu.VMEM((blocks * ROWS, up_width), f32),
            pltpu.SMEM((blocks + 1,), jnp.int32),
        ],
        compiler_params=vmem_limit(28),
        cost_estimate=work(4),
        name="near_self",
    )(mine, sent, upsample)


def finish_kernel(
    mine_ref,
    theirs_ref,
    centers_ref,
    offsets_ref,
    translate_ref,
    upsample_ref,
    sent_ref,
    recv_ref,
    own_near_ref,
    out_ref,
    high_ref,
    low_ref,
    raised,
    near,
    pts,
    far,
    coef_wide,
    order,
):
    up_count = upsample_ref.shape[1]
    split_upsample(upsample_ref, high_ref, low_ref)
    cells, count = offsets_ref.shape[1:]
    peers, blocks, _, width = recv_ref.shape
    blocks = blocks - 1
    slots = blocks // 2
    me = lax.axis_index("cell")

    def place(pair):
        peer = pair // blocks
        return peer, pair - peer * blocks

    def alive(pair):
        peer, block = place(pair)
        found, _ = direction(mine_ref, theirs_ref, peer, block, slots)
        return jnp.where(peer == me, 0, found)

    held = listed(peers * blocks, alive, order)
    for peer in range(peers):
        rows = recv_ref[peer, 0:blocks].reshape(blocks * ROWS, width)
        near[peer * blocks * ROWS : (peer + 1) * blocks * ROWS, :] = rows

    total = recv_ref[0, blocks]
    for peer in range(1, peers):
        total = total + recv_ref[peer, blocks]
    odd = lax.rem(lax.axis_index("slab"), 2)
    local = jnp.zeros((ROWS, NT), f32)
    for tile, which in enumerate((0, 2 - odd, 1 + odd)):
        summed = total[:, tile * LANE : (tile + 1) * LANE]
        rows = [
            jnp.concatenate([summed[2 * c : 2 * c + 1], summed[2 * c + 1 : 2 * c + 2]], axis=1)
            for c in range(3)
        ]
        rows.append(jnp.zeros((ROWS - 3, 2 * LANE), f32))
        local = local + lax.dot_general(
            jnp.concatenate(rows, axis=0)[:, 0:NT],
            translate_ref[which],
            NT_DIMS,
            precision=highest,
            preferred_element_type=f32,
        )
    nt_width = rounded_up(NT, LANE)
    padded = jnp.concatenate([local, jnp.zeros((ROWS, nt_width - NT), f32)], axis=1)
    tall = jnp.concatenate([padded, jnp.zeros((LANE - ROWS, nt_width), f32)], axis=0)
    upright = jnp.transpose(tall)
    for comp in range(3):
        coef_wide[comp] = jnp.broadcast_to(upright[:, comp : comp + 1], (nt_width, LANE))

    for coord in range(3):
        shift = center_columns(centers_ref[coord : coord + 1, :], cells)
        pack_points(pts, offsets_ref, coord, shift, cells, count)
    raised[...] = upsampled(near[...], high_ref, low_ref)

    def compute(pair):
        peer, block = place(pair)
        at = pl.multiple_of(pair * ROWS, ROWS)
        target = sent_ref[peer, opposite(block, slots)]
        return near_one(raised[pl.ds(at, ROWS), :], recv_ref[peer, block], target, count, up_count)

    def two(step):
        chosen = [order[2 * step + at] for at in range(2)]
        results = [compute(pair) for pair in chosen]
        for pair, result in zip(chosen, results):
            near[pl.ds(pl.multiple_of(pair * ROWS, ROWS), ROWS), :] = result

    slices = 6
    chunk = pts.shape[1] // 4

    def evaluate(step):
        comp = step // 2
        for part in range(2):
            start = pl.multiple_of((step - 2 * comp) * 2 * chunk + part * chunk, ROWS)
            x, y, z = (pts[coord, pl.ds(start, chunk), :] for coord in range(3))
            by_x = None
            for i in range(DEGREE, -1, -1):
                by_y = None
                for j in range(DEGREE - i, -1, -1):
                    by_z = None
                    for k in range(DEGREE - i - j, -1, -1):
                        at = TERM_AT[(i, j, k)]
                        value = coef_wide[comp, at : at + 1, :]
                        by_z = value if by_z is None else by_z * z + value
                    by_y = by_z if by_y is None else by_y * y + by_z
                by_x = by_y if by_x is None else by_x * x + by_y
            far[comp, pl.ds(start, chunk), :] = by_x

    steps = (held + 1) // 2
    shared = jnp.minimum(steps, slices)

    def both(step, carry):
        evaluate(step)
        two(step)
        return carry

    def near_only(step, carry):
        two(step)
        return carry

    def far_only(step, carry):
        evaluate(step)
        return carry

    lax.fori_loop(0, shared, both, 0)
    lax.fori_loop(shared, steps, near_only, 0)
    lax.fori_loop(shared, slices, far_only, 0)

    full = count // LANE
    rest = count - full * LANE
    half = cells // 2
    for comp in range(3):
        for tile in range(full):
            out_ref[comp, :, tile * LANE : (tile + 1) * LANE] = far[
                comp, tile * cells : (tile + 1) * cells, :
            ]
        tail = far[comp, full * cells : full * cells + half, :]
        out_ref[comp, 0:half, full * LANE : count] = tail[:, 0:rest]
        out_ref[comp, half:cells, full * LANE : count] = tail[:, LANE // 2 : LANE // 2 + rest]

    def add(cell, value):
        for comp in range(3):
            out_ref[comp, pl.ds(cell, 1), :] = (
                out_ref[comp, pl.ds(cell, 1), :] + value[3 + comp : 4 + comp, 0:count]
            )

    def add_pair(step, carry):
        pair = order[step]
        peer, block = place(pair)
        _, cell = direction(mine_ref, theirs_ref, peer, block, slots)
        add(cell, near[pl.ds(pl.multiple_of(pair * ROWS, ROWS), ROWS), :])
        return carry

    lax.fori_loop(0, held, add_pair, 0)

    def add_own(block, carry):
        found, cell = direction(mine_ref, theirs_ref, me, block, slots)

        @pl.when(found > 0)
        def _():
            add(cell, own_near_ref[block])

        return carry

    lax.fori_loop(0, blocks, add_own, 0)


def finish(mine, theirs, centers, offsets, translate, upsample, sent, recv, own_near):
    cells, count = offsets.shape[1:]
    peers, blocks, _, width = sent.shape
    blocks = blocks - 1
    total = cells * (count // LANE) + cells // 2
    pairs = peers * blocks
    up_width = rounded_up(upsample.shape[1], LANE)
    return pl.pallas_call(
        finish_kernel,
        out_shape=jax.ShapeDtypeStruct(offsets.shape, f32),
        in_specs=[SMEM, SMEM] + [VMEM] * 7,
        scratch_shapes=[
            pltpu.VMEM((width, up_width), bf16),
            pltpu.VMEM((width, up_width), bf16),
            pltpu.VMEM((pairs * ROWS, up_width), f32),
            pltpu.VMEM((pairs * ROWS, width), f32),
            pltpu.VMEM((3, total, LANE), f32),
            pltpu.VMEM((3, total, LANE), f32),
            pltpu.VMEM((3, rounded_up(NT, LANE), LANE), f32),
            pltpu.SMEM((pairs + 1,), jnp.int32),
        ],
        compiler_params=vmem_limit(28),
        cost_estimate=work(15),
        name="finish",
    )(mine, theirs, centers, offsets, translate, upsample, sent, recv, own_near)


def on_device(centers, offsets, forces, upsample, translate, owner_cell, peer_cell, live):
    cells, count = offsets.shape[1:]
    peers, slots = owner_cell.shape[1:]
    slabs = lax.axis_size("slab")
    exchange = functools.partial(
        lax.all_to_all, axis_name="cell", split_axis=0, concat_axis=0, tiled=True
    )
    mine = pair_table(peer_cell, live, owner_cell)
    theirs = exchange(mine)
    centers, mine = lax.optimization_barrier((centers, mine))
    scale = 1.0 / math.sqrt(cells * peers * count)
    own = moments(centers, offsets, forces, scale)
    swaps = [
        [(i, i + 1) for i in range(first, slabs - 1, 2)]
        + [(i + 1, i) for i in range(first, slabs - 1, 2)]
        for first in (0, 1)
    ]
    inner = lax.ppermute(own, "slab", swaps[0])
    outer = lax.ppermute(own, "slab", swaps[1])
    sent = pack(mine, theirs, slots, centers, offsets, forces, own, inner, outer)
    recv = exchange(sent)
    own_near = near_self(mine, sent, upsample)
    return finish(mine, theirs, centers, offsets, translate, upsample, sent, recv, own_near)


def solution(mesh):
    return jax.shard_map(
        on_device,
        mesh=mesh,
        in_specs=(
            P(None, ("slab", "cell")),
            P(None, ("slab", "cell"), None),
            P(None, ("slab", "cell"), None),
            P(),
            P(),
            P(("slab", "cell"), None, None),
            P(("slab", "cell"), None, None),
            P(("slab", "cell"), None, None),
        ),
        out_specs=P(None, ("slab", "cell"), None),
        check_vma=False,
    )
```

```python
import functools
import math

import jax
import jax.numpy as jnp
from jax import lax
from jax.experimental import pallas as pl
from jax.experimental.pallas import tpu as pltpu
from jax.sharding import PartitionSpec as P

DEGREE = 8
LANE = 128
ROWS = 8
soften = 0.0025
highest = lax.Precision.HIGHEST
f32 = jnp.float32
bf16 = jnp.bfloat16

TERMS = [
    (i, j, k)
    for i in range(DEGREE + 1)
    for j in range(DEGREE + 1 - i)
    for k in range(DEGREE + 1 - i - j)
]
TERM_AT = {term: at for at, term in enumerate(TERMS)}
NT = len(TERMS)
SECTION = 256

NN = (((1,), (0,)), ((), ()))
NT_DIMS = (((1,), (1,)), ((), ()))


def rounded_up(size, unit):
    return -(-size // unit) * unit


def vmem_limit(mib):
    return pltpu.CompilerParams(vmem_limit_bytes=mib * 1024 * 1024)


def work(micros):
    return pl.CostEstimate(flops=int(micros * 1.0e9), bytes_accessed=0, transcendentals=0)


SMEM = pl.BlockSpec(memory_space=pltpu.SMEM)
VMEM = pl.BlockSpec(memory_space=pltpu.VMEM)
HBM = pl.BlockSpec(memory_space=pltpu.HBM)


def fetch(pairs, sems):
    copies = [
        pltpu.make_async_copy(source, target, sems.at[at])
        for at, (source, target) in enumerate(pairs)
    ]
    for copy in copies:
        copy.start()
    return copies


def center_columns(center_row, cells):
    row = lax.broadcasted_iota(jnp.int32, (cells, cells), 0)
    col = lax.broadcasted_iota(jnp.int32, (cells, cells), 1)
    diagonal = jnp.where(row == col, jnp.broadcast_to(center_row, (cells, cells)), 0.0)
    return lax.dot_general(
        diagonal, jnp.ones((cells, LANE), f32), NN, precision=highest, preferred_element_type=f32
    )


def packed_tail(first, second, width):
    gap = jnp.zeros((first.shape[0], LANE // 2 - width), f32)
    return jnp.concatenate([first, gap, second, gap], axis=1)


def pack_points(store, array_ref, coord, shift, cells, count):
    full = count // LANE
    rest = count - full * LANE
    half = cells // 2
    for tile in range(full):
        part = array_ref[coord, :, tile * LANE : (tile + 1) * LANE]
        if shift is not None:
            part = part + shift
        store[coord, tile * cells : (tile + 1) * cells, :] = part
    first = array_ref[coord, :half, full * LANE : count]
    second = array_ref[coord, half:, full * LANE : count]
    if shift is not None:
        first = first + shift[:half, :rest]
        second = second + shift[half:, :rest]
    store[coord, full * cells : full * cells + half, :] = packed_tail(first, second, rest)


def moments_kernel(
    scale, centers_ref, offsets_hbm, forces_hbm, out_ref, offsets_ref, forces_ref, sems, pts, frc, acc
):
    copies = fetch([(offsets_hbm, offsets_ref), (forces_hbm, forces_ref)], sems)
    for copy in copies:
        copy.wait()
    cells, count = offsets_ref.shape[1:]
    for coord in range(3):
        shift = center_columns(centers_ref[coord : coord + 1, :], cells)
        pack_points(pts, offsets_ref, coord, shift, cells, count)
        pack_points(frc, forces_ref, coord, None, cells, count)
    total = pts.shape[1]
    chunk = total // 2

    def one_component(comp, carry):
        for part in range(2):
            rows = slice(part * chunk, (part + 1) * chunk)
            x, y, z = (pts[coord, rows, :] for coord in range(3))
            by_x = frc[comp, rows, :]
            for i in range(DEGREE + 1):
                if i:
                    by_x = by_x * x
                by_y = by_x
                for j in range(DEGREE + 1 - i):
                    if j:
                        by_y = by_y * y
                    by_z = by_y
                    for k in range(DEGREE + 1 - i - j):
                        if k:
                            by_z = by_z * z
                        at = TERM_AT[(i, j, k)] * ROWS
                        summed = jnp.sum(by_z.reshape(chunk // ROWS, ROWS, LANE), axis=0)
                        if part:
                            summed = summed + acc[comp, at : at + ROWS, :]
                        acc[comp, at : at + ROWS, :] = summed
        return carry

    lax.fori_loop(0, 3, one_component, 0)
    out_ref[...] = jnp.zeros_like(out_ref)
    ones = jnp.ones((ROWS, LANE), f32)
    for comp in range(3):
        folded = acc[comp, pl.ds(0, NT, stride=ROWS), :]
        for row in range(1, ROWS):
            folded = folded + acc[comp, pl.ds(row, NT, stride=ROWS), :]
        sums = lax.dot_general(
            ones, folded, NT_DIMS, precision=highest, preferred_element_type=f32
        )
        out_ref[2 * comp : 2 * comp + 1, :] = sums[0:1, 0:LANE] * scale
        out_ref[2 * comp + 1 : 2 * comp + 2, 0 : NT - LANE] = sums[0:1, LANE:NT] * scale


def moments(centers, offsets, forces, scale):
    cells, count = offsets.shape[1:]
    total = cells * (count // LANE) + cells // 2
    return pl.pallas_call(
        functools.partial(moments_kernel, scale),
        out_shape=jax.ShapeDtypeStruct((ROWS, LANE), f32),
        in_specs=[VMEM, HBM, HBM],
        scratch_shapes=[
            pltpu.VMEM(offsets.shape, f32),
            pltpu.VMEM(forces.shape, f32),
            pltpu.SemaphoreType.DMA((2,)),
            pltpu.VMEM((3, total, LANE), f32),
            pltpu.VMEM((3, total, LANE), f32),
            pltpu.VMEM((3, NT * ROWS, LANE), f32),
        ],
        compiler_params=vmem_limit(60),
        cost_estimate=work(3),
        name="moments",
    )(centers, offsets, forces)


PARTNER, LIVE, OWNER = 0, 1, 2


def table_kernel(partner_ref, live_ref, owner_ref, out_ref):
    peers = out_ref.shape[0]
    lane = lax.broadcasted_iota(jnp.int32, (1, LANE), 1)
    out_ref[...] = jnp.zeros_like(out_ref)
    for peer in range(peers):
        for row, ref in ((PARTNER, partner_ref), (LIVE, live_ref), (OWNER, owner_ref)):
            values = jnp.zeros((1, LANE), jnp.int32)
            for slot in range(ref.shape[1]):
                values = jnp.where(lane == slot, ref[0, slot, peer], values)
            out_ref[peer, row : row + 1, :] = values


def pair_table(peer_cell, live, owner_cell):
    turned = [jnp.swapaxes(each, 1, 2) for each in (peer_cell, live, owner_cell)]
    return pl.pallas_call(
        table_kernel,
        out_shape=jax.ShapeDtypeStruct((peer_cell.shape[1], 4, LANE), jnp.int32),
        in_specs=[SMEM, SMEM, SMEM],
        compiler_params=vmem_limit(60),
        name="pair_table",
    )(*turned)


def pack_kernel(
    mine_ref,
    theirs_ref,
    centers_ref,
    offsets_ref,
    forces_ref,
    own_ref,
    inner_ref,
    outer_ref,
    out_ref,
):
    peers, blocks, _, width = out_ref.shape
    slots = blocks // 2
    count = offsets_ref.shape[2]
    out_ref[...] = jnp.zeros_like(out_ref)
    for peer in range(peers):
        for tile, held_ref in enumerate((own_ref, inner_ref, outer_ref)):
            out_ref[peer, blocks - 1, :, tile * LANE : (tile + 1) * LANE] = held_ref[...]

    def one_cell(peer, block, cell):
        for coord in range(3):
            out_ref[peer, block, coord : coord + 1, 0:count] = offsets_ref[
                coord, pl.ds(cell, 1), :
            ]
            out_ref[peer, block, 3 + coord : 4 + coord, 0:count] = forces_ref[
                coord, pl.ds(cell, 1), :
            ]
            out_ref[peer, block, coord : coord + 1, count:width] = jnp.full(
                (1, width - count), centers_ref[coord, cell], f32
            )

    def one_peer(peer, carry):
        for slot in range(slots):
            one_cell(peer, slot, mine_ref[peer, OWNER, slot])
            one_cell(peer, slots + slot, theirs_ref[peer, PARTNER, slot])
        return carry

    lax.fori_loop(0, peers, one_peer, 0)


def pack(mine, theirs, slots, centers, offsets, forces, own, inner, outer):
    peers = mine.shape[0]
    width = rounded_up(offsets.shape[2], LANE)
    return pl.pallas_call(
        pack_kernel,
        out_shape=jax.ShapeDtypeStruct((peers, 2 * slots + 1, ROWS, width), f32),
        in_specs=[SMEM, SMEM, SMEM] + [VMEM] * 5,
        compiler_params=vmem_limit(28),
        cost_estimate=work(1),
        name="pack",
    )(mine, theirs, centers, offsets, forces, own, inner, outer)


def two_parts(value):
    high = value.astype(bf16)
    return high, (value - high.astype(f32)).astype(bf16)


def three_parts(value):
    high = value.astype(bf16).astype(f32)
    rest = value - high
    middle = rest.astype(bf16).astype(f32)
    return high, middle, rest - middle


def upsampled(rows, up_high, up_low):
    size = rows.shape[0]
    rows_high, rows_low = two_parts(rows)
    both = jnp.concatenate([rows_high, rows_low], axis=0)
    by_high = lax.dot_general(both, up_high[...], NN, preferred_element_type=f32)
    by_low = lax.dot_general(rows_high, up_low[...], NN, preferred_element_type=f32)
    return by_high[:size] + (by_high[size:] + by_low)


def woven(pieces, beside=None):
    results = [None] * len(pieces)
    open_ones = list(range(len(pieces)))
    while open_ones:
        for at in list(open_ones):
            try:
                next(pieces[at])
            except StopIteration as stop:
                results[at] = stop.value
                open_ones.remove(at)
            if beside is not None:
                next(beside, None)
    if beside is not None:
        for _ in beside:
            pass
    return results


def near_one(raised, source, target, count, up_count):
    width = target.shape[1]
    up_width = raised.shape[1]
    held = rounded_up(count, 16)
    row = lax.broadcasted_iota(jnp.int32, (ROWS, 1), 0)
    is_place = row < 3

    def by_row(parts):
        result = jnp.zeros((ROWS, parts[0].shape[1]), f32)
        for at, part in enumerate(parts):
            result = jnp.where(row == at, part, result)
        return result

    apart = jnp.where(is_place, source[:, count : count + 1] - target[:, count : count + 1], 0.0)
    both = raised + apart
    z = jnp.where(is_place, both, 0.0)
    z_low = pltpu.roll(z, 3, 0)
    z_sq = jnp.sum(z * z, axis=0, keepdims=True)
    z_dot_g = jnp.sum(z_low * both, axis=0, keepdims=True)
    blocks = [both]
    blocks += [both[a : a + 1] * both for a in range(3)]
    blocks.append((z_sq + 2.0 * soften) * both + z_dot_g * z_low)
    split = [three_parts(block) for block in blocks]
    columns = jnp.concatenate([parts[p] for p in range(3) for parts in split], axis=0).astype(bf16)

    zh, zm, zl = three_parts(-2.0 * z)
    one_z = jnp.ones((1, up_width), f32)
    z_norm = by_row([one_z, one_z, one_z, *three_parts(z_sq + soften)])
    z_side = jnp.concatenate(
        [zh, zh, zm, zm, zl, zh, z_norm, jnp.zeros_like(z_norm)], axis=0
    ).astype(bf16)

    y = jnp.where(is_place, target, 0.0)
    y_sq = jnp.sum(y * y, axis=0, keepdims=True)
    yh, ym, yl = three_parts(y)
    one_y = jnp.ones((1, width), f32)
    y_norm = by_row([*three_parts(y_sq), one_y, one_y, one_y])
    y_side = jnp.concatenate([yh, ym, yh, ym, yh, yl, y_norm, jnp.zeros_like(y_norm)], axis=0)
    y_rows = jnp.transpose(y_side)[0:held].astype(bf16)

    yield
    highs, lows = [], []
    for start in range(0, up_width, SECTION):
        span = slice(start, min(start + SECTION, up_width))
        radius_sq = lax.dot_general(y_rows, z_side[:, span], NN, preferred_element_type=f32)
        inverse = lax.rsqrt(radius_sq)
        high, low = two_parts(inverse * inverse * inverse)
        highs.append(high)
        lows.append(low)
        yield
    by_high = lax.dot_general(
        jnp.concatenate(highs, axis=1), columns, NT_DIMS, preferred_element_type=f32
    )
    yield
    by_low = lax.dot_general(
        jnp.concatenate(lows, axis=1), columns, NT_DIMS, preferred_element_type=f32
    )
    yield
    summed = by_high + by_low
    lanes = summed.shape[1]
    summed = jnp.concatenate([summed, jnp.zeros((held, LANE - lanes), f32)], axis=1)
    summed = jnp.concatenate([summed, jnp.zeros((width - held, LANE), f32)], axis=0)
    across = jnp.transpose(summed)
    third = 5 * ROWS
    folded = across[0:third] + (across[third : 2 * third] + across[2 * third : 3 * third])
    plain, constant = folded[0:ROWS], folded[4 * ROWS : 5 * ROWS]
    crossed = [folded[(1 + a) * ROWS : (2 + a) * ROWS] for a in range(3)]
    y_low = pltpu.roll(y, 3, 0)
    along = jnp.sum(y_low * plain, axis=0, keepdims=True)
    for a in range(3):
        along = along - crossed[a][3 + a : 4 + a]
    value = y_sq * plain + y_low * along + constant
    for a in range(3):
        value = value - 2.0 * (y[a : a + 1] * crossed[a])
        turned = jnp.sum(y_low * crossed[a], axis=0, keepdims=True)
        value = value - jnp.where(row == 3 + a, turned, 0.0)
    return value * (1.0 / up_count)


def direction(mine_ref, theirs_ref, peer, block, slots):
    backward = block < slots
    slot = jnp.where(backward, block, block - slots)
    alive = jnp.where(backward, theirs_ref[peer, LIVE, slot], mine_ref[peer, LIVE, slot])
    cell = jnp.where(backward, theirs_ref[peer, PARTNER, slot], mine_ref[peer, OWNER, slot])
    return alive, cell


def opposite(block, slots):
    return jnp.where(block < slots, block + slots, block - slots)


def listed(total, alive, order):
    def body(at, held):
        order[held] = at
        return held + alive(at)

    held = lax.fori_loop(0, total, body, 0)

    @pl.when(held > 0)
    def _():
        order[held] = order[jnp.maximum(held - 1, 0)]

    return held


def split_upsample(upsample_ref, high_ref, low_ref):
    count, up_count = upsample_ref.shape
    below = count // 16 * 16
    beyond = up_count // LANE * LANE
    for ref in (high_ref, low_ref):
        ref[below:, :] = jnp.zeros((ref.shape[0] - below, ref.shape[1]), bf16)
        ref[:, beyond:] = jnp.zeros((ref.shape[0], ref.shape[1] - beyond), bf16)
    high, low = two_parts(upsample_ref[...])
    for ref, part in ((high_ref, high), (low_ref, low)):
        ref[0:count, 0:up_count] = part


def near_self_kernel(
    mine_ref, sent_ref, upsample_ref, out_ref, high_ref, low_ref, raised, order
):
    blocks, width = out_ref.shape[0], out_ref.shape[2]
    slots = blocks // 2
    count, up_count = upsample_ref.shape
    me = lax.axis_index("cell")
    split_upsample(upsample_ref, high_ref, low_ref)
    source = sent_ref[me, 0:blocks]
    raised[...] = upsampled(source.reshape(blocks * ROWS, width), high_ref, low_ref)

    def alive(block):
        return mine_ref[me, LIVE, jnp.where(block < slots, block, block - slots)]

    def compute(block):
        at = pl.multiple_of(block * ROWS, ROWS)
        target = sent_ref[me, opposite(block, slots)]
        return near_one(raised[pl.ds(at, ROWS), :], sent_ref[me, block], target, count, up_count)

    def two(step, carry):
        pair = [order[2 * step + at] for at in range(2)]
        results = woven([compute(block) for block in pair])
        for block, result in zip(pair, results):
            out_ref[block] = result
        return carry

    held = listed(blocks, alive, order)
    lax.fori_loop(0, (held + 1) // 2, two, 0)


def near_self(mine, sent, upsample):
    _, blocks, _, width = sent.shape
    blocks = blocks - 1
    up_width = rounded_up(upsample.shape[1], LANE)
    return pl.pallas_call(
        near_self_kernel,
        out_shape=jax.ShapeDtypeStruct((blocks, ROWS, width), f32),
        in_specs=[SMEM, VMEM, VMEM],
        scratch_shapes=[
            pltpu.VMEM((width, up_width), bf16),
            pltpu.VMEM((width, up_width), bf16),
            pltpu.VMEM((blocks * ROWS, up_width), f32),
            pltpu.SMEM((blocks + 1,), jnp.int32),
        ],
        compiler_params=vmem_limit(28),
        cost_estimate=work(4),
        name="near_self",
    )(mine, sent, upsample)


def finish_kernel(
    mine_ref,
    theirs_ref,
    centers_ref,
    offsets_ref,
    translate_ref,
    upsample_ref,
    sent_ref,
    recv_ref,
    own_near_ref,
    out_ref,
    high_ref,
    low_ref,
    raised,
    near,
    pts,
    far,
    coef_wide,
    order,
):
    up_count = upsample_ref.shape[1]
    split_upsample(upsample_ref, high_ref, low_ref)
    cells, count = offsets_ref.shape[1:]
    peers, blocks, _, width = recv_ref.shape
    blocks = blocks - 1
    slots = blocks // 2
    me = lax.axis_index("cell")

    def place(pair):
        peer = pair // blocks
        return peer, pair - peer * blocks

    def alive(pair):
        peer, block = place(pair)
        found, _ = direction(mine_ref, theirs_ref, peer, block, slots)
        return jnp.where(peer == me, 0, found)

    held = listed(peers * blocks, alive, order)
    for peer in range(peers):
        rows = recv_ref[peer, 0:blocks].reshape(blocks * ROWS, width)
        near[peer * blocks * ROWS : (peer + 1) * blocks * ROWS, :] = rows

    total = recv_ref[0, blocks]
    for peer in range(1, peers):
        total = total + recv_ref[peer, blocks]
    odd = lax.rem(lax.axis_index("slab"), 2)
    local = jnp.zeros((ROWS, NT), f32)
    for tile, which in enumerate((0, 2 - odd, 1 + odd)):
        summed = total[:, tile * LANE : (tile + 1) * LANE]
        rows = [
            jnp.concatenate([summed[2 * c : 2 * c + 1], summed[2 * c + 1 : 2 * c + 2]], axis=1)
            for c in range(3)
        ]
        rows.append(jnp.zeros((ROWS - 3, 2 * LANE), f32))
        local = local + lax.dot_general(
            jnp.concatenate(rows, axis=0)[:, 0:NT],
            translate_ref[which],
            NT_DIMS,
            precision=highest,
            preferred_element_type=f32,
        )
    nt_width = rounded_up(NT, LANE)
    padded = jnp.concatenate([local, jnp.zeros((ROWS, nt_width - NT), f32)], axis=1)
    tall = jnp.concatenate([padded, jnp.zeros((LANE - ROWS, nt_width), f32)], axis=0)
    upright = jnp.transpose(tall)
    for comp in range(3):
        coef_wide[comp] = jnp.broadcast_to(upright[:, comp : comp + 1], (nt_width, LANE))

    for coord in range(3):
        shift = center_columns(centers_ref[coord : coord + 1, :], cells)
        pack_points(pts, offsets_ref, coord, shift, cells, count)
    raised[...] = upsampled(near[...], high_ref, low_ref)

    def compute(pair):
        peer, block = place(pair)
        at = pl.multiple_of(pair * ROWS, ROWS)
        target = sent_ref[peer, opposite(block, slots)]
        return near_one(raised[pl.ds(at, ROWS), :], recv_ref[peer, block], target, count, up_count)

    def two(step, beside=None):
        chosen = [order[2 * step + at] for at in range(2)]
        results = woven([compute(pair) for pair in chosen], beside)
        for pair, result in zip(chosen, results):
            near[pl.ds(pl.multiple_of(pair * ROWS, ROWS), ROWS), :] = result

    slices = 6
    chunk = pts.shape[1] // 4

    def evaluate(step):
        comp = step // 2
        for part in range(2):
            start = pl.multiple_of((step - 2 * comp) * 2 * chunk + part * chunk, ROWS)
            x, y, z = (pts[coord, pl.ds(start, chunk), :] for coord in range(3))
            by_x = None
            for i in range(DEGREE, -1, -1):
                by_y = None
                for j in range(DEGREE - i, -1, -1):
                    by_z = None
                    for k in range(DEGREE - i - j, -1, -1):
                        at = TERM_AT[(i, j, k)]
                        value = coef_wide[comp, at : at + 1, :]
                        by_z = value if by_z is None else by_z * z + value
                    by_y = by_z if by_y is None else by_y * y + by_z
                by_x = by_y if by_x is None else by_x * x + by_y
                yield
            far[comp, pl.ds(start, chunk), :] = by_x

    steps = (held + 1) // 2
    shared = jnp.minimum(steps, slices)

    def both(step, carry):
        two(step, evaluate(step))
        return carry

    def near_only(step, carry):
        two(step)
        return carry

    def far_only(step, carry):
        woven([evaluate(step)])
        return carry

    lax.fori_loop(0, shared, both, 0)
    lax.fori_loop(shared, steps, near_only, 0)
    lax.fori_loop(shared, slices, far_only, 0)

    full = count // LANE
    rest = count - full * LANE
    half = cells // 2
    for comp in range(3):
        for tile in range(full):
            out_ref[comp, :, tile * LANE : (tile + 1) * LANE] = far[
                comp, tile * cells : (tile + 1) * cells, :
            ]
        tail = far[comp, full * cells : full * cells + half, :]
        out_ref[comp, 0:half, full * LANE : count] = tail[:, 0:rest]
        out_ref[comp, half:cells, full * LANE : count] = tail[:, LANE // 2 : LANE // 2 + rest]

    def add(cell, value):
        for comp in range(3):
            out_ref[comp, pl.ds(cell, 1), :] = (
                out_ref[comp, pl.ds(cell, 1), :] + value[3 + comp : 4 + comp, 0:count]
            )

    def add_pair(step, carry):
        pair = order[step]
        peer, block = place(pair)
        _, cell = direction(mine_ref, theirs_ref, peer, block, slots)
        add(cell, near[pl.ds(pl.multiple_of(pair * ROWS, ROWS), ROWS), :])
        return carry

    lax.fori_loop(0, held, add_pair, 0)

    def add_own(block, carry):
        found, cell = direction(mine_ref, theirs_ref, me, block, slots)

        @pl.when(found > 0)
        def _():
            add(cell, own_near_ref[block])

        return carry

    lax.fori_loop(0, blocks, add_own, 0)


def finish(mine, theirs, centers, offsets, translate, upsample, sent, recv, own_near):
    cells, count = offsets.shape[1:]
    peers, blocks, _, width = sent.shape
    blocks = blocks - 1
    total = cells * (count // LANE) + cells // 2
    pairs = peers * blocks
    up_width = rounded_up(upsample.shape[1], LANE)
    return pl.pallas_call(
        finish_kernel,
        out_shape=jax.ShapeDtypeStruct(offsets.shape, f32),
        in_specs=[SMEM, SMEM] + [VMEM] * 7,
        scratch_shapes=[
            pltpu.VMEM((width, up_width), bf16),
            pltpu.VMEM((width, up_width), bf16),
            pltpu.VMEM((pairs * ROWS, up_width), f32),
            pltpu.VMEM((pairs * ROWS, width), f32),
            pltpu.VMEM((3, total, LANE), f32),
            pltpu.VMEM((3, total, LANE), f32),
            pltpu.VMEM((3, rounded_up(NT, LANE), LANE), f32),
            pltpu.SMEM((pairs + 1,), jnp.int32),
        ],
        compiler_params=vmem_limit(28),
        cost_estimate=work(15),
        name="finish",
    )(mine, theirs, centers, offsets, translate, upsample, sent, recv, own_near)


def on_device(centers, offsets, forces, upsample, translate, owner_cell, peer_cell, live):
    cells, count = offsets.shape[1:]
    peers, slots = owner_cell.shape[1:]
    slabs = lax.axis_size("slab")
    exchange = functools.partial(
        lax.all_to_all, axis_name="cell", split_axis=0, concat_axis=0, tiled=True
    )
    mine = pair_table(peer_cell, live, owner_cell)
    theirs = exchange(mine)
    centers, mine = lax.optimization_barrier((centers, mine))
    scale = 1.0 / math.sqrt(cells * peers * count)
    own = moments(centers, offsets, forces, scale)
    swaps = [
        [(i, i + 1) for i in range(first, slabs - 1, 2)]
        + [(i + 1, i) for i in range(first, slabs - 1, 2)]
        for first in (0, 1)
    ]
    inner = lax.ppermute(own, "slab", swaps[0])
    outer = lax.ppermute(own, "slab", swaps[1])
    sent = pack(mine, theirs, slots, centers, offsets, forces, own, inner, outer)
    recv = exchange(sent)
    own_near = near_self(mine, sent, upsample)
    return finish(mine, theirs, centers, offsets, translate, upsample, sent, recv, own_near)


def solution(mesh):
    return jax.shard_map(
        on_device,
        mesh=mesh,
        in_specs=(
            P(None, ("slab", "cell")),
            P(None, ("slab", "cell"), None),
            P(None, ("slab", "cell"), None),
            P(),
            P(),
            P(("slab", "cell"), None, None),
            P(("slab", "cell"), None, None),
            P(("slab", "cell"), None, None),
        ),
        out_specs=P(None, ("slab", "cell"), None),
        check_vma=False,
    )
```

```python
import functools
import math

import jax
import jax.numpy as jnp
from jax import lax
from jax.experimental import pallas as pl
from jax.experimental.pallas import tpu as pltpu
from jax.sharding import PartitionSpec as P

DEGREE = 8
LANE = 128
ROWS = 8
soften = 0.0025
highest = lax.Precision.HIGHEST
f32 = jnp.float32
bf16 = jnp.bfloat16

TERMS = [
    (i, j, k)
    for i in range(DEGREE + 1)
    for j in range(DEGREE + 1 - i)
    for k in range(DEGREE + 1 - i - j)
]
TERM_AT = {term: at for at, term in enumerate(TERMS)}
NT = len(TERMS)
SECTION = 256

NN = (((1,), (0,)), ((), ()))
NT_DIMS = (((1,), (1,)), ((), ()))


def rounded_up(size, unit):
    return -(-size // unit) * unit


def vmem_limit(mib):
    return pltpu.CompilerParams(vmem_limit_bytes=mib * 1024 * 1024)


def work(micros):
    return pl.CostEstimate(flops=int(micros * 1.0e9), bytes_accessed=0, transcendentals=0)


SMEM = pl.BlockSpec(memory_space=pltpu.SMEM)
VMEM = pl.BlockSpec(memory_space=pltpu.VMEM)
HBM = pl.BlockSpec(memory_space=pltpu.HBM)


def fetch(pairs, sems):
    copies = [
        pltpu.make_async_copy(source, target, sems.at[at])
        for at, (source, target) in enumerate(pairs)
    ]
    for copy in copies:
        copy.start()
    return copies


def center_columns(center_row, cells):
    row = lax.broadcasted_iota(jnp.int32, (cells, cells), 0)
    col = lax.broadcasted_iota(jnp.int32, (cells, cells), 1)
    diagonal = jnp.where(row == col, jnp.broadcast_to(center_row, (cells, cells)), 0.0)
    return lax.dot_general(
        diagonal, jnp.ones((cells, LANE), f32), NN, precision=highest, preferred_element_type=f32
    )


def packed_tail(first, second, width):
    gap = jnp.zeros((first.shape[0], LANE // 2 - width), f32)
    return jnp.concatenate([first, gap, second, gap], axis=1)


def pack_points(store, array_ref, coord, shift, cells, count):
    full = count // LANE
    rest = count - full * LANE
    half = cells // 2
    for tile in range(full):
        part = array_ref[coord, :, tile * LANE : (tile + 1) * LANE]
        if shift is not None:
            part = part + shift
        store[coord, tile * cells : (tile + 1) * cells, :] = part
    first = array_ref[coord, :half, full * LANE : count]
    second = array_ref[coord, half:, full * LANE : count]
    if shift is not None:
        first = first + shift[:half, :rest]
        second = second + shift[half:, :rest]
    store[coord, full * cells : full * cells + half, :] = packed_tail(first, second, rest)


def moments_kernel(
    scale, centers_ref, offsets_hbm, forces_hbm, out_ref, offsets_ref, forces_ref, sems, pts, frc, acc
):
    copies = fetch([(offsets_hbm, offsets_ref), (forces_hbm, forces_ref)], sems)
    for copy in copies:
        copy.wait()
    cells, count = offsets_ref.shape[1:]
    for coord in range(3):
        shift = center_columns(centers_ref[coord : coord + 1, :], cells)
        pack_points(pts, offsets_ref, coord, shift, cells, count)
        pack_points(frc, forces_ref, coord, None, cells, count)
    total = pts.shape[1]
    chunk = total // 2

    def one_component(comp, carry):
        for part in range(2):
            rows = slice(part * chunk, (part + 1) * chunk)
            x, y, z = (pts[coord, rows, :] for coord in range(3))
            by_x = frc[comp, rows, :]
            for i in range(DEGREE + 1):
                if i:
                    by_x = by_x * x
                by_y = by_x
                for j in range(DEGREE + 1 - i):
                    if j:
                        by_y = by_y * y
                    by_z = by_y
                    for k in range(DEGREE + 1 - i - j):
                        if k:
                            by_z = by_z * z
                        at = TERM_AT[(i, j, k)] * ROWS
                        summed = jnp.sum(by_z.reshape(chunk // ROWS, ROWS, LANE), axis=0)
                        if part:
                            summed = summed + acc[comp, at : at + ROWS, :]
                        acc[comp, at : at + ROWS, :] = summed
        return carry

    lax.fori_loop(0, 3, one_component, 0)
    out_ref[...] = jnp.zeros_like(out_ref)
    ones = jnp.ones((ROWS, LANE), f32)
    for comp in range(3):
        folded = acc[comp, pl.ds(0, NT, stride=ROWS), :]
        for row in range(1, ROWS):
            folded = folded + acc[comp, pl.ds(row, NT, stride=ROWS), :]
        sums = lax.dot_general(
            ones, folded, NT_DIMS, precision=highest, preferred_element_type=f32
        )
        out_ref[2 * comp : 2 * comp + 1, :] = sums[0:1, 0:LANE] * scale
        out_ref[2 * comp + 1 : 2 * comp + 2, 0 : NT - LANE] = sums[0:1, LANE:NT] * scale


def moments(centers, offsets, forces, scale):
    cells, count = offsets.shape[1:]
    total = cells * (count // LANE) + cells // 2
    return pl.pallas_call(
        functools.partial(moments_kernel, scale),
        out_shape=jax.ShapeDtypeStruct((ROWS, LANE), f32),
        in_specs=[VMEM, HBM, HBM],
        scratch_shapes=[
            pltpu.VMEM(offsets.shape, f32),
            pltpu.VMEM(forces.shape, f32),
            pltpu.SemaphoreType.DMA((2,)),
            pltpu.VMEM((3, total, LANE), f32),
            pltpu.VMEM((3, total, LANE), f32),
            pltpu.VMEM((3, NT * ROWS, LANE), f32),
        ],
        compiler_params=vmem_limit(60),
        cost_estimate=work(3),
        name="moments",
    )(centers, offsets, forces)


PARTNER, LIVE, OWNER = 0, 1, 2


def table_kernel(partner_ref, live_ref, owner_ref, out_ref):
    peers = out_ref.shape[0]
    lane = lax.broadcasted_iota(jnp.int32, (1, LANE), 1)
    out_ref[...] = jnp.zeros_like(out_ref)
    for peer in range(peers):
        for row, ref in ((PARTNER, partner_ref), (LIVE, live_ref), (OWNER, owner_ref)):
            values = jnp.zeros((1, LANE), jnp.int32)
            for slot in range(ref.shape[1]):
                values = jnp.where(lane == slot, ref[0, slot, peer], values)
            out_ref[peer, row : row + 1, :] = values


def pair_table(peer_cell, live, owner_cell):
    turned = [jnp.swapaxes(each, 1, 2) for each in (peer_cell, live, owner_cell)]
    return pl.pallas_call(
        table_kernel,
        out_shape=jax.ShapeDtypeStruct((peer_cell.shape[1], 4, LANE), jnp.int32),
        in_specs=[SMEM, SMEM, SMEM],
        compiler_params=vmem_limit(60),
        name="pair_table",
    )(*turned)


def pack_kernel(
    mine_ref,
    theirs_ref,
    centers_ref,
    offsets_ref,
    forces_ref,
    own_ref,
    inner_ref,
    outer_ref,
    out_ref,
):
    peers, blocks, _, width = out_ref.shape
    slots = blocks // 2
    count = offsets_ref.shape[2]
    out_ref[...] = jnp.zeros_like(out_ref)
    for peer in range(peers):
        for tile, held_ref in enumerate((own_ref, inner_ref, outer_ref)):
            out_ref[peer, blocks - 1, :, tile * LANE : (tile + 1) * LANE] = held_ref[...]

    def one_cell(peer, block, cell):
        for coord in range(3):
            out_ref[peer, block, coord : coord + 1, 0:count] = offsets_ref[
                coord, pl.ds(cell, 1), :
            ]
            out_ref[peer, block, 3 + coord : 4 + coord, 0:count] = forces_ref[
                coord, pl.ds(cell, 1), :
            ]
            out_ref[peer, block, coord : coord + 1, count:width] = jnp.full(
                (1, width - count), centers_ref[coord, cell], f32
            )

    def one_peer(peer, carry):
        for slot in range(slots):
            one_cell(peer, slot, mine_ref[peer, OWNER, slot])
            one_cell(peer, slots + slot, theirs_ref[peer, PARTNER, slot])
        return carry

    lax.fori_loop(0, peers, one_peer, 0)


def pack(mine, theirs, slots, centers, offsets, forces, own, inner, outer):
    peers = mine.shape[0]
    width = rounded_up(offsets.shape[2], LANE)
    return pl.pallas_call(
        pack_kernel,
        out_shape=jax.ShapeDtypeStruct((peers, 2 * slots + 1, ROWS, width), f32),
        in_specs=[SMEM, SMEM, SMEM] + [VMEM] * 5,
        compiler_params=vmem_limit(28),
        cost_estimate=work(1),
        name="pack",
    )(mine, theirs, centers, offsets, forces, own, inner, outer)


def two_parts(value):
    high = value.astype(bf16)
    return high, (value - high.astype(f32)).astype(bf16)


def three_parts(value):
    high = value.astype(bf16).astype(f32)
    rest = value - high
    middle = rest.astype(bf16).astype(f32)
    return high, middle, rest - middle


def upsampled(rows, up_high, up_low):
    size = rows.shape[0]
    rows_high, rows_low = two_parts(rows)
    both = jnp.concatenate([rows_high, rows_low], axis=0)
    by_high = lax.dot_general(both, up_high[...], NN, preferred_element_type=f32)
    by_low = lax.dot_general(rows_high, up_low[...], NN, preferred_element_type=f32)
    return by_high[:size] + (by_high[size:] + by_low)


def near_one(raised, source, target, count, up_count):
    width = target.shape[1]
    up_width = raised.shape[1]
    held = rounded_up(count, 16)
    row = lax.broadcasted_iota(jnp.int32, (ROWS, 1), 0)
    is_place = row < 3

    def by_row(parts):
        result = jnp.zeros((ROWS, parts[0].shape[1]), f32)
        for at, part in enumerate(parts):
            result = jnp.where(row == at, part, result)
        return result

    apart = jnp.where(is_place, source[:, count : count + 1] - target[:, count : count + 1], 0.0)
    both = raised + apart
    z = jnp.where(is_place, both, 0.0)
    z_low = pltpu.roll(z, 3, 0)
    z_sq = jnp.sum(z * z, axis=0, keepdims=True)
    z_dot_g = jnp.sum(z_low * both, axis=0, keepdims=True)
    blocks = [both]
    blocks += [both[a : a + 1] * both for a in range(3)]
    blocks.append((z_sq + 2.0 * soften) * both + z_dot_g * z_low)
    split = [three_parts(block) for block in blocks]
    columns = jnp.concatenate([parts[p] for p in range(3) for parts in split], axis=0)

    zh, zm, zl = three_parts(-2.0 * z)
    one_z = jnp.ones((1, up_width), f32)
    z_norm = by_row([one_z, one_z, one_z, *three_parts(z_sq + soften)])
    z_side = jnp.concatenate(
        [zh, zh, zm, zm, zl, zh, z_norm, jnp.zeros_like(z_norm)], axis=0
    )

    y = jnp.where(is_place, target, 0.0)
    y_sq = jnp.sum(y * y, axis=0, keepdims=True)
    yh, ym, yl = three_parts(y)
    one_y = jnp.ones((1, width), f32)
    y_norm = by_row([*three_parts(y_sq), one_y, one_y, one_y])
    y_side = jnp.concatenate([yh, ym, yh, ym, yh, yl, y_norm, jnp.zeros_like(y_norm)], axis=0)
    y_rows = jnp.transpose(y_side)[0:held]

    weights = []
    for start in range(0, up_width, SECTION):
        span = slice(start, min(start + SECTION, up_width))
        radius_sq = lax.dot_general(y_rows, z_side[:, span], NN, preferred_element_type=f32)
        inverse = lax.rsqrt(radius_sq)
        weight = inverse * inverse * inverse
        scaled = weight * 65537.0
        high = scaled - (scaled - weight)
        weights.append(jnp.concatenate([high, weight - high], axis=0))
    total = lax.dot_general(
        jnp.concatenate(weights, axis=1), columns, NT_DIMS, preferred_element_type=f32
    )
    summed = total[:held] + total[held:]
    lanes = summed.shape[1]
    summed = jnp.concatenate([summed, jnp.zeros((held, LANE - lanes), f32)], axis=1)
    summed = jnp.concatenate([summed, jnp.zeros((width - held, LANE), f32)], axis=0)
    across = jnp.transpose(summed)
    third = 5 * ROWS
    folded = across[0:third] + (across[third : 2 * third] + across[2 * third : 3 * third])
    plain, constant = folded[0:ROWS], folded[4 * ROWS : 5 * ROWS]
    crossed = [folded[(1 + a) * ROWS : (2 + a) * ROWS] for a in range(3)]
    y_low = pltpu.roll(y, 3, 0)
    along = jnp.sum(y_low * plain, axis=0, keepdims=True)
    for a in range(3):
        along = along - crossed[a][3 + a : 4 + a]
    value = y_sq * plain + y_low * along + constant
    for a in range(3):
        value = value - 2.0 * (y[a : a + 1] * crossed[a])
        turned = jnp.sum(y_low * crossed[a], axis=0, keepdims=True)
        value = value - jnp.where(row == 3 + a, turned, 0.0)
    return value * (1.0 / up_count)


def direction(mine_ref, theirs_ref, peer, block, slots):
    backward = block < slots
    slot = jnp.where(backward, block, block - slots)
    alive = jnp.where(backward, theirs_ref[peer, LIVE, slot], mine_ref[peer, LIVE, slot])
    cell = jnp.where(backward, theirs_ref[peer, PARTNER, slot], mine_ref[peer, OWNER, slot])
    return alive, cell


def opposite(block, slots):
    return jnp.where(block < slots, block + slots, block - slots)


def listed(total, alive, order):
    def body(at, held):
        order[held] = at
        return held + alive(at)

    held = lax.fori_loop(0, total, body, 0)

    @pl.when(held > 0)
    def _():
        order[held] = order[jnp.maximum(held - 1, 0)]

    return held


def split_upsample(upsample_ref, high_ref, low_ref):
    count, up_count = upsample_ref.shape
    below = count // 16 * 16
    beyond = up_count // LANE * LANE
    for ref in (high_ref, low_ref):
        ref[below:, :] = jnp.zeros((ref.shape[0] - below, ref.shape[1]), bf16)
        ref[:, beyond:] = jnp.zeros((ref.shape[0], ref.shape[1] - beyond), bf16)
    high, low = two_parts(upsample_ref[...])
    for ref, part in ((high_ref, high), (low_ref, low)):
        ref[0:count, 0:up_count] = part


def near_self_kernel(
    mine_ref, sent_ref, upsample_ref, out_ref, high_ref, low_ref, raised, order
):
    blocks, width = out_ref.shape[0], out_ref.shape[2]
    slots = blocks // 2
    count, up_count = upsample_ref.shape
    me = lax.axis_index("cell")
    split_upsample(upsample_ref, high_ref, low_ref)
    source = sent_ref[me, 0:blocks]
    raised[...] = upsampled(source.reshape(blocks * ROWS, width), high_ref, low_ref)

    def alive(block):
        return mine_ref[me, LIVE, jnp.where(block < slots, block, block - slots)]

    def compute(block):
        at = pl.multiple_of(block * ROWS, ROWS)
        target = sent_ref[me, opposite(block, slots)]
        return near_one(raised[pl.ds(at, ROWS), :], sent_ref[me, block], target, count, up_count)

    def two(step, carry):
        pair = [order[2 * step + at] for at in range(2)]
        results = [compute(block) for block in pair]
        for block, result in zip(pair, results):
            out_ref[block] = result
        return carry

    held = listed(blocks, alive, order)
    lax.fori_loop(0, (held + 1) // 2, two, 0)


def near_self(mine, sent, upsample):
    _, blocks, _, width = sent.shape
    blocks = blocks - 1
    up_width = rounded_up(upsample.shape[1], LANE)
    return pl.pallas_call(
        near_self_kernel,
        out_shape=jax.ShapeDtypeStruct((blocks, ROWS, width), f32),
        in_specs=[SMEM, VMEM, VMEM],
        scratch_shapes=[
            pltpu.VMEM((width, up_width), bf16),
            pltpu.VMEM((width, up_width), bf16),
            pltpu.VMEM((blocks * ROWS, up_width), f32),
            pltpu.SMEM((blocks + 1,), jnp.int32),
        ],
        compiler_params=vmem_limit(28),
        cost_estimate=work(4),
        name="near_self",
    )(mine, sent, upsample)


def finish_kernel(
    mine_ref,
    theirs_ref,
    centers_ref,
    offsets_ref,
    translate_ref,
    upsample_ref,
    sent_ref,
    recv_ref,
    own_near_ref,
    out_ref,
    high_ref,
    low_ref,
    raised,
    near,
    pts,
    far,
    coef_wide,
    order,
):
    up_count = upsample_ref.shape[1]
    split_upsample(upsample_ref, high_ref, low_ref)
    cells, count = offsets_ref.shape[1:]
    peers, blocks, _, width = recv_ref.shape
    blocks = blocks - 1
    slots = blocks // 2
    me = lax.axis_index("cell")

    def place(pair):
        peer = pair // blocks
        return peer, pair - peer * blocks

    def alive(pair):
        peer, block = place(pair)
        found, _ = direction(mine_ref, theirs_ref, peer, block, slots)
        return jnp.where(peer == me, 0, found)

    held = listed(peers * blocks, alive, order)
    for peer in range(peers):
        rows = recv_ref[peer, 0:blocks].reshape(blocks * ROWS, width)
        near[peer * blocks * ROWS : (peer + 1) * blocks * ROWS, :] = rows

    total = recv_ref[0, blocks]
    for peer in range(1, peers):
        total = total + recv_ref[peer, blocks]
    odd = lax.rem(lax.axis_index("slab"), 2)
    local = jnp.zeros((ROWS, NT), f32)
    for tile, which in enumerate((0, 2 - odd, 1 + odd)):
        summed = total[:, tile * LANE : (tile + 1) * LANE]
        rows = [
            jnp.concatenate([summed[2 * c : 2 * c + 1], summed[2 * c + 1 : 2 * c + 2]], axis=1)
            for c in range(3)
        ]
        rows.append(jnp.zeros((ROWS - 3, 2 * LANE), f32))
        local = local + lax.dot_general(
            jnp.concatenate(rows, axis=0)[:, 0:NT],
            translate_ref[which],
            NT_DIMS,
            precision=highest,
            preferred_element_type=f32,
        )
    nt_width = rounded_up(NT, LANE)
    padded = jnp.concatenate([local, jnp.zeros((ROWS, nt_width - NT), f32)], axis=1)
    tall = jnp.concatenate([padded, jnp.zeros((LANE - ROWS, nt_width), f32)], axis=0)
    upright = jnp.transpose(tall)
    for comp in range(3):
        coef_wide[comp] = jnp.broadcast_to(upright[:, comp : comp + 1], (nt_width, LANE))

    for coord in range(3):
        shift = center_columns(centers_ref[coord : coord + 1, :], cells)
        pack_points(pts, offsets_ref, coord, shift, cells, count)
    raised[...] = upsampled(near[...], high_ref, low_ref)

    def compute(pair):
        peer, block = place(pair)
        at = pl.multiple_of(pair * ROWS, ROWS)
        target = sent_ref[peer, opposite(block, slots)]
        return near_one(raised[pl.ds(at, ROWS), :], recv_ref[peer, block], target, count, up_count)

    def two(step):
        chosen = [order[2 * step + at] for at in range(2)]
        results = [compute(pair) for pair in chosen]
        for pair, result in zip(chosen, results):
            near[pl.ds(pl.multiple_of(pair * ROWS, ROWS), ROWS), :] = result

    slices = 6
    chunk = pts.shape[1] // 4

    def evaluate(step):
        comp = step // 2
        for part in range(2):
            start = pl.multiple_of((step - 2 * comp) * 2 * chunk + part * chunk, ROWS)
            x, y, z = (pts[coord, pl.ds(start, chunk), :] for coord in range(3))
            by_x = None
            for i in range(DEGREE, -1, -1):
                by_y = None
                for j in range(DEGREE - i, -1, -1):
                    by_z = None
                    for k in range(DEGREE - i - j, -1, -1):
                        at = TERM_AT[(i, j, k)]
                        value = coef_wide[comp, at : at + 1, :]
                        by_z = value if by_z is None else by_z * z + value
                    by_y = by_z if by_y is None else by_y * y + by_z
                by_x = by_y if by_x is None else by_x * x + by_y
            far[comp, pl.ds(start, chunk), :] = by_x

    steps = (held + 1) // 2
    shared = jnp.minimum(steps, slices)

    def both(step, carry):
        evaluate(step)
        two(step)
        return carry

    def near_only(step, carry):
        two(step)
        return carry

    def far_only(step, carry):
        evaluate(step)
        return carry

    lax.fori_loop(0, shared, both, 0)
    lax.fori_loop(shared, steps, near_only, 0)
    lax.fori_loop(shared, slices, far_only, 0)

    full = count // LANE
    rest = count - full * LANE
    half = cells // 2
    for comp in range(3):
        for tile in range(full):
            out_ref[comp, :, tile * LANE : (tile + 1) * LANE] = far[
                comp, tile * cells : (tile + 1) * cells, :
            ]
        tail = far[comp, full * cells : full * cells + half, :]
        out_ref[comp, 0:half, full * LANE : count] = tail[:, 0:rest]
        out_ref[comp, half:cells, full * LANE : count] = tail[:, LANE // 2 : LANE // 2 + rest]

    def add(cell, value):
        for comp in range(3):
            out_ref[comp, pl.ds(cell, 1), :] = (
                out_ref[comp, pl.ds(cell, 1), :] + value[3 + comp : 4 + comp, 0:count]
            )

    def add_pair(step, carry):
        pair = order[step]
        peer, block = place(pair)
        _, cell = direction(mine_ref, theirs_ref, peer, block, slots)
        add(cell, near[pl.ds(pl.multiple_of(pair * ROWS, ROWS), ROWS), :])
        return carry

    lax.fori_loop(0, held, add_pair, 0)

    def add_own(block, carry):
        found, cell = direction(mine_ref, theirs_ref, me, block, slots)

        @pl.when(found > 0)
        def _():
            add(cell, own_near_ref[block])

        return carry

    lax.fori_loop(0, blocks, add_own, 0)


def finish(mine, theirs, centers, offsets, translate, upsample, sent, recv, own_near):
    cells, count = offsets.shape[1:]
    peers, blocks, _, width = sent.shape
    blocks = blocks - 1
    total = cells * (count // LANE) + cells // 2
    pairs = peers * blocks
    up_width = rounded_up(upsample.shape[1], LANE)
    return pl.pallas_call(
        finish_kernel,
        out_shape=jax.ShapeDtypeStruct(offsets.shape, f32),
        in_specs=[SMEM, SMEM] + [VMEM] * 7,
        scratch_shapes=[
            pltpu.VMEM((width, up_width), bf16),
            pltpu.VMEM((width, up_width), bf16),
            pltpu.VMEM((pairs * ROWS, up_width), f32),
            pltpu.VMEM((pairs * ROWS, width), f32),
            pltpu.VMEM((3, total, LANE), f32),
            pltpu.VMEM((3, total, LANE), f32),
            pltpu.VMEM((3, rounded_up(NT, LANE), LANE), f32),
            pltpu.SMEM((pairs + 1,), jnp.int32),
        ],
        compiler_params=vmem_limit(28),
        cost_estimate=work(15),
        name="finish",
    )(mine, theirs, centers, offsets, translate, upsample, sent, recv, own_near)


def on_device(centers, offsets, forces, upsample, translate, owner_cell, peer_cell, live):
    cells, count = offsets.shape[1:]
    peers, slots = owner_cell.shape[1:]
    slabs = lax.axis_size("slab")
    exchange = functools.partial(
        lax.all_to_all, axis_name="cell", split_axis=0, concat_axis=0, tiled=True
    )
    mine = pair_table(peer_cell, live, owner_cell)
    theirs = exchange(mine)
    centers, mine = lax.optimization_barrier((centers, mine))
    scale = 1.0 / math.sqrt(cells * peers * count)
    own = moments(centers, offsets, forces, scale)
    swaps = [
        [(i, i + 1) for i in range(first, slabs - 1, 2)]
        + [(i + 1, i) for i in range(first, slabs - 1, 2)]
        for first in (0, 1)
    ]
    inner = lax.ppermute(own, "slab", swaps[0])
    outer = lax.ppermute(own, "slab", swaps[1])
    sent = pack(mine, theirs, slots, centers, offsets, forces, own, inner, outer)
    recv = exchange(sent)
    own_near = near_self(mine, sent, upsample)
    return finish(mine, theirs, centers, offsets, translate, upsample, sent, recv, own_near)


def solution(mesh):
    return jax.shard_map(
        on_device,
        mesh=mesh,
        in_specs=(
            P(None, ("slab", "cell")),
            P(None, ("slab", "cell"), None),
            P(None, ("slab", "cell"), None),
            P(),
            P(),
            P(("slab", "cell"), None, None),
            P(("slab", "cell"), None, None),
            P(("slab", "cell"), None, None),
        ),
        out_specs=P(None, ("slab", "cell"), None),
        check_vma=False,
    )
```

```python
import functools
import math

import jax
import jax.numpy as jnp
from jax import lax
from jax.experimental import pallas as pl
from jax.experimental.pallas import tpu as pltpu
from jax.sharding import PartitionSpec as P

DEGREE = 8
LANE = 128
ROWS = 8
soften = 0.0025
highest = lax.Precision.HIGHEST
f32 = jnp.float32
bf16 = jnp.bfloat16

TERMS = [
    (i, j, k)
    for i in range(DEGREE + 1)
    for j in range(DEGREE + 1 - i)
    for k in range(DEGREE + 1 - i - j)
]
TERM_AT = {term: at for at, term in enumerate(TERMS)}
NT = len(TERMS)
SECTION = 256
BY_VECTOR = (1, 3)

NN = (((1,), (0,)), ((), ()))
NT_DIMS = (((1,), (1,)), ((), ()))


def rounded_up(size, unit):
    return -(-size // unit) * unit


def vmem_limit(mib):
    return pltpu.CompilerParams(vmem_limit_bytes=mib * 1024 * 1024)


def work(micros):
    return pl.CostEstimate(flops=int(micros * 1.0e9), bytes_accessed=0, transcendentals=0)


SMEM = pl.BlockSpec(memory_space=pltpu.SMEM)
VMEM = pl.BlockSpec(memory_space=pltpu.VMEM)
HBM = pl.BlockSpec(memory_space=pltpu.HBM)


def fetch(pairs, sems):
    copies = [
        pltpu.make_async_copy(source, target, sems.at[at])
        for at, (source, target) in enumerate(pairs)
    ]
    for copy in copies:
        copy.start()
    return copies


def center_columns(center_row, cells):
    row = lax.broadcasted_iota(jnp.int32, (cells, cells), 0)
    col = lax.broadcasted_iota(jnp.int32, (cells, cells), 1)
    diagonal = jnp.where(row == col, jnp.broadcast_to(center_row, (cells, cells)), 0.0)
    return lax.dot_general(
        diagonal, jnp.ones((cells, LANE), f32), NN, precision=highest, preferred_element_type=f32
    )


def packed_tail(first, second, width):
    gap = jnp.zeros((first.shape[0], LANE // 2 - width), f32)
    return jnp.concatenate([first, gap, second, gap], axis=1)


def pack_points(store, array_ref, coord, shift, cells, count):
    full = count // LANE
    rest = count - full * LANE
    half = cells // 2
    for tile in range(full):
        part = array_ref[coord, :, tile * LANE : (tile + 1) * LANE]
        if shift is not None:
            part = part + shift
        store[coord, tile * cells : (tile + 1) * cells, :] = part
    first = array_ref[coord, :half, full * LANE : count]
    second = array_ref[coord, half:, full * LANE : count]
    if shift is not None:
        first = first + shift[:half, :rest]
        second = second + shift[half:, :rest]
    store[coord, full * cells : full * cells + half, :] = packed_tail(first, second, rest)


def moments_kernel(
    scale, centers_ref, offsets_hbm, forces_hbm, out_ref, offsets_ref, forces_ref, sems, pts, frc, acc
):
    copies = fetch([(offsets_hbm, offsets_ref), (forces_hbm, forces_ref)], sems)
    for copy in copies:
        copy.wait()
    cells, count = offsets_ref.shape[1:]
    for coord in range(3):
        shift = center_columns(centers_ref[coord : coord + 1, :], cells)
        pack_points(pts, offsets_ref, coord, shift, cells, count)
        pack_points(frc, forces_ref, coord, None, cells, count)
    total = pts.shape[1]
    chunk = total // 2

    def one_component(comp, carry):
        for part in range(2):
            rows = slice(part * chunk, (part + 1) * chunk)
            x, y, z = (pts[coord, rows, :] for coord in range(3))
            by_x = frc[comp, rows, :]
            for i in range(DEGREE + 1):
                if i:
                    by_x = by_x * x
                by_y = by_x
                for j in range(DEGREE + 1 - i):
                    if j:
                        by_y = by_y * y
                    by_z = by_y
                    for k in range(DEGREE + 1 - i - j):
                        if k:
                            by_z = by_z * z
                        at = TERM_AT[(i, j, k)] * ROWS
                        summed = jnp.sum(by_z.reshape(chunk // ROWS, ROWS, LANE), axis=0)
                        if part:
                            summed = summed + acc[comp, at : at + ROWS, :]
                        acc[comp, at : at + ROWS, :] = summed
        return carry

    lax.fori_loop(0, 3, one_component, 0)
    out_ref[...] = jnp.zeros_like(out_ref)
    ones = jnp.ones((ROWS, LANE), f32)
    for comp in range(3):
        folded = acc[comp, pl.ds(0, NT, stride=ROWS), :]
        for row in range(1, ROWS):
            folded = folded + acc[comp, pl.ds(row, NT, stride=ROWS), :]
        sums = lax.dot_general(
            ones, folded, NT_DIMS, precision=highest, preferred_element_type=f32
        )
        out_ref[2 * comp : 2 * comp + 1, :] = sums[0:1, 0:LANE] * scale
        out_ref[2 * comp + 1 : 2 * comp + 2, 0 : NT - LANE] = sums[0:1, LANE:NT] * scale


def moments(centers, offsets, forces, scale):
    cells, count = offsets.shape[1:]
    total = cells * (count // LANE) + cells // 2
    return pl.pallas_call(
        functools.partial(moments_kernel, scale),
        out_shape=jax.ShapeDtypeStruct((ROWS, LANE), f32),
        in_specs=[VMEM, HBM, HBM],
        scratch_shapes=[
            pltpu.VMEM(offsets.shape, f32),
            pltpu.VMEM(forces.shape, f32),
            pltpu.SemaphoreType.DMA((2,)),
            pltpu.VMEM((3, total, LANE), f32),
            pltpu.VMEM((3, total, LANE), f32),
            pltpu.VMEM((3, NT * ROWS, LANE), f32),
        ],
        compiler_params=vmem_limit(60),
        cost_estimate=work(3),
        name="moments",
    )(centers, offsets, forces)


PARTNER, LIVE, OWNER = 0, 1, 2


def table_kernel(partner_ref, live_ref, owner_ref, out_ref):
    peers = out_ref.shape[0]
    lane = lax.broadcasted_iota(jnp.int32, (1, LANE), 1)
    out_ref[...] = jnp.zeros_like(out_ref)
    for peer in range(peers):
        for row, ref in ((PARTNER, partner_ref), (LIVE, live_ref), (OWNER, owner_ref)):
            values = jnp.zeros((1, LANE), jnp.int32)
            for slot in range(ref.shape[1]):
                values = jnp.where(lane == slot, ref[0, slot, peer], values)
            out_ref[peer, row : row + 1, :] = values


def pair_table(peer_cell, live, owner_cell):
    turned = [jnp.swapaxes(each, 1, 2) for each in (peer_cell, live, owner_cell)]
    return pl.pallas_call(
        table_kernel,
        out_shape=jax.ShapeDtypeStruct((peer_cell.shape[1], 4, LANE), jnp.int32),
        in_specs=[SMEM, SMEM, SMEM],
        compiler_params=vmem_limit(60),
        name="pair_table",
    )(*turned)


def pack_kernel(
    mine_ref,
    theirs_ref,
    centers_ref,
    offsets_ref,
    forces_ref,
    own_ref,
    inner_ref,
    outer_ref,
    out_ref,
):
    peers, blocks, _, width = out_ref.shape
    slots = blocks // 2
    count = offsets_ref.shape[2]
    out_ref[...] = jnp.zeros_like(out_ref)
    for peer in range(peers):
        for tile, held_ref in enumerate((own_ref, inner_ref, outer_ref)):
            out_ref[peer, blocks - 1, :, tile * LANE : (tile + 1) * LANE] = held_ref[...]

    def one_cell(peer, block, cell):
        for coord in range(3):
            out_ref[peer, block, coord : coord + 1, 0:count] = offsets_ref[
                coord, pl.ds(cell, 1), :
            ]
            out_ref[peer, block, 3 + coord : 4 + coord, 0:count] = forces_ref[
                coord, pl.ds(cell, 1), :
            ]
            out_ref[peer, block, coord : coord + 1, count:width] = jnp.full(
                (1, width - count), centers_ref[coord, cell], f32
            )

    def one_peer(peer, carry):
        for slot in range(slots):
            one_cell(peer, slot, mine_ref[peer, OWNER, slot])
            one_cell(peer, slots + slot, theirs_ref[peer, PARTNER, slot])
        return carry

    lax.fori_loop(0, peers, one_peer, 0)


def pack(mine, theirs, slots, centers, offsets, forces, own, inner, outer):
    peers = mine.shape[0]
    width = rounded_up(offsets.shape[2], LANE)
    return pl.pallas_call(
        pack_kernel,
        out_shape=jax.ShapeDtypeStruct((peers, 2 * slots + 1, ROWS, width), f32),
        in_specs=[SMEM, SMEM, SMEM] + [VMEM] * 5,
        compiler_params=vmem_limit(28),
        cost_estimate=work(1),
        name="pack",
    )(mine, theirs, centers, offsets, forces, own, inner, outer)


def two_parts(value):
    high = value.astype(bf16)
    return high, (value - high.astype(f32)).astype(bf16)


def three_parts(value):
    high = value.astype(bf16).astype(f32)
    rest = value - high
    middle = rest.astype(bf16).astype(f32)
    return high, middle, rest - middle


def upsampled(rows, up_high, up_low):
    size = rows.shape[0]
    rows_high, rows_low = two_parts(rows)
    both = jnp.concatenate([rows_high, rows_low], axis=0)
    by_high = lax.dot_general(both, up_high[...], NN, preferred_element_type=f32)
    by_low = lax.dot_general(rows_high, up_low[...], NN, preferred_element_type=f32)
    return by_high[:size] + (by_high[size:] + by_low)


def near_one(raised, source, target, count, up_count):
    width = target.shape[1]
    up_width = raised.shape[1]
    held = rounded_up(count, 16)
    row = lax.broadcasted_iota(jnp.int32, (ROWS, 1), 0)
    is_place = row < 3

    def by_row(parts):
        result = jnp.zeros((ROWS, parts[0].shape[1]), f32)
        for at, part in enumerate(parts):
            result = jnp.where(row == at, part, result)
        return result

    apart = jnp.where(is_place, source[:, count : count + 1] - target[:, count : count + 1], 0.0)
    both = raised + apart
    z = jnp.where(is_place, both, 0.0)
    z_low = pltpu.roll(z, 3, 0)
    z_sq = jnp.sum(z * z, axis=0, keepdims=True)
    z_dot_g = jnp.sum(z_low * both, axis=0, keepdims=True)
    blocks = [both]
    blocks += [both[a : a + 1] * both for a in range(3)]
    blocks.append((z_sq + 2.0 * soften) * both + z_dot_g * z_low)
    split = [three_parts(block) for block in blocks]
    columns = jnp.concatenate([parts[p] for p in range(3) for parts in split], axis=0).astype(bf16)

    z_twice = -2.0 * z
    zh, zm, zl = three_parts(z_twice)
    one_z = jnp.ones((1, up_width), f32)
    z_norm = by_row([one_z, one_z, one_z, *three_parts(z_sq + soften)])
    z_side = jnp.concatenate(
        [zh, zh, zm, zm, zl, zh, z_norm, jnp.zeros_like(z_norm)], axis=0
    ).astype(bf16)

    y = jnp.where(is_place, target, 0.0)
    y_sq = jnp.sum(y * y, axis=0, keepdims=True)
    yh, ym, yl = three_parts(y)
    one_y = jnp.ones((1, width), f32)
    y_norm = by_row([*three_parts(y_sq), one_y, one_y, one_y])
    y_plain = jnp.where(row == 3, y_sq + soften, y)
    y_side = jnp.concatenate([yh, ym, yh, ym, yh, yl, y_norm, y_plain], axis=0)
    y_turned = jnp.transpose(y_side)[0:held]
    y_columns = [y_turned[:, 7 * ROWS + at : 7 * ROWS + at + 1] for at in range(4)]
    y_rows = y_turned.astype(bf16)

    weights = []
    for start in range(0, up_width, SECTION):
        span = slice(start, min(start + SECTION, up_width))
        if start // SECTION in BY_VECTOR:
            radius_sq = y_columns[3] + z_sq[:, span]
            for a in range(3):
                radius_sq = radius_sq + y_columns[a] * z_twice[a : a + 1, span]
        else:
            radius_sq = lax.dot_general(y_rows, z_side[:, span], NN, preferred_element_type=f32)
        inverse = lax.rsqrt(radius_sq)
        weights.append(jnp.concatenate(two_parts(inverse * inverse * inverse), axis=0))
    total = lax.dot_general(
        jnp.concatenate(weights, axis=1), columns, NT_DIMS, preferred_element_type=f32
    )
    summed = total[:held] + total[held:]
    lanes = summed.shape[1]
    summed = jnp.concatenate([summed, jnp.zeros((held, LANE - lanes), f32)], axis=1)
    summed = jnp.concatenate([summed, jnp.zeros((width - held, LANE), f32)], axis=0)
    across = jnp.transpose(summed)
    third = 5 * ROWS
    folded = across[0:third] + (across[third : 2 * third] + across[2 * third : 3 * third])
    plain, constant = folded[0:ROWS], folded[4 * ROWS : 5 * ROWS]
    crossed = [folded[(1 + a) * ROWS : (2 + a) * ROWS] for a in range(3)]
    y_low = pltpu.roll(y, 3, 0)
    along = jnp.sum(y_low * plain, axis=0, keepdims=True)
    for a in range(3):
        along = along - crossed[a][3 + a : 4 + a]
    value = y_sq * plain + y_low * along + constant
    for a in range(3):
        value = value - 2.0 * (y[a : a + 1] * crossed[a])
        turned = jnp.sum(y_low * crossed[a], axis=0, keepdims=True)
        value = value - jnp.where(row == 3 + a, turned, 0.0)
    return value * (1.0 / up_count)


def direction(mine_ref, theirs_ref, peer, block, slots):
    backward = block < slots
    slot = jnp.where(backward, block, block - slots)
    alive = jnp.where(backward, theirs_ref[peer, LIVE, slot], mine_ref[peer, LIVE, slot])
    cell = jnp.where(backward, theirs_ref[peer, PARTNER, slot], mine_ref[peer, OWNER, slot])
    return alive, cell


def opposite(block, slots):
    return jnp.where(block < slots, block + slots, block - slots)


def listed(total, alive, order):
    def body(at, held):
        order[held] = at
        return held + alive(at)

    held = lax.fori_loop(0, total, body, 0)

    @pl.when(held > 0)
    def _():
        order[held] = order[jnp.maximum(held - 1, 0)]

    return held


def split_upsample(upsample_ref, high_ref, low_ref):
    count, up_count = upsample_ref.shape
    below = count // 16 * 16
    beyond = up_count // LANE * LANE
    for ref in (high_ref, low_ref):
        ref[below:, :] = jnp.zeros((ref.shape[0] - below, ref.shape[1]), bf16)
        ref[:, beyond:] = jnp.zeros((ref.shape[0], ref.shape[1] - beyond), bf16)
    high, low = two_parts(upsample_ref[...])
    for ref, part in ((high_ref, high), (low_ref, low)):
        ref[0:count, 0:up_count] = part


def near_self_kernel(
    mine_ref,
    sent_ref,
    upsample_ref,
    centers_ref,
    offsets_ref,
    out_ref,
    pts,
    high_ref,
    low_ref,
    raised,
    order,
):
    blocks, width = out_ref.shape[0], out_ref.shape[2]
    slots = blocks // 2
    count, up_count = upsample_ref.shape
    me = lax.axis_index("cell")
    cells = offsets_ref.shape[1]
    for coord in range(3):
        shift = center_columns(centers_ref[coord : coord + 1, :], cells)
        pack_points(pts, offsets_ref, coord, shift, cells, count)
    split_upsample(upsample_ref, high_ref, low_ref)
    source = sent_ref[me, 0:blocks]
    raised[...] = upsampled(source.reshape(blocks * ROWS, width), high_ref, low_ref)

    def alive(block):
        return mine_ref[me, LIVE, jnp.where(block < slots, block, block - slots)]

    def compute(block):
        at = pl.multiple_of(block * ROWS, ROWS)
        target = sent_ref[me, opposite(block, slots)]
        return near_one(raised[pl.ds(at, ROWS), :], sent_ref[me, block], target, count, up_count)

    def two(step, carry):
        pair = [order[2 * step + at] for at in range(2)]
        results = [compute(block) for block in pair]
        for block, result in zip(pair, results):
            out_ref[block] = result
        return carry

    held = listed(blocks, alive, order)
    lax.fori_loop(0, (held + 1) // 2, two, 0)


def near_self(mine, sent, upsample, centers, offsets):
    _, blocks, _, width = sent.shape
    blocks = blocks - 1
    cells, count = offsets.shape[1:]
    total = cells * (count // LANE) + cells // 2
    up_width = rounded_up(upsample.shape[1], LANE)
    return pl.pallas_call(
        near_self_kernel,
        out_shape=(
            jax.ShapeDtypeStruct((blocks, ROWS, width), f32),
            jax.ShapeDtypeStruct((3, total, LANE), f32),
        ),
        in_specs=[SMEM] + [VMEM] * 4,
        scratch_shapes=[
            pltpu.VMEM((width, up_width), bf16),
            pltpu.VMEM((width, up_width), bf16),
            pltpu.VMEM((blocks * ROWS, up_width), f32),
            pltpu.SMEM((blocks + 1,), jnp.int32),
        ],
        compiler_params=vmem_limit(28),
        cost_estimate=work(4),
        name="near_self",
    )(mine, sent, upsample, centers, offsets)


def finish_kernel(
    mine_ref,
    theirs_ref,
    pts,
    translate_ref,
    upsample_ref,
    sent_ref,
    recv_ref,
    own_near_ref,
    out_ref,
    high_ref,
    low_ref,
    raised,
    near,
    far,
    coef_wide,
    order,
):
    up_count = upsample_ref.shape[1]
    split_upsample(upsample_ref, high_ref, low_ref)
    cells, count = out_ref.shape[1:]
    peers, blocks, _, width = recv_ref.shape
    blocks = blocks - 1
    slots = blocks // 2
    me = lax.axis_index("cell")

    def place(pair):
        peer = pair // blocks
        return peer, pair - peer * blocks

    def alive(pair):
        peer, block = place(pair)
        found, _ = direction(mine_ref, theirs_ref, peer, block, slots)
        return jnp.where(peer == me, 0, found)

    held = listed(peers * blocks, alive, order)
    for peer in range(peers):
        rows = recv_ref[peer, 0:blocks].reshape(blocks * ROWS, width)
        near[peer * blocks * ROWS : (peer + 1) * blocks * ROWS, :] = rows

    total = recv_ref[0, blocks]
    for peer in range(1, peers):
        total = total + recv_ref[peer, blocks]
    odd = lax.rem(lax.axis_index("slab"), 2)
    local = jnp.zeros((ROWS, NT), f32)
    for tile, which in enumerate((0, 2 - odd, 1 + odd)):
        summed = total[:, tile * LANE : (tile + 1) * LANE]
        rows = [
            jnp.concatenate([summed[2 * c : 2 * c + 1], summed[2 * c + 1 : 2 * c + 2]], axis=1)
            for c in range(3)
        ]
        rows.append(jnp.zeros((ROWS - 3, 2 * LANE), f32))
        local = local + lax.dot_general(
            jnp.concatenate(rows, axis=0)[:, 0:NT],
            translate_ref[which],
            NT_DIMS,
            precision=highest,
            preferred_element_type=f32,
        )
    nt_width = rounded_up(NT, LANE)
    padded = jnp.concatenate([local, jnp.zeros((ROWS, nt_width - NT), f32)], axis=1)
    tall = jnp.concatenate([padded, jnp.zeros((LANE - ROWS, nt_width), f32)], axis=0)
    upright = jnp.transpose(tall)
    for comp in range(3):
        coef_wide[comp] = jnp.broadcast_to(upright[:, comp : comp + 1], (nt_width, LANE))

    raised[...] = upsampled(near[...], high_ref, low_ref)

    def compute(pair):
        peer, block = place(pair)
        at = pl.multiple_of(pair * ROWS, ROWS)
        target = sent_ref[peer, opposite(block, slots)]
        return near_one(raised[pl.ds(at, ROWS), :], recv_ref[peer, block], target, count, up_count)

    def two(step):
        chosen = [order[2 * step + at] for at in range(2)]
        results = [compute(pair) for pair in chosen]
        for pair, result in zip(chosen, results):
            near[pl.ds(pl.multiple_of(pair * ROWS, ROWS), ROWS), :] = result

    slices = 6
    chunk = pts.shape[1] // 4

    def evaluate(step):
        comp = step // 2
        for part in range(2):
            start = pl.multiple_of((step - 2 * comp) * 2 * chunk + part * chunk, ROWS)
            x, y, z = (pts[coord, pl.ds(start, chunk), :] for coord in range(3))
            by_x = None
            for i in range(DEGREE, -1, -1):
                by_y = None
                for j in range(DEGREE - i, -1, -1):
                    by_z = None
                    for k in range(DEGREE - i - j, -1, -1):
                        at = TERM_AT[(i, j, k)]
                        value = coef_wide[comp, at : at + 1, :]
                        by_z = value if by_z is None else by_z * z + value
                    by_y = by_z if by_y is None else by_y * y + by_z
                by_x = by_y if by_x is None else by_x * x + by_y
            far[comp, pl.ds(start, chunk), :] = by_x

    steps = (held + 1) // 2
    shared = jnp.minimum(steps, slices)

    def both(step, carry):
        evaluate(step)
        two(step)
        return carry

    def near_only(step, carry):
        two(step)
        return carry

    def far_only(step, carry):
        evaluate(step)
        return carry

    lax.fori_loop(0, shared, both, 0)
    lax.fori_loop(shared, steps, near_only, 0)
    lax.fori_loop(shared, slices, far_only, 0)

    full = count // LANE
    rest = count - full * LANE
    half = cells // 2
    for comp in range(3):
        for tile in range(full):
            out_ref[comp, :, tile * LANE : (tile + 1) * LANE] = far[
                comp, tile * cells : (tile + 1) * cells, :
            ]
        tail = far[comp, full * cells : full * cells + half, :]
        out_ref[comp, 0:half, full * LANE : count] = tail[:, 0:rest]
        out_ref[comp, half:cells, full * LANE : count] = tail[:, LANE // 2 : LANE // 2 + rest]

    def add(cell, value):
        for comp in range(3):
            out_ref[comp, pl.ds(cell, 1), :] = (
                out_ref[comp, pl.ds(cell, 1), :] + value[3 + comp : 4 + comp, 0:count]
            )

    def add_pair(step, carry):
        pair = order[step]
        peer, block = place(pair)
        _, cell = direction(mine_ref, theirs_ref, peer, block, slots)
        add(cell, near[pl.ds(pl.multiple_of(pair * ROWS, ROWS), ROWS), :])
        return carry

    lax.fori_loop(0, held, add_pair, 0)

    def add_own(block, carry):
        found, cell = direction(mine_ref, theirs_ref, me, block, slots)

        @pl.when(found > 0)
        def _():
            add(cell, own_near_ref[block])

        return carry

    lax.fori_loop(0, blocks, add_own, 0)


def finish(mine, theirs, points, translate, upsample, sent, recv, own_near, out_shape):
    cells, count = out_shape[1:]
    peers, blocks, _, width = sent.shape
    blocks = blocks - 1
    total = cells * (count // LANE) + cells // 2
    pairs = peers * blocks
    up_width = rounded_up(upsample.shape[1], LANE)
    return pl.pallas_call(
        finish_kernel,
        out_shape=jax.ShapeDtypeStruct(out_shape, f32),
        in_specs=[SMEM, SMEM] + [VMEM] * 6,
        scratch_shapes=[
            pltpu.VMEM((width, up_width), bf16),
            pltpu.VMEM((width, up_width), bf16),
            pltpu.VMEM((pairs * ROWS, up_width), f32),
            pltpu.VMEM((pairs * ROWS, width), f32),
            pltpu.VMEM((3, total, LANE), f32),
            pltpu.VMEM((3, rounded_up(NT, LANE), LANE), f32),
            pltpu.SMEM((pairs + 1,), jnp.int32),
        ],
        compiler_params=vmem_limit(28),
        cost_estimate=work(15),
        name="finish",
    )(mine, theirs, points, translate, upsample, sent, recv, own_near)


def on_device(centers, offsets, forces, upsample, translate, owner_cell, peer_cell, live):
    cells, count = offsets.shape[1:]
    peers, slots = owner_cell.shape[1:]
    slabs = lax.axis_size("slab")
    exchange = functools.partial(
        lax.all_to_all, axis_name="cell", split_axis=0, concat_axis=0, tiled=True
    )
    mine = pair_table(peer_cell, live, owner_cell)
    theirs = exchange(mine)
    centers, mine = lax.optimization_barrier((centers, mine))
    scale = 1.0 / math.sqrt(cells * peers * count)
    own = moments(centers, offsets, forces, scale)
    swaps = [
        [(i, i + 1) for i in range(first, slabs - 1, 2)]
        + [(i + 1, i) for i in range(first, slabs - 1, 2)]
        for first in (0, 1)
    ]
    inner = lax.ppermute(own, "slab", swaps[0])
    outer = lax.ppermute(own, "slab", swaps[1])
    sent = pack(mine, theirs, slots, centers, offsets, forces, own, inner, outer)
    recv = exchange(sent)
    own_near, points = near_self(mine, sent, upsample, centers, offsets)
    return finish(mine, theirs, points, translate, upsample, sent, recv, own_near, offsets.shape)


def solution(mesh):
    return jax.shard_map(
        on_device,
        mesh=mesh,
        in_specs=(
            P(None, ("slab", "cell")),
            P(None, ("slab", "cell"), None),
            P(None, ("slab", "cell"), None),
            P(),
            P(),
            P(("slab", "cell"), None, None),
            P(("slab", "cell"), None, None),
            P(("slab", "cell"), None, None),
        ),
        out_specs=P(None, ("slab", "cell"), None),
        check_vma=False,
    )
```

```python
import functools
import math

import jax
import jax.numpy as jnp
from jax import lax
from jax.experimental import pallas as pl
from jax.experimental.pallas import tpu as pltpu
from jax.sharding import PartitionSpec as P

DEGREE = 8
LANE = 128
ROWS = 8
soften = 0.0025
highest = lax.Precision.HIGHEST
f32 = jnp.float32
bf16 = jnp.bfloat16

TERMS = [
    (i, j, k)
    for i in range(DEGREE + 1)
    for j in range(DEGREE + 1 - i)
    for k in range(DEGREE + 1 - i - j)
]
TERM_AT = {term: at for at, term in enumerate(TERMS)}
NT = len(TERMS)
SECTION = 256

NN = (((1,), (0,)), ((), ()))
NT_DIMS = (((1,), (1,)), ((), ()))


def rounded_up(size, unit):
    return -(-size // unit) * unit


def vmem_limit(mib):
    return pltpu.CompilerParams(vmem_limit_bytes=mib * 1024 * 1024)


def work(micros):
    return pl.CostEstimate(flops=int(micros * 1.0e9), bytes_accessed=0, transcendentals=0)


SMEM = pl.BlockSpec(memory_space=pltpu.SMEM)
VMEM = pl.BlockSpec(memory_space=pltpu.VMEM)


def center_columns(center_row, cells):
    row = lax.broadcasted_iota(jnp.int32, (cells, cells), 0)
    col = lax.broadcasted_iota(jnp.int32, (cells, cells), 1)
    diagonal = jnp.where(row == col, jnp.broadcast_to(center_row, (cells, cells)), 0.0)
    return lax.dot_general(
        diagonal, jnp.ones((cells, LANE), f32), NN, precision=highest, preferred_element_type=f32
    )


def packed_tail(first, second, width):
    gap = jnp.zeros((first.shape[0], LANE // 2 - width), f32)
    return jnp.concatenate([first, gap, second, gap], axis=1)


def pack_points(store, array_ref, coord, shift, cells, count):
    full = count // LANE
    rest = count - full * LANE
    half = cells // 2
    for tile in range(full):
        part = array_ref[coord, :, tile * LANE : (tile + 1) * LANE]
        if shift is not None:
            part = part + shift
        store[coord, tile * cells : (tile + 1) * cells, :] = part
    first = array_ref[coord, :half, full * LANE : count]
    second = array_ref[coord, half:, full * LANE : count]
    if shift is not None:
        first = first + shift[:half, :rest]
        second = second + shift[half:, :rest]
    store[coord, full * cells : full * cells + half, :] = packed_tail(first, second, rest)


def moments_kernel(scale, centers_ref, offsets_ref, forces_ref, out_ref, pts, frc, acc):
    cells, count = offsets_ref.shape[1:]
    for coord in range(3):
        shift = center_columns(centers_ref[coord : coord + 1, :], cells)
        pack_points(pts, offsets_ref, coord, shift, cells, count)
        pack_points(frc, forces_ref, coord, None, cells, count)
    total = pts.shape[1]
    chunk = total // 2

    def one_component(comp, carry):
        for part in range(2):
            rows = slice(part * chunk, (part + 1) * chunk)
            x, y, z = (pts[coord, rows, :] for coord in range(3))
            by_x = frc[comp, rows, :]
            for i in range(DEGREE + 1):
                if i:
                    by_x = by_x * x
                by_y = by_x
                for j in range(DEGREE + 1 - i):
                    if j:
                        by_y = by_y * y
                    by_z = by_y
                    for k in range(DEGREE + 1 - i - j):
                        if k:
                            by_z = by_z * z
                        at = TERM_AT[(i, j, k)] * ROWS
                        summed = jnp.sum(by_z.reshape(chunk // ROWS, ROWS, LANE), axis=0)
                        if part:
                            summed = summed + acc[comp, at : at + ROWS, :]
                        acc[comp, at : at + ROWS, :] = summed
        return carry

    lax.fori_loop(0, 3, one_component, 0)
    out_ref[...] = jnp.zeros_like(out_ref)
    ones = jnp.ones((ROWS, LANE), f32)
    for comp in range(3):
        folded = acc[comp, pl.ds(0, NT, stride=ROWS), :]
        for row in range(1, ROWS):
            folded = folded + acc[comp, pl.ds(row, NT, stride=ROWS), :]
        sums = lax.dot_general(
            ones, folded, NT_DIMS, precision=highest, preferred_element_type=f32
        )
        out_ref[2 * comp : 2 * comp + 1, :] = sums[0:1, 0:LANE] * scale
        out_ref[2 * comp + 1 : 2 * comp + 2, 0 : NT - LANE] = sums[0:1, LANE:NT] * scale


def moments(centers, offsets, forces, scale):
    cells, count = offsets.shape[1:]
    total = cells * (count // LANE) + cells // 2
    return pl.pallas_call(
        functools.partial(moments_kernel, scale),
        out_shape=jax.ShapeDtypeStruct((ROWS, LANE), f32),
        scratch_shapes=[
            pltpu.VMEM((3, total, LANE), f32),
            pltpu.VMEM((3, total, LANE), f32),
            pltpu.VMEM((3, NT * ROWS, LANE), f32),
        ],
        compiler_params=vmem_limit(28),
        cost_estimate=work(3),
        name="moments",
    )(centers, offsets, forces)


PARTNER, LIVE, OWNER = 0, 1, 2


def table_kernel(partner_ref, live_ref, owner_ref, out_ref):
    peers = out_ref.shape[0]
    lane = lax.broadcasted_iota(jnp.int32, (1, LANE), 1)
    out_ref[...] = jnp.zeros_like(out_ref)
    for peer in range(peers):
        for row, ref in ((PARTNER, partner_ref), (LIVE, live_ref), (OWNER, owner_ref)):
            values = jnp.zeros((1, LANE), jnp.int32)
            for slot in range(ref.shape[1]):
                values = jnp.where(lane == slot, ref[0, slot, peer], values)
            out_ref[peer, row : row + 1, :] = values


def pair_table(peer_cell, live, owner_cell):
    turned = [jnp.swapaxes(each, 1, 2) for each in (peer_cell, live, owner_cell)]
    return pl.pallas_call(
        table_kernel,
        out_shape=jax.ShapeDtypeStruct((peer_cell.shape[1], 4, LANE), jnp.int32),
        in_specs=[SMEM, SMEM, SMEM],
        compiler_params=vmem_limit(60),
        name="pair_table",
    )(*turned)


def pack_kernel(
    mine_ref,
    theirs_ref,
    centers_ref,
    offsets_ref,
    forces_ref,
    own_ref,
    inner_ref,
    outer_ref,
    out_ref,
):
    peers, blocks, _, width = out_ref.shape
    slots = blocks // 2
    count = offsets_ref.shape[2]
    out_ref[...] = jnp.zeros_like(out_ref)
    for peer in range(peers):
        for tile, held_ref in enumerate((own_ref, inner_ref, outer_ref)):
            out_ref[peer, blocks - 1, :, tile * LANE : (tile + 1) * LANE] = held_ref[...]

    def one_cell(peer, block, cell):
        for coord in range(3):
            out_ref[peer, block, coord : coord + 1, 0:count] = offsets_ref[
                coord, pl.ds(cell, 1), :
            ]
            out_ref[peer, block, 3 + coord : 4 + coord, 0:count] = forces_ref[
                coord, pl.ds(cell, 1), :
            ]
            out_ref[peer, block, coord : coord + 1, count:width] = jnp.full(
                (1, width - count), centers_ref[coord, cell], f32
            )

    def one_peer(peer, carry):
        for slot in range(slots):
            one_cell(peer, slot, mine_ref[peer, OWNER, slot])
            one_cell(peer, slots + slot, theirs_ref[peer, PARTNER, slot])
        return carry

    lax.fori_loop(0, peers, one_peer, 0)


def pack(mine, theirs, slots, centers, offsets, forces, own, inner, outer):
    peers = mine.shape[0]
    width = rounded_up(offsets.shape[2], LANE)
    return pl.pallas_call(
        pack_kernel,
        out_shape=jax.ShapeDtypeStruct((peers, 2 * slots + 1, ROWS, width), f32),
        in_specs=[SMEM, SMEM, SMEM] + [VMEM] * 5,
        compiler_params=vmem_limit(28),
        cost_estimate=work(1),
        name="pack",
    )(mine, theirs, centers, offsets, forces, own, inner, outer)


def two_parts(value):
    high = value.astype(bf16)
    return high, (value - high.astype(f32)).astype(bf16)


def three_parts(value):
    high = value.astype(bf16).astype(f32)
    rest = value - high
    middle = rest.astype(bf16).astype(f32)
    return high, middle, rest - middle


def upsampled(rows, up_high, up_low):
    size = rows.shape[0]
    rows_high, rows_low = two_parts(rows)
    both = jnp.concatenate([rows_high, rows_low], axis=0)
    by_high = lax.dot_general(both, up_high[...], NN, preferred_element_type=f32)
    by_low = lax.dot_general(rows_high, up_low[...], NN, preferred_element_type=f32)
    return by_high[:size] + (by_high[size:] + by_low)


def near_one(raised, source, target, count, up_count):
    width = target.shape[1]
    up_width = raised.shape[1]
    held = rounded_up(count, 16)
    row = lax.broadcasted_iota(jnp.int32, (ROWS, 1), 0)
    is_place = row < 3

    def by_row(parts):
        result = jnp.zeros((ROWS, parts[0].shape[1]), f32)
        for at, part in enumerate(parts):
            result = jnp.where(row == at, part, result)
        return result

    apart = jnp.where(is_place, source[:, count : count + 1] - target[:, count : count + 1], 0.0)
    both = raised + apart
    z = jnp.where(is_place, both, 0.0)
    z_low = pltpu.roll(z, 3, 0)
    z_sq = jnp.sum(z * z, axis=0, keepdims=True)
    z_dot_g = jnp.sum(z_low * both, axis=0, keepdims=True)
    blocks = [both]
    blocks += [both[a : a + 1] * both for a in range(3)]
    blocks.append((z_sq + 2.0 * soften) * both + z_dot_g * z_low)
    split = [three_parts(block) for block in blocks]
    columns = jnp.concatenate([parts[p] for p in range(3) for parts in split], axis=0).astype(bf16)

    zh, zm, zl = three_parts(-2.0 * z)
    one_z = jnp.ones((1, up_width), f32)
    z_norm = by_row([one_z, one_z, one_z, *three_parts(z_sq + soften)])
    z_side = jnp.concatenate(
        [zh, zh, zm, zm, zl, zh, z_norm, jnp.zeros_like(z_norm)], axis=0
    ).astype(bf16)

    y = jnp.where(is_place, target, 0.0)
    y_sq = jnp.sum(y * y, axis=0, keepdims=True)
    yh, ym, yl = three_parts(y)
    one_y = jnp.ones((1, width), f32)
    y_norm = by_row([*three_parts(y_sq), one_y, one_y, one_y])
    y_side = jnp.concatenate([yh, ym, yh, ym, yh, yl, y_norm, jnp.zeros_like(y_norm)], axis=0)
    y_rows = jnp.transpose(y_side)[0:held].astype(bf16)

    weights = []
    for start in range(0, up_width, SECTION):
        span = slice(start, min(start + SECTION, up_width))
        radius_sq = lax.dot_general(y_rows, z_side[:, span], NN, preferred_element_type=f32)
        inverse = lax.rsqrt(radius_sq)
        weights.append(jnp.concatenate(two_parts(inverse * inverse * inverse), axis=0))
    total = lax.dot_general(
        jnp.concatenate(weights, axis=1), columns, NT_DIMS, preferred_element_type=f32
    )
    summed = total[:held] + total[held:]
    lanes = summed.shape[1]
    summed = jnp.concatenate([summed, jnp.zeros((held, LANE - lanes), f32)], axis=1)
    summed = jnp.concatenate([summed, jnp.zeros((width - held, LANE), f32)], axis=0)
    across = jnp.transpose(summed)
    third = 5 * ROWS
    folded = across[0:third] + (across[third : 2 * third] + across[2 * third : 3 * third])
    plain, constant = folded[0:ROWS], folded[4 * ROWS : 5 * ROWS]
    crossed = [folded[(1 + a) * ROWS : (2 + a) * ROWS] for a in range(3)]
    y_low = pltpu.roll(y, 3, 0)
    along = jnp.sum(y_low * plain, axis=0, keepdims=True)
    for a in range(3):
        along = along - crossed[a][3 + a : 4 + a]
    value = y_sq * plain + y_low * along + constant
    for a in range(3):
        value = value - 2.0 * (y[a : a + 1] * crossed[a])
        turned = jnp.sum(y_low * crossed[a], axis=0, keepdims=True)
        value = value - jnp.where(row == 3 + a, turned, 0.0)
    return value * (1.0 / up_count)


def direction(mine_ref, theirs_ref, peer, block, slots):
    backward = block < slots
    slot = jnp.where(backward, block, block - slots)
    alive = jnp.where(backward, theirs_ref[peer, LIVE, slot], mine_ref[peer, LIVE, slot])
    cell = jnp.where(backward, theirs_ref[peer, PARTNER, slot], mine_ref[peer, OWNER, slot])
    return alive, cell


def opposite(block, slots):
    return jnp.where(block < slots, block + slots, block - slots)


def listed(total, alive, order):
    def body(at, held):
        order[held] = at
        return held + alive(at)

    held = lax.fori_loop(0, total, body, 0)

    @pl.when(held > 0)
    def _():
        order[held] = order[jnp.maximum(held - 1, 0)]

    return held


def split_upsample(upsample_ref, high_ref, low_ref):
    count, up_count = upsample_ref.shape
    below = count // 16 * 16
    beyond = up_count // LANE * LANE
    for ref in (high_ref, low_ref):
        ref[below:, :] = jnp.zeros((ref.shape[0] - below, ref.shape[1]), bf16)
        ref[:, beyond:] = jnp.zeros((ref.shape[0], ref.shape[1] - beyond), bf16)
    high, low = two_parts(upsample_ref[...])
    for ref, part in ((high_ref, high), (low_ref, low)):
        ref[0:count, 0:up_count] = part


def near_self_kernel(
    mine_ref,
    sent_ref,
    upsample_ref,
    centers_ref,
    offsets_ref,
    out_ref,
    pts,
    high_ref,
    low_ref,
    raised,
    order,
):
    blocks, width = out_ref.shape[0], out_ref.shape[2]
    slots = blocks // 2
    count, up_count = upsample_ref.shape
    me = lax.axis_index("cell")
    cells = offsets_ref.shape[1]
    for coord in range(3):
        shift = center_columns(centers_ref[coord : coord + 1, :], cells)
        pack_points(pts, offsets_ref, coord, shift, cells, count)
    split_upsample(upsample_ref, high_ref, low_ref)
    source = sent_ref[me, 0:blocks]
    raised[...] = upsampled(source.reshape(blocks * ROWS, width), high_ref, low_ref)

    def alive(block):
        return mine_ref[me, LIVE, jnp.where(block < slots, block, block - slots)]

    def compute(block):
        at = pl.multiple_of(block * ROWS, ROWS)
        target = sent_ref[me, opposite(block, slots)]
        return near_one(raised[pl.ds(at, ROWS), :], sent_ref[me, block], target, count, up_count)

    def two(step, carry):
        pair = [order[2 * step + at] for at in range(2)]
        results = [compute(block) for block in pair]
        for block, result in zip(pair, results):
            out_ref[block] = result
        return carry

    held = listed(blocks, alive, order)
    lax.fori_loop(0, (held + 1) // 2, two, 0)


def near_self(mine, sent, upsample, centers, offsets):
    _, blocks, _, width = sent.shape
    blocks = blocks - 1
    cells, count = offsets.shape[1:]
    total = cells * (count // LANE) + cells // 2
    up_width = rounded_up(upsample.shape[1], LANE)
    return pl.pallas_call(
        near_self_kernel,
        out_shape=(
            jax.ShapeDtypeStruct((blocks, ROWS, width), f32),
            jax.ShapeDtypeStruct((3, total, LANE), f32),
        ),
        in_specs=[SMEM] + [VMEM] * 4,
        scratch_shapes=[
            pltpu.VMEM((width, up_width), bf16),
            pltpu.VMEM((width, up_width), bf16),
            pltpu.VMEM((blocks * ROWS, up_width), f32),
            pltpu.SMEM((blocks + 1,), jnp.int32),
        ],
        compiler_params=vmem_limit(28),
        cost_estimate=work(4),
        name="near_self",
    )(mine, sent, upsample, centers, offsets)


def finish_kernel(
    mine_ref,
    theirs_ref,
    pts,
    translate_ref,
    upsample_ref,
    sent_ref,
    recv_ref,
    own_near_ref,
    out_ref,
    high_ref,
    low_ref,
    raised,
    near,
    far,
    coef_wide,
    order,
):
    up_count = upsample_ref.shape[1]
    split_upsample(upsample_ref, high_ref, low_ref)
    cells, count = out_ref.shape[1:]
    peers, blocks, _, width = recv_ref.shape
    blocks = blocks - 1
    slots = blocks // 2
    me = lax.axis_index("cell")

    def place(pair):
        peer = pair // blocks
        return peer, pair - peer * blocks

    def alive(pair):
        peer, block = place(pair)
        found, _ = direction(mine_ref, theirs_ref, peer, block, slots)
        return jnp.where(peer == me, 0, found)

    held = listed(peers * blocks, alive, order)
    for peer in range(peers):
        rows = recv_ref[peer, 0:blocks].reshape(blocks * ROWS, width)
        near[peer * blocks * ROWS : (peer + 1) * blocks * ROWS, :] = rows

    total = recv_ref[0, blocks]
    for peer in range(1, peers):
        total = total + recv_ref[peer, blocks]
    odd = lax.rem(lax.axis_index("slab"), 2)
    local = jnp.zeros((ROWS, NT), f32)
    for tile, which in enumerate((0, 2 - odd, 1 + odd)):
        summed = total[:, tile * LANE : (tile + 1) * LANE]
        rows = [
            jnp.concatenate([summed[2 * c : 2 * c + 1], summed[2 * c + 1 : 2 * c + 2]], axis=1)
            for c in range(3)
        ]
        rows.append(jnp.zeros((ROWS - 3, 2 * LANE), f32))
        local = local + lax.dot_general(
            jnp.concatenate(rows, axis=0)[:, 0:NT],
            translate_ref[which],
            NT_DIMS,
            precision=highest,
            preferred_element_type=f32,
        )
    nt_width = rounded_up(NT, LANE)
    padded = jnp.concatenate([local, jnp.zeros((ROWS, nt_width - NT), f32)], axis=1)
    tall = jnp.concatenate([padded, jnp.zeros((LANE - ROWS, nt_width), f32)], axis=0)
    upright = jnp.transpose(tall)
    for comp in range(3):
        coef_wide[comp] = jnp.broadcast_to(upright[:, comp : comp + 1], (nt_width, LANE))

    raised[...] = upsampled(near[...], high_ref, low_ref)

    def compute(pair):
        peer, block = place(pair)
        at = pl.multiple_of(pair * ROWS, ROWS)
        target = sent_ref[peer, opposite(block, slots)]
        return near_one(raised[pl.ds(at, ROWS), :], recv_ref[peer, block], target, count, up_count)

    def two(step):
        chosen = [order[2 * step + at] for at in range(2)]
        results = [compute(pair) for pair in chosen]
        for pair, result in zip(chosen, results):
            near[pl.ds(pl.multiple_of(pair * ROWS, ROWS), ROWS), :] = result

    slices = 6
    chunk = pts.shape[1] // 4

    def evaluate(step):
        comp = step // 2
        for part in range(2):
            start = pl.multiple_of((step - 2 * comp) * 2 * chunk + part * chunk, ROWS)
            x, y, z = (pts[coord, pl.ds(start, chunk), :] for coord in range(3))
            by_x = None
            for i in range(DEGREE, -1, -1):
                by_y = None
                for j in range(DEGREE - i, -1, -1):
                    by_z = None
                    for k in range(DEGREE - i - j, -1, -1):
                        at = TERM_AT[(i, j, k)]
                        value = coef_wide[comp, at : at + 1, :]
                        by_z = value if by_z is None else by_z * z + value
                    by_y = by_z if by_y is None else by_y * y + by_z
                by_x = by_y if by_x is None else by_x * x + by_y
            far[comp, pl.ds(start, chunk), :] = by_x

    steps = (held + 1) // 2
    shared = jnp.minimum(steps, slices)

    def both(step, carry):
        evaluate(step)
        two(step)
        return carry

    def near_only(step, carry):
        two(step)
        return carry

    def far_only(step, carry):
        evaluate(step)
        return carry

    lax.fori_loop(0, shared, both, 0)
    lax.fori_loop(shared, steps, near_only, 0)
    lax.fori_loop(shared, slices, far_only, 0)

    full = count // LANE
    rest = count - full * LANE
    half = cells // 2
    for comp in range(3):
        for tile in range(full):
            out_ref[comp, :, tile * LANE : (tile + 1) * LANE] = far[
                comp, tile * cells : (tile + 1) * cells, :
            ]
        tail = far[comp, full * cells : full * cells + half, :]
        out_ref[comp, 0:half, full * LANE : count] = tail[:, 0:rest]
        out_ref[comp, half:cells, full * LANE : count] = tail[:, LANE // 2 : LANE // 2 + rest]

    def add(cell, value):
        for comp in range(3):
            out_ref[comp, pl.ds(cell, 1), :] = (
                out_ref[comp, pl.ds(cell, 1), :] + value[3 + comp : 4 + comp, 0:count]
            )

    def add_pair(step, carry):
        pair = order[step]
        peer, block = place(pair)
        _, cell = direction(mine_ref, theirs_ref, peer, block, slots)
        add(cell, near[pl.ds(pl.multiple_of(pair * ROWS, ROWS), ROWS), :])
        return carry

    lax.fori_loop(0, held, add_pair, 0)

    def add_own(block, carry):
        found, cell = direction(mine_ref, theirs_ref, me, block, slots)

        @pl.when(found > 0)
        def _():
            add(cell, own_near_ref[block])

        return carry

    lax.fori_loop(0, blocks, add_own, 0)


def finish(mine, theirs, points, translate, upsample, sent, recv, own_near, out_shape):
    cells, count = out_shape[1:]
    peers, blocks, _, width = sent.shape
    blocks = blocks - 1
    total = cells * (count // LANE) + cells // 2
    pairs = peers * blocks
    up_width = rounded_up(upsample.shape[1], LANE)
    return pl.pallas_call(
        finish_kernel,
        out_shape=jax.ShapeDtypeStruct(out_shape, f32),
        in_specs=[SMEM, SMEM] + [VMEM] * 6,
        scratch_shapes=[
            pltpu.VMEM((width, up_width), bf16),
            pltpu.VMEM((width, up_width), bf16),
            pltpu.VMEM((pairs * ROWS, up_width), f32),
            pltpu.VMEM((pairs * ROWS, width), f32),
            pltpu.VMEM((3, total, LANE), f32),
            pltpu.VMEM((3, rounded_up(NT, LANE), LANE), f32),
            pltpu.SMEM((pairs + 1,), jnp.int32),
        ],
        compiler_params=vmem_limit(28),
        cost_estimate=work(15),
        name="finish",
    )(mine, theirs, points, translate, upsample, sent, recv, own_near)


def on_device(centers, offsets, forces, upsample, translate, owner_cell, peer_cell, live):
    cells, count = offsets.shape[1:]
    peers, slots = owner_cell.shape[1:]
    slabs = lax.axis_size("slab")
    exchange = functools.partial(
        lax.all_to_all, axis_name="cell", split_axis=0, concat_axis=0, tiled=True
    )
    mine = pair_table(peer_cell, live, owner_cell)
    theirs = exchange(mine)
    centers, mine = lax.optimization_barrier((centers, mine))
    scale = 1.0 / math.sqrt(cells * peers * count)
    own = moments(centers, offsets, forces, scale)
    swaps = [
        [(i, i + 1) for i in range(first, slabs - 1, 2)]
        + [(i + 1, i) for i in range(first, slabs - 1, 2)]
        for first in (0, 1)
    ]
    inner = lax.ppermute(own, "slab", swaps[0])
    outer = lax.ppermute(own, "slab", swaps[1])
    sent = pack(mine, theirs, slots, centers, offsets, forces, own, inner, outer)
    recv = exchange(sent)
    own_near, points = near_self(mine, sent, upsample, centers, offsets)
    return finish(mine, theirs, points, translate, upsample, sent, recv, own_near, offsets.shape)


def solution(mesh):
    return jax.shard_map(
        on_device,
        mesh=mesh,
        in_specs=(
            P(None, ("slab", "cell")),
            P(None, ("slab", "cell"), None),
            P(None, ("slab", "cell"), None),
            P(),
            P(),
            P(("slab", "cell"), None, None),
            P(("slab", "cell"), None, None),
            P(("slab", "cell"), None, None),
        ),
        out_specs=P(None, ("slab", "cell"), None),
        check_vma=False,
    )
```

```python
import functools
import math

import jax
import jax.numpy as jnp
from jax import lax
from jax.experimental import pallas as pl
from jax.experimental.pallas import tpu as pltpu
from jax.sharding import PartitionSpec as P

DEGREE = 8
LANE = 128
ROWS = 8
soften = 0.0025
highest = lax.Precision.HIGHEST
f32 = jnp.float32
bf16 = jnp.bfloat16

TERMS = [
    (i, j, k)
    for i in range(DEGREE + 1)
    for j in range(DEGREE + 1 - i)
    for k in range(DEGREE + 1 - i - j)
]
TERM_AT = {term: at for at, term in enumerate(TERMS)}
NT = len(TERMS)
SECTION = 256

NN = (((1,), (0,)), ((), ()))
NT_DIMS = (((1,), (1,)), ((), ()))


def rounded_up(size, unit):
    return -(-size // unit) * unit


def vmem_limit(mib):
    return pltpu.CompilerParams(vmem_limit_bytes=mib * 1024 * 1024)


def work(micros):
    return pl.CostEstimate(flops=int(micros * 1.0e9), bytes_accessed=0, transcendentals=0)


SMEM = pl.BlockSpec(memory_space=pltpu.SMEM)
VMEM = pl.BlockSpec(memory_space=pltpu.VMEM)


def packed_tail(first, second, width):
    gap = jnp.zeros((first.shape[0], LANE // 2 - width), f32)
    return jnp.concatenate([first, gap, second, gap], axis=1)


def pack_points(store, cells_ref, coord, source, count):
    cells = cells_ref.shape[1]
    shift = cells_ref[source, :, count : count + 1]
    full = count // LANE
    rest = count - full * LANE
    half = cells // 2
    for tile in range(full):
        part = cells_ref[source, :, tile * LANE : (tile + 1) * LANE]
        part = part + shift
        store[coord, tile * cells : (tile + 1) * cells, :] = part
    first = cells_ref[source, :half, full * LANE : count] + shift[:half]
    second = cells_ref[source, half:, full * LANE : count] + shift[half:]
    store[coord, full * cells : full * cells + half, :] = packed_tail(first, second, rest)


def moments_kernel(scale, count, cells_ref, out_ref, pts, frc, acc):
    for coord in range(3):
        pack_points(pts, cells_ref, coord, coord, count)
        pack_points(frc, cells_ref, coord, 3 + coord, count)
    total = pts.shape[1]
    chunk = total // 2

    def one_component(comp, carry):
        for part in range(2):
            rows = slice(part * chunk, (part + 1) * chunk)
            x, y, z = (pts[coord, rows, :] for coord in range(3))
            by_x = frc[comp, rows, :]
            for i in range(DEGREE + 1):
                if i:
                    by_x = by_x * x
                by_y = by_x
                for j in range(DEGREE + 1 - i):
                    if j:
                        by_y = by_y * y
                    by_z = by_y
                    for k in range(DEGREE + 1 - i - j):
                        if k:
                            by_z = by_z * z
                        at = TERM_AT[(i, j, k)] * ROWS
                        summed = jnp.sum(by_z.reshape(chunk // ROWS, ROWS, LANE), axis=0)
                        if part:
                            summed = summed + acc[comp, at : at + ROWS, :]
                        acc[comp, at : at + ROWS, :] = summed
        return carry

    lax.fori_loop(0, 3, one_component, 0)
    out_ref[...] = jnp.zeros_like(out_ref)
    ones = jnp.ones((ROWS, LANE), f32)
    for comp in range(3):
        folded = acc[comp, pl.ds(0, NT, stride=ROWS), :]
        for row in range(1, ROWS):
            folded = folded + acc[comp, pl.ds(row, NT, stride=ROWS), :]
        sums = lax.dot_general(
            ones, folded, NT_DIMS, precision=highest, preferred_element_type=f32
        )
        out_ref[2 * comp : 2 * comp + 1, :] = sums[0:1, 0:LANE] * scale
        out_ref[2 * comp + 1 : 2 * comp + 2, 0 : NT - LANE] = sums[0:1, LANE:NT] * scale


def moments(held, count, scale):
    cells = held.shape[1]
    total = cells * (count // LANE) + cells // 2
    return pl.pallas_call(
        functools.partial(moments_kernel, scale, count),
        out_shape=jax.ShapeDtypeStruct((ROWS, LANE), f32),
        scratch_shapes=[
            pltpu.VMEM((3, total, LANE), f32),
            pltpu.VMEM((3, total, LANE), f32),
            pltpu.VMEM((3, NT * ROWS, LANE), f32),
        ],
        compiler_params=vmem_limit(28),
        cost_estimate=work(3),
        name="moments",
    )(held)


PARTNER, LIVE, OWNER = 0, 1, 2


def table_kernel(partner_ref, live_ref, owner_ref, out_ref):
    peers = out_ref.shape[0]
    lane = lax.broadcasted_iota(jnp.int32, (1, LANE), 1)
    out_ref[...] = jnp.zeros_like(out_ref)
    for peer in range(peers):
        for row, ref in ((PARTNER, partner_ref), (LIVE, live_ref), (OWNER, owner_ref)):
            values = jnp.zeros((1, LANE), jnp.int32)
            for slot in range(ref.shape[1]):
                values = jnp.where(lane == slot, ref[0, slot, peer], values)
            out_ref[peer, row : row + 1, :] = values


def pair_table(peer_cell, live, owner_cell):
    turned = [jnp.swapaxes(each, 1, 2) for each in (peer_cell, live, owner_cell)]
    return pl.pallas_call(
        table_kernel,
        out_shape=jax.ShapeDtypeStruct((peer_cell.shape[1], 4, LANE), jnp.int32),
        in_specs=[SMEM, SMEM, SMEM],
        compiler_params=vmem_limit(60),
        name="pair_table",
    )(*turned)


def pack_kernel(
    mine_ref,
    theirs_ref,
    cells_ref,
    own_ref,
    inner_ref,
    outer_ref,
    out_ref,
):
    peers, blocks, _, width = out_ref.shape
    slots = blocks // 2
    out_ref[...] = jnp.zeros_like(out_ref)
    for peer in range(peers):
        for tile, held_ref in enumerate((own_ref, inner_ref, outer_ref)):
            out_ref[peer, blocks - 1, :, tile * LANE : (tile + 1) * LANE] = held_ref[...]

    def one_cell(peer, block, cell):
        for row in range(6):
            out_ref[peer, block, row : row + 1, :] = cells_ref[row, pl.ds(cell, 1), :]

    def one_peer(peer, carry):
        for slot in range(slots):
            one_cell(peer, slot, mine_ref[peer, OWNER, slot])
            one_cell(peer, slots + slot, theirs_ref[peer, PARTNER, slot])
        return carry

    lax.fori_loop(0, peers, one_peer, 0)


def pack(mine, theirs, slots, held, own, inner, outer):
    peers = mine.shape[0]
    width = held.shape[2]
    return pl.pallas_call(
        pack_kernel,
        out_shape=jax.ShapeDtypeStruct((peers, 2 * slots + 1, ROWS, width), f32),
        in_specs=[SMEM, SMEM] + [VMEM] * 4,
        compiler_params=vmem_limit(28),
        cost_estimate=work(1),
        name="pack",
    )(mine, theirs, held, own, inner, outer)


def two_parts(value):
    high = value.astype(bf16)
    return high, (value - high.astype(f32)).astype(bf16)


def three_parts(value):
    high = value.astype(bf16).astype(f32)
    rest = value - high
    middle = rest.astype(bf16).astype(f32)
    return high, middle, rest - middle


def upsampled(rows, up_high, up_low):
    size = rows.shape[0]
    rows_high, rows_low = two_parts(rows)
    both = jnp.concatenate([rows_high, rows_low], axis=0)
    by_high = lax.dot_general(both, up_high[...], NN, preferred_element_type=f32)
    by_low = lax.dot_general(rows_high, up_low[...], NN, preferred_element_type=f32)
    return by_high[:size] + (by_high[size:] + by_low)


def near_one(raised, source, target, count, up_count):
    width = target.shape[1]
    up_width = raised.shape[1]
    held = rounded_up(count, 16)
    row = lax.broadcasted_iota(jnp.int32, (ROWS, 1), 0)
    is_place = row < 3

    def by_row(parts):
        result = jnp.zeros((ROWS, parts[0].shape[1]), f32)
        for at, part in enumerate(parts):
            result = jnp.where(row == at, part, result)
        return result

    apart = jnp.where(is_place, source[:, count : count + 1] - target[:, count : count + 1], 0.0)
    both = raised + apart
    z = jnp.where(is_place, both, 0.0)
    z_low = pltpu.roll(z, 3, 0)
    z_sq = jnp.sum(z * z, axis=0, keepdims=True)
    z_dot_g = jnp.sum(z_low * both, axis=0, keepdims=True)
    blocks = [both]
    blocks += [both[a : a + 1] * both for a in range(3)]
    blocks.append((z_sq + 2.0 * soften) * both + z_dot_g * z_low)
    split = [three_parts(block) for block in blocks]
    columns = jnp.concatenate([parts[p] for p in range(3) for parts in split], axis=0).astype(bf16)

    zh, zm, zl = three_parts(-2.0 * z)
    one_z = jnp.ones((1, up_width), f32)
    z_norm = by_row([one_z, one_z, one_z, *three_parts(z_sq + soften)])
    z_side = jnp.concatenate(
        [zh, zh, zm, zm, zl, zh, z_norm, jnp.zeros_like(z_norm)], axis=0
    ).astype(bf16)

    y = jnp.where(is_place, target, 0.0)
    y_sq = jnp.sum(y * y, axis=0, keepdims=True)
    yh, ym, yl = three_parts(y)
    one_y = jnp.ones((1, width), f32)
    y_norm = by_row([*three_parts(y_sq), one_y, one_y, one_y])
    y_side = jnp.concatenate([yh, ym, yh, ym, yh, yl, y_norm, jnp.zeros_like(y_norm)], axis=0)
    y_rows = jnp.transpose(y_side)[0:held].astype(bf16)

    weights = []
    for start in range(0, up_width, SECTION):
        span = slice(start, min(start + SECTION, up_width))
        radius_sq = lax.dot_general(y_rows, z_side[:, span], NN, preferred_element_type=f32)
        inverse = lax.rsqrt(radius_sq)
        weights.append(jnp.concatenate(two_parts(inverse * inverse * inverse), axis=0))
    total = lax.dot_general(
        jnp.concatenate(weights, axis=1), columns, NT_DIMS, preferred_element_type=f32
    )
    summed = total[:held] + total[held:]
    lanes = summed.shape[1]
    summed = jnp.concatenate([summed, jnp.zeros((held, LANE - lanes), f32)], axis=1)
    summed = jnp.concatenate([summed, jnp.zeros((width - held, LANE), f32)], axis=0)
    across = jnp.transpose(summed)
    third = 5 * ROWS
    folded = across[0:third] + (across[third : 2 * third] + across[2 * third : 3 * third])
    plain, constant = folded[0:ROWS], folded[4 * ROWS : 5 * ROWS]
    crossed = [folded[(1 + a) * ROWS : (2 + a) * ROWS] for a in range(3)]
    y_low = pltpu.roll(y, 3, 0)
    along = jnp.sum(y_low * plain, axis=0, keepdims=True)
    for a in range(3):
        along = along - crossed[a][3 + a : 4 + a]
    value = y_sq * plain + y_low * along + constant
    for a in range(3):
        value = value - 2.0 * (y[a : a + 1] * crossed[a])
        turned = jnp.sum(y_low * crossed[a], axis=0, keepdims=True)
        value = value - jnp.where(row == 3 + a, turned, 0.0)
    return value * (1.0 / up_count)


def direction(mine_ref, theirs_ref, peer, block, slots):
    backward = block < slots
    slot = jnp.where(backward, block, block - slots)
    alive = jnp.where(backward, theirs_ref[peer, LIVE, slot], mine_ref[peer, LIVE, slot])
    cell = jnp.where(backward, theirs_ref[peer, PARTNER, slot], mine_ref[peer, OWNER, slot])
    return alive, cell


def opposite(block, slots):
    return jnp.where(block < slots, block + slots, block - slots)


def listed(total, alive, order):
    def body(at, held):
        order[held] = at
        return held + alive(at)

    held = lax.fori_loop(0, total, body, 0)

    @pl.when(held > 0)
    def _():
        order[held] = order[jnp.maximum(held - 1, 0)]

    return held


def split_upsample(upsample_ref, high_ref, low_ref):
    count, up_count = upsample_ref.shape
    below = count // 16 * 16
    beyond = up_count // LANE * LANE
    for ref in (high_ref, low_ref):
        ref[below:, :] = jnp.zeros((ref.shape[0] - below, ref.shape[1]), bf16)
        ref[:, beyond:] = jnp.zeros((ref.shape[0], ref.shape[1] - beyond), bf16)
    high, low = two_parts(upsample_ref[...])
    for ref, part in ((high_ref, high), (low_ref, low)):
        ref[0:count, 0:up_count] = part


def near_self_kernel(
    mine_ref,
    sent_ref,
    upsample_ref,
    cells_ref,
    out_ref,
    pts,
    high_ref,
    low_ref,
    raised,
    order,
):
    blocks, width = out_ref.shape[0], out_ref.shape[2]
    slots = blocks // 2
    count, up_count = upsample_ref.shape
    me = lax.axis_index("cell")
    for coord in range(3):
        pack_points(pts, cells_ref, coord, coord, count)
    split_upsample(upsample_ref, high_ref, low_ref)
    source = sent_ref[me, 0:blocks]
    raised[...] = upsampled(source.reshape(blocks * ROWS, width), high_ref, low_ref)

    def alive(block):
        return mine_ref[me, LIVE, jnp.where(block < slots, block, block - slots)]

    def compute(block):
        at = pl.multiple_of(block * ROWS, ROWS)
        target = sent_ref[me, opposite(block, slots)]
        return near_one(raised[pl.ds(at, ROWS), :], sent_ref[me, block], target, count, up_count)

    def two(step, carry):
        pair = [order[2 * step + at] for at in range(2)]
        results = [compute(block) for block in pair]
        for block, result in zip(pair, results):
            out_ref[block] = result
        return carry

    held = listed(blocks, alive, order)
    lax.fori_loop(0, (held + 1) // 2, two, 0)


def near_self(mine, sent, upsample, held):
    _, blocks, _, width = sent.shape
    blocks = blocks - 1
    total = held.shape[1] * (upsample.shape[0] // LANE) + held.shape[1] // 2
    up_width = rounded_up(upsample.shape[1], LANE)
    return pl.pallas_call(
        near_self_kernel,
        out_shape=(
            jax.ShapeDtypeStruct((blocks, ROWS, width), f32),
            jax.ShapeDtypeStruct((3, total, LANE), f32),
        ),
        in_specs=[SMEM] + [VMEM] * 3,
        scratch_shapes=[
            pltpu.VMEM((width, up_width), bf16),
            pltpu.VMEM((width, up_width), bf16),
            pltpu.VMEM((blocks * ROWS, up_width), f32),
            pltpu.SMEM((blocks + 1,), jnp.int32),
        ],
        compiler_params=vmem_limit(28),
        cost_estimate=work(4),
        name="near_self",
    )(mine, sent, upsample, held)


def finish_kernel(
    mine_ref,
    theirs_ref,
    pts,
    translate_ref,
    upsample_ref,
    sent_ref,
    recv_ref,
    own_near_ref,
    out_ref,
    high_ref,
    low_ref,
    raised,
    near,
    far,
    coef_wide,
    order,
):
    up_count = upsample_ref.shape[1]
    split_upsample(upsample_ref, high_ref, low_ref)
    cells, count = out_ref.shape[1:]
    peers, blocks, _, width = recv_ref.shape
    blocks = blocks - 1
    slots = blocks // 2
    me = lax.axis_index("cell")

    def place(pair):
        peer = pair // blocks
        return peer, pair - peer * blocks

    def alive(pair):
        peer, block = place(pair)
        found, _ = direction(mine_ref, theirs_ref, peer, block, slots)
        return jnp.where(peer == me, 0, found)

    held = listed(peers * blocks, alive, order)
    for peer in range(peers):
        rows = recv_ref[peer, 0:blocks].reshape(blocks * ROWS, width)
        near[peer * blocks * ROWS : (peer + 1) * blocks * ROWS, :] = rows

    total = recv_ref[0, blocks]
    for peer in range(1, peers):
        total = total + recv_ref[peer, blocks]
    odd = lax.rem(lax.axis_index("slab"), 2)
    local = jnp.zeros((ROWS, NT), f32)
    for tile, which in enumerate((0, 2 - odd, 1 + odd)):
        summed = total[:, tile * LANE : (tile + 1) * LANE]
        rows = [
            jnp.concatenate([summed[2 * c : 2 * c + 1], summed[2 * c + 1 : 2 * c + 2]], axis=1)
            for c in range(3)
        ]
        rows.append(jnp.zeros((ROWS - 3, 2 * LANE), f32))
        local = local + lax.dot_general(
            jnp.concatenate(rows, axis=0)[:, 0:NT],
            translate_ref[which],
            NT_DIMS,
            precision=highest,
            preferred_element_type=f32,
        )
    nt_width = rounded_up(NT, LANE)
    padded = jnp.concatenate([local, jnp.zeros((ROWS, nt_width - NT), f32)], axis=1)
    tall = jnp.concatenate([padded, jnp.zeros((LANE - ROWS, nt_width), f32)], axis=0)
    upright = jnp.transpose(tall)
    for comp in range(3):
        coef_wide[comp] = jnp.broadcast_to(upright[:, comp : comp + 1], (nt_width, LANE))

    raised[...] = upsampled(near[...], high_ref, low_ref)

    def compute(pair):
        peer, block = place(pair)
        at = pl.multiple_of(pair * ROWS, ROWS)
        target = sent_ref[peer, opposite(block, slots)]
        return near_one(raised[pl.ds(at, ROWS), :], recv_ref[peer, block], target, count, up_count)

    def two(step):
        chosen = [order[2 * step + at] for at in range(2)]
        results = [compute(pair) for pair in chosen]
        for pair, result in zip(chosen, results):
            near[pl.ds(pl.multiple_of(pair * ROWS, ROWS), ROWS), :] = result

    slices = 6
    chunk = pts.shape[1] // 4

    def evaluate(step):
        comp = step // 2
        for part in range(2):
            start = pl.multiple_of((step - 2 * comp) * 2 * chunk + part * chunk, ROWS)
            x, y, z = (pts[coord, pl.ds(start, chunk), :] for coord in range(3))
            by_x = None
            for i in range(DEGREE, -1, -1):
                by_y = None
                for j in range(DEGREE - i, -1, -1):
                    by_z = None
                    for k in range(DEGREE - i - j, -1, -1):
                        at = TERM_AT[(i, j, k)]
                        value = coef_wide[comp, at : at + 1, :]
                        by_z = value if by_z is None else by_z * z + value
                    by_y = by_z if by_y is None else by_y * y + by_z
                by_x = by_y if by_x is None else by_x * x + by_y
            far[comp, pl.ds(start, chunk), :] = by_x

    steps = (held + 1) // 2
    shared = jnp.minimum(steps, slices)

    def both(step, carry):
        evaluate(step)
        two(step)
        return carry

    def near_only(step, carry):
        two(step)
        return carry

    def far_only(step, carry):
        evaluate(step)
        return carry

    lax.fori_loop(0, shared, both, 0)
    lax.fori_loop(shared, steps, near_only, 0)
    lax.fori_loop(shared, slices, far_only, 0)

    full = count // LANE
    rest = count - full * LANE
    half = cells // 2
    for comp in range(3):
        for tile in range(full):
            out_ref[comp, :, tile * LANE : (tile + 1) * LANE] = far[
                comp, tile * cells : (tile + 1) * cells, :
            ]
        tail = far[comp, full * cells : full * cells + half, :]
        out_ref[comp, 0:half, full * LANE : count] = tail[:, 0:rest]
        out_ref[comp, half:cells, full * LANE : count] = tail[:, LANE // 2 : LANE // 2 + rest]

    def add(cell, value):
        for comp in range(3):
            out_ref[comp, pl.ds(cell, 1), :] = (
                out_ref[comp, pl.ds(cell, 1), :] + value[3 + comp : 4 + comp, 0:count]
            )

    def add_pair(step, carry):
        pair = order[step]
        peer, block = place(pair)
        _, cell = direction(mine_ref, theirs_ref, peer, block, slots)
        add(cell, near[pl.ds(pl.multiple_of(pair * ROWS, ROWS), ROWS), :])
        return carry

    lax.fori_loop(0, held, add_pair, 0)

    def add_own(block, carry):
        found, cell = direction(mine_ref, theirs_ref, me, block, slots)

        @pl.when(found > 0)
        def _():
            add(cell, own_near_ref[block])

        return carry

    lax.fori_loop(0, blocks, add_own, 0)


def finish(mine, theirs, points, translate, upsample, sent, recv, own_near, out_shape):
    cells, count = out_shape[1:]
    peers, blocks, _, width = sent.shape
    blocks = blocks - 1
    total = cells * (count // LANE) + cells // 2
    pairs = peers * blocks
    up_width = rounded_up(upsample.shape[1], LANE)
    return pl.pallas_call(
        finish_kernel,
        out_shape=jax.ShapeDtypeStruct(out_shape, f32),
        in_specs=[SMEM, SMEM] + [VMEM] * 6,
        scratch_shapes=[
            pltpu.VMEM((width, up_width), bf16),
            pltpu.VMEM((width, up_width), bf16),
            pltpu.VMEM((pairs * ROWS, up_width), f32),
            pltpu.VMEM((pairs * ROWS, width), f32),
            pltpu.VMEM((3, total, LANE), f32),
            pltpu.VMEM((3, rounded_up(NT, LANE), LANE), f32),
            pltpu.SMEM((pairs + 1,), jnp.int32),
        ],
        compiler_params=vmem_limit(28),
        cost_estimate=work(15),
        name="finish",
    )(mine, theirs, points, translate, upsample, sent, recv, own_near)


def on_device(centers, offsets, forces, upsample, translate, owner_cell, peer_cell, live):
    cells, count = offsets.shape[1:]
    peers, slots = owner_cell.shape[1:]
    slabs = lax.axis_size("slab")
    exchange = functools.partial(
        lax.all_to_all, axis_name="cell", split_axis=0, concat_axis=0, tiled=True
    )
    mine = pair_table(peer_cell, live, owner_cell)
    theirs = exchange(mine)
    spare = rounded_up(count, LANE) - count
    held = jnp.concatenate(
        [
            jnp.concatenate([offsets, jnp.broadcast_to(centers[:, :, None], (3, cells, spare))], 2),
            jnp.pad(forces, ((0, 0), (0, 0), (0, spare))),
        ],
        axis=0,
    )
    held, mine = lax.optimization_barrier((held, mine))
    scale = 1.0 / math.sqrt(cells * peers * count)
    own = moments(held, count, scale)
    swaps = [
        [(i, i + 1) for i in range(first, slabs - 1, 2)]
        + [(i + 1, i) for i in range(first, slabs - 1, 2)]
        for first in (0, 1)
    ]
    inner = lax.ppermute(own, "slab", swaps[0])
    outer = lax.ppermute(own, "slab", swaps[1])
    sent = pack(mine, theirs, slots, held, own, inner, outer)
    recv = exchange(sent)
    own_near, points = near_self(mine, sent, upsample, held)
    return finish(mine, theirs, points, translate, upsample, sent, recv, own_near, offsets.shape)


def solution(mesh):
    return jax.shard_map(
        on_device,
        mesh=mesh,
        in_specs=(
            P(None, ("slab", "cell")),
            P(None, ("slab", "cell"), None),
            P(None, ("slab", "cell"), None),
            P(),
            P(),
            P(("slab", "cell"), None, None),
            P(("slab", "cell"), None, None),
            P(("slab", "cell"), None, None),
        ),
        out_specs=P(None, ("slab", "cell"), None),
        check_vma=False,
    )
```
